32 devices in a mesh: batch: 4 (over y, x), tensor: 8 (over z, core).
Axes of the slice: x: 2, y: 2, z: 4, core: 2. Of those that a mesh axis runs over, the one named last changes fastest.
Arguments:
- tokens: bfloat16 [2048, 2048], P('batch', 'tensor'), may hold values from -6 to 6
- captions: bfloat16 [1024, 4096], P('batch', 'tensor'), may hold values from -6 to 6
- mask_counts: int32 [8], P('batch'), may hold values from 1 to 256, as said below
- mask_positions: int32 [8, 256], P('batch'), may hold values from 0 to 255, each once within a row
- cotangent: bfloat16 [2048, 2048], P('batch', 'tensor'), may hold values from -6 to 6
- mask_embed: bfloat16 [2048], P('tensor'), may hold values from -6 to 6
- position_embed: bfloat16 [256, 2048], P(None, 'tensor'), may hold values from -3 to 3
- norm_self: bfloat16 [2048], P('tensor'), may hold values from 0.099609375 to 1.8984375
- query_self: bfloat16 [2048, 2048], P(None, 'tensor'), may hold values from -0.125 to 0.125
- key_self: bfloat16 [2048, 2048], P(None, 'tensor'), may hold values from -0.125 to 0.125
- value_self: bfloat16 [2048, 2048], P(None, 'tensor'), may hold values from -0.125 to 0.125
- out_self: bfloat16 [2048, 2048], P('tensor'), may hold values from -1.25 to 1.25
- norm_cross: bfloat16 [2048], P('tensor'), may hold values from 0.099609375 to 1.8984375
- query_cross: bfloat16 [2048, 2048], P(None, 'tensor'), may hold values from -0.125 to 0.125
- key_text: bfloat16 [4096, 2048], P(None, 'tensor'), may hold values from -0.09375 to 0.09375
- value_text: bfloat16 [4096, 2048], P(None, 'tensor'), may hold values from -0.09375 to 0.09375
- out_cross: bfloat16 [2048, 2048], P('tensor'), may hold values from -0.875 to 0.875
- norm_feed: bfloat16 [2048], P('tensor'), may hold values from 0.099609375 to 1.8984375
- up_weight: bfloat16 [2048, 8192], P(None, 'tensor'), may hold values from -0.125 to 0.125
- down_weight: bfloat16 [8192, 2048], P('tensor'), may hold values from -0.0625 to 0.0625
Outputs:
- layer_out: bfloat16 [2048, 2048], P('batch', 'tensor')
- tokens_grad: bfloat16 [2048, 2048], P('batch', 'tensor')
- captions_grad: bfloat16 [1024, 4096], P('batch', 'tensor')
- mask_embed_grad: float32 [2048], P('tensor')
- position_embed_grad: float32 [256, 2048], P(None, 'tensor')
- norm_self_grad: float32 [2048], P('tensor')
- query_self_grad: float32 [2048, 2048], P(None, 'tensor')
- key_self_grad: float32 [2048, 2048], P(None, 'tensor')
- value_self_grad: float32 [2048, 2048], P(None, 'tensor')
- out_self_grad: float32 [2048, 2048], P('tensor')
- norm_cross_grad: float32 [2048], P('tensor')
- query_cross_grad: float32 [2048, 2048], P(None, 'tensor')
- key_text_grad: float32 [4096, 2048], P(None, 'tensor')
- value_text_grad: float32 [4096, 2048], P(None, 'tensor')
- out_cross_grad: float32 [2048, 2048], P('tensor')
- norm_feed_grad: float32 [2048], P('tensor')
- up_weight_grad: float32 [2048, 8192], P(None, 'tensor')
- down_weight_grad: float32 [8192, 2048], P('tensor')
The draws below stay inside these ranges and needn't reach their ends.
Inputs may be any that keep to these rules, and one draw needn't show every extreme that they name: `mask_counts`: every draw has an image with all 256 tokens masked and one with a single masked token; counts are skewed towards few masked tokens. `mask_positions`: each row holds every position of the image once.
All inputs are finite; a program needn't handle non-finite values.
Results may differ from the reference program's by a relative error of at most 0.025.
Values may be sent and summed in bfloat16 or wider, within the bound.
No kernel may reach another device: no remote copies, remote signals or barrier semaphores. Data moves between devices by JAX's collectives and lax.ppermute only.
A program may use at most 192 MiB of HBM per device.

```python
import jax
import jax.numpy as jnp
from jax import lax

D = 2048
HEADS = 16
HEAD_DIM = 128
FF = 8192
TXT_D = 4096
TXT_LEN = 128
IMG_LEN = 256
IMG_DEV = 2
IMAGES = 8
TOKENS = 2048
TEXT_TOKENS = 1024
N_BATCH = 4


def draw_mask_counts(key, part):
    first_key, second_key, third_key = jax.random.split(key, 3)
    first = jax.random.randint(first_key, (IMAGES,), 0, IMG_LEN)
    second = jax.random.randint(second_key, (IMAGES,), 0, IMG_LEN)
    counts = first * second // IMG_LEN + 1
    chosen = jax.random.randint(third_key, (), 0, IMAGES)
    index_row = jnp.arange(IMAGES)
    counts = jnp.where(index_row == chosen, IMG_LEN, counts)
    counts = jnp.where(index_row == (chosen + 1) % IMAGES, 1, counts)
    return counts.astype(jnp.int32)


def level_of(key, shape, shards, low, high):
    factor_of = 1.0
    for axis_at, parts in shards:
        steps = jax.random.uniform(jax.random.fold_in(jax.random.fold_in(key, 6), axis_at), (parts,), jnp.float32, low / len(shards), high / len(shards))
        factor_of = factor_of * jnp.repeat(jnp.exp(steps), shape[axis_at] // parts).reshape((-1,) + (1,) * (len(shape) - 1 - axis_at))
    return factor_of


def scatter_about(key, dims, spread, limit, cuts=(), kind=jnp.bfloat16):
    level = level_of(key, dims, cuts, -0.22, 0.18) if cuts else 1.0
    array = jax.random.normal(key, dims, jnp.float32) * spread * level
    return jnp.minimum(jnp.maximum(array, -limit), limit).astype(kind)


def setup_inputs(seed: int = 0) -> dict:
    keys = jax.random.split(jax.random.key(seed), 21)
    return {
        "tokens": scatter_about(keys[0], (TOKENS, D), 1.0, 6.0, ((0, 4), (1, 8))),
        "captions": scatter_about(keys[1], (TEXT_TOKENS, TXT_D), 1.0, 6.0, ((0, 4), (1, 8))),
        "mask_counts": draw_mask_counts(jax.random.fold_in(keys[20], 71), 0),
        "mask_positions": jax.vmap(lambda own: jax.random.permutation(own, IMG_LEN))(jax.random.split(keys[3], IMAGES)).reshape((IMAGES, IMG_LEN)).astype(jnp.int32),
        "cotangent": scatter_about(keys[4], (TOKENS, D), 1.0, 6.0, ((0, 4), (1, 8))),
        "mask_embed": scatter_about(keys[5], (D,), 1.0, 6.0, ((0, 8),)),
        "position_embed": scatter_about(keys[6], (IMG_LEN, D), 0.5, 3.0, ((1, 8),)),
        "norm_self": jnp.clip(1.0 + 0.18 * jax.random.normal(keys[7], (D,), jnp.float32), 0.099609375, 1.8984375).astype(jnp.bfloat16),
        "query_self": scatter_about(keys[8], (D, D), D ** -0.5, 0.125, ((1, 8),)),
        "key_self": scatter_about(keys[9], (D, D), D ** -0.5, 0.125, ((1, 8),)),
        "value_self": scatter_about(keys[10], (D, D), D ** -0.5, 0.125, ((1, 8),)),
        "out_self": scatter_about(keys[11], (D, D), (3 * D // IMG_LEN) ** -0.5, 1.25, ((0, 8),)),
        "norm_cross": jnp.clip(1.0 + 0.18 * jax.random.normal(keys[12], (D,), jnp.float32), 0.099609375, 1.8984375).astype(jnp.bfloat16),
        "query_cross": scatter_about(keys[13], (D, D), D ** -0.5, 0.125, ((1, 8),)),
        "key_text": scatter_about(keys[14], (TXT_D, D), TXT_D ** -0.5, 0.09375, ((1, 8),)),
        "value_text": scatter_about(keys[15], (TXT_D, D), TXT_D ** -0.5, 0.09375, ((1, 8),)),
        "out_cross": scatter_about(keys[16], (D, D), (3 * D // TXT_LEN) ** -0.5, 0.875, ((0, 8),)),
        "norm_feed": jnp.clip(1.0 + 0.18 * jax.random.normal(keys[17], (D,), jnp.float32), 0.099609375, 1.8984375).astype(jnp.bfloat16),
        "up_weight": scatter_about(keys[18], (D, FF), D ** -0.5, 0.125, ((1, 8),)),
        "down_weight": scatter_about(keys[19], (FF, D), FF ** -0.5, 0.0625, ((0, 8),)),
    }


HIGH = lax.Precision.HIGHEST
EPS = 1e-06

@jax.custom_vjp
def low(v):
    return lax.optimization_barrier(v.astype(jnp.bfloat16)).astype(jnp.float32)

@jax.custom_vjp
def low_back(v):
    return v

def low_keep(v):
    return (low(v), None)

def low_pass(kept, grad):
    return (grad,)

def back_keep(v):
    return (v, None)

def back_low(kept, grad):
    return (low(grad),)
low.defvjp(low_keep, low_pass)
low_back.defvjp(back_keep, back_low)

def mask_table(counts, positions):
    slot_ids = jnp.arange(positions.shape[1], dtype=jnp.int32)
    active = slot_ids[None, :] < counts[:, None]
    matched = (positions[:, :, None] == slot_ids[None, None, :]) & active[:, :, None]
    return jnp.any(matched, axis=1)

def gelu_tanh(values):
    return 0.5 * values * (1.0 + jnp.tanh(0.7978845608028654 * (values + 0.044715 * values * values * values)))

def layer_norm(stream, gain_vec):
    row_mean = lax.optimization_barrier(jnp.mean(stream, axis=-1, keepdims=True))
    variance = lax.optimization_barrier(jnp.mean(stream * stream, axis=-1, keepdims=True)) - row_mean * row_mean
    return (stream - row_mean) * lax.rsqrt(variance + EPS) * gain_vec

def project(left, right):
    return jnp.einsum('bld,de->ble', left, right, precision=HIGH)

def attend(queries, key_rows, value_rows):
    images, q_len, _ = queries.shape
    k_len = key_rows.shape[1]
    q_heads = queries.reshape(images, q_len, HEADS, HEAD_DIM)
    k_heads = key_rows.reshape(images, k_len, HEADS, HEAD_DIM)
    v_heads = value_rows.reshape(images, k_len, HEADS, HEAD_DIM)
    scores = low_back(jnp.einsum('bqhd,bkhd->bhqk', q_heads, k_heads, precision=HIGH) * HEAD_DIM ** (-0.5))
    row_max = lax.optimization_barrier(jnp.max(scores, axis=-1, keepdims=True))
    exp_terms = jnp.exp(scores - row_max)
    attn_probs = exp_terms / lax.optimization_barrier(jnp.sum(exp_terms, axis=-1, keepdims=True))
    mixed = jnp.einsum('bhqk,bkhd->bqhd', low(attn_probs), v_heads, precision=HIGH)
    return mixed.reshape(images, q_len, HEADS * HEAD_DIM)

def forward(weights, stream_in, text, masked):
    mask_embed, position_embed, norm_self, query_self, key_self, value_self, out_self, norm_cross, query_cross, key_text, value_text, out_cross, norm_feed, up_weight, down_weight = weights
    stream_zero = jnp.where(masked[:, :, None], mask_embed[None, None, :], stream_in) + position_embed[None]
    normed = low(layer_norm(stream_zero, norm_self))
    queries = low_back(low(project(normed, query_self)))
    key_rows = low_back(low(project(normed, key_self)))
    value_rows = low_back(low(project(normed, value_self)))
    mixed = low_back(low(attend(queries, key_rows, value_rows)))
    stream_one = stream_zero + low_back(project(mixed, out_self))
    normed = low(layer_norm(stream_one, norm_cross))
    queries = low_back(low(project(normed, query_cross)))
    key_rows = low_back(low(project(text, key_text)))
    value_rows = low_back(low(project(text, value_text)))
    mixed = low_back(low(attend(queries, key_rows, value_rows)))
    stream_two = stream_one + low_back(project(mixed, out_cross))
    normed = low(layer_norm(stream_two, norm_feed))
    hidden = low_back(project(normed, up_weight))
    return stream_two + low_back(project(low(gelu_tanh(hidden)), down_weight))

def reference(tokens, captions, mask_counts, mask_positions, cotangent, mask_embed, position_embed, norm_self, query_self, key_self, value_self, out_self, norm_cross, query_cross, key_text, value_text, out_cross, norm_feed, up_weight, down_weight):
    weights = tuple((matrix.astype(jnp.float32) for matrix in (mask_embed, position_embed, norm_self, query_self, key_self, value_self, out_self, norm_cross, query_cross, key_text, value_text, out_cross, norm_feed, up_weight, down_weight)))
    masked = mask_table(mask_counts, mask_positions)
    stream_in = tokens.astype(jnp.float32).reshape(N_BATCH, IMG_DEV, IMG_LEN, D)
    text = captions.astype(jnp.float32).reshape(N_BATCH, IMG_DEV, TXT_LEN, TXT_D)
    seeds = cotangent.astype(jnp.float32).reshape(N_BATCH, IMG_DEV, IMG_LEN, D)
    masks = masked.reshape(N_BATCH, IMG_DEV, IMG_LEN)

    def group_step(totals, pieces):
        part_in, part_text, part_seed, part_mask = pieces

        def local_layer(weight_set, stream, words):
            return forward(weight_set, stream, words, part_mask)
        result, pullback = jax.vjp(local_layer, weights, part_in, part_text)
        weight_grads, stream_grad, text_grad = pullback(part_seed * part_mask[:, :, None].astype(jnp.float32))
        totals = jax.tree.map(jnp.add, totals, weight_grads)
        return (totals, (result.astype(jnp.bfloat16), stream_grad.astype(jnp.bfloat16), text_grad.astype(jnp.bfloat16)))
    zeros = tuple((jnp.zeros_like(matrix) for matrix in weights))
    totals, (outputs, stream_grads, text_grads) = lax.scan(group_step, zeros, (stream_in, text, seeds, masks))
    return (outputs.reshape(TOKENS, D), stream_grads.reshape(TOKENS, D), text_grads.reshape(TEXT_TOKENS, TXT_D), totals[0], totals[1], totals[2], totals[3], totals[4], totals[5], totals[6], totals[7], totals[8], totals[9], totals[10], totals[11], totals[12], totals[13], totals[14])
```

```python
import jax
import jax.numpy as jnp
from jax import lax
from jax.experimental import pallas as pl
from jax.experimental.pallas import tpu as pltpu
from jax.sharding import PartitionSpec as P

HEAD_DIM = 128
IMG_LEN = 256
EPS = 1e-06
F32 = jnp.float32
BF16 = jnp.bfloat16
INV_ROOT = float(HEAD_DIM) ** (-0.5)
PAD = 16
DIRECT = ()
COST = {"self_forward": 17, "text_project": 25, "cross_forward": 0, "seed_product": 12, "feed_both": 6, "out_product": 15, "cross_backward": 20, "self_backward": 27, "self_end": 5, "text_back": 8, "down_grads": 17, "up_grads": 14, "text_grads": 15, "self_grads": 40, "cross_parts": 7, "self_parts": 7, "cross_finish": 0, "self_finish": 5}
DONE_BY = {"T1": "scattered1", "KV": "scattered1", "T2": "scattered2", "X1": "partial2", "X2": "scattered2", "T3": "scattered2", "DA": "scattered2", "Y1": "partial3", "X3": "mixed2", "Y2": "partial3", "F1": "scattered3", "OUT": "mixed2", "Y3": "scattered3", "F2": "mixed3", "A1": "partial4", "A2": "scattered4", "F3": "mixed3", "C0": "scattered4", "TB": "scattered4", "U1": "mixed4", "C1": "scattered4", "GD": "mixed4", "U2": "partial5", "D": "partial5", "GU": "partial5", "GT": "scattered5", "Q1": "scattered5", "Q2": "small", "S0": "scattered5", "S1": "scattered5", "S2": "small"}
AFTER = {"Y1": ("X2",), "A1": ("F2",), "U1": ("TB",), "D": ("C1", "U1",), "S1": ("Q2",), "GQ": ("S1",), "S2": ("GQ",), "GT": ("GU",)}


def contract(left, right, left_dim, right_dim):
    return lax.dot_general(
        left, right, (((left_dim,), (right_dim,)), ((), ())), preferred_element_type=F32
    )


def tie(*values):
    leaves, tree = jax.tree.flatten(values)
    arrays = iter(lax.optimization_barrier([v for v in leaves if not isinstance(v, int)]))
    return tree.unflatten([v if isinstance(v, int) else next(arrays) for v in leaves])


def gather_cols(array):
    return lax.all_gather(array, "tensor", axis=1, tiled=True)


def scatter_cols(array):
    return lax.psum_scatter(array, "tensor", scatter_dimension=1, tiled=True)


def square_batch():
    return lax.axis_size("batch") == 4


def hop(array, flip):
    pairs = [(i, i ^ flip) for i in range(lax.axis_size("batch"))]
    return lax.ppermute(array, "batch", pairs)


def swap_core(array):
    pairs = [(i, i ^ 1) for i in range(lax.axis_size("tensor"))]
    return lax.ppermute(array, "tensor", pairs)


def ring_others(array):
    size, own = lax.axis_size("batch"), lax.axis_index("batch")
    whole = lax.all_gather(array, "batch", axis=0, tiled=False)
    return [
        lax.dynamic_index_in_dim(whole, lax.rem(own + k, size), 0, keepdims=False)
        for k in range(1, size)
    ]


def direct(array):
    moved = [hop(array, k) for k in (1, 2, 3)] if square_batch() else ring_others(array)
    return [[(m, 0)] for m in moved]


class Spread:
    def __init__(self, array, shared):
        self.array, self.shared = array, shared

    def step_one(self):
        if not square_batch():
            return ring_others(self.array)
        return [hop(self.array, 1), hop(self.array, 2)]

    def step_two(self, held):
        rows = self.array.shape[0]
        if square_batch():
            cut = rows // 2
            along, across = held
            groups = [
                [(along, 0)],
                [(across, 0)],
                [(hop(along[:cut], 2), 0), (hop(across[cut:], 1), cut)],
            ]
        else:
            groups = [[(piece, 0)] for piece in held]
        return groups

    def swap(self, groups):
        if self.shared:
            rows = self.array.shape[0]
            groups = [g + [(swap_core(piece), rows + at) for piece, at in g] for g in groups]
        return groups


def direct_sum(array):
    if not square_batch():
        return lax.psum(array.astype(BF16), "batch").astype(F32)
    low = array.astype(BF16)
    moved = [hop(low, k) for k in (1, 2, 3)]
    return array + moved[0].astype(F32) + moved[1].astype(F32) + moved[2].astype(F32)


def params():
    return pltpu.CompilerParams(vmem_limit_bytes=56 << 20)


def cost(micros):
    return pl.CostEstimate(
        flops=1000, bytes_accessed=int(1e6 * micros) + 1000, transcendentals=0
    )


def struct(shape, dtype):
    return jax.ShapeDtypeStruct(shape, dtype)


def by_rows(rows, width, first=0):
    return pl.BlockSpec((rows, width), lambda i, *_: (first + i, 0))


def turned_rows(rows, width):
    blocks = IMG_LEN // rows
    return pl.BlockSpec((rows, width), lambda i, place: (image_turn(i, place, blocks), 0))


def fixed(shape, row=0, col=0):
    return pl.BlockSpec(shape, lambda i, *_: (row, col))


def call(name, kernel, place, grid, in_specs, out_specs, outs, args, scratch=(), aliases=None):
    return pl.pallas_call(
        kernel,
        grid_spec=pltpu.PrefetchScalarGridSpec(
            num_scalar_prefetch=1,
            grid=grid,
            in_specs=in_specs,
            out_specs=out_specs,
            scratch_shapes=list(scratch),
        ),
        out_shape=outs,
        input_output_aliases=aliases or {},
        compiler_params=params(),
        cost_estimate=cost(COST[name]),
        name=name,
    )(place, *args)


def core_of(place):
    return place[0] % 2


class Packed:
    def __init__(self, rows, text_rows):
        self.rows = rows
        self.pos = rows
        self.text = rows + IMG_LEN
        self.seed = self.text + text_rows
        self.vec = self.seed + rows
        self.total = self.vec + PAD


def pack_rows(at, counts, positions, tokens, captions, cotangent, position_embed, vectors):
    rows, columns = tokens.shape
    images = rows // IMG_LEN
    text_rows = captions.shape[0]
    text_blocks = captions.shape[1] // columns

    def kernel(counts, order, tok, cap, cot, pos, *rest):
        out, block, mask = rest[-3:]
        out[: at.pos, :] = tok[...]
        out[at.pos : at.text, :] = pos[...]
        for k in range(text_blocks):
            low = at.text + k * text_rows
            out[low : low + text_rows, :] = cap[:, k * columns : (k + 1) * columns]
        lines = [v[...].astype(F32).reshape(1, columns) for v in rest[:-3]]
        lines.append(jnp.zeros((PAD - len(lines), columns), F32))
        vec = jnp.concatenate(lines, axis=0).astype(BF16)
        out[at.vec :, :] = vec
        block[...] = vec
        place = lax.broadcasted_iota(jnp.int32, (IMG_LEN, IMG_LEN), 0)
        slot = lax.broadcasted_iota(jnp.int32, (IMG_LEN, IMG_LEN), 1)
        for i in range(images):
            hit = (order[i : i + 1, :] == place) & (slot < counts[i])
            column = jnp.max(hit.astype(F32), axis=1, keepdims=True)
            own = slice(i * IMG_LEN, (i + 1) * IMG_LEN)
            mask[own, :] = column
            out[at.seed + i * IMG_LEN : at.seed + (i + 1) * IMG_LEN, :] = jnp.where(
                column > 0.0, cot[own, :].astype(F32), 0.0
            ).astype(BF16)

    vmem = pl.BlockSpec(memory_space=pltpu.VMEM)
    outs = [
        struct((at.total, columns), BF16),
        struct((PAD, columns), BF16),
        struct((rows, 1), F32),
    ]
    args = (counts, positions, tokens, captions, cotangent, position_embed, *vectors)
    return pl.pallas_call(
        kernel,
        in_specs=[pl.BlockSpec(memory_space=pltpu.SMEM)] + [vmem] * (len(args) - 1),
        out_specs=[vmem] * 3,
        out_shape=outs,
        compiler_params=params(),
        cost_estimate=cost(2),
        name="pack_rows",
    )(*args)


def normalize(stream):
    width = stream.shape[1]
    mean = jnp.sum(stream, axis=1, keepdims=True) * (1.0 / width)
    var = jnp.sum(stream * stream, axis=1, keepdims=True) * (1.0 / width) - mean * mean
    inv_std = lax.rsqrt(var + EPS)
    return (stream - mean) * inv_std, mean, inv_std


def norm_back(grad, normed, inv_std, gain):
    width = grad.shape[1]
    normal = normed * (1.0 / gain)
    scaled = grad * gain
    first = jnp.sum(scaled, axis=1, keepdims=True) * (1.0 / width)
    second = jnp.sum(grad * normed, axis=1, keepdims=True) * (1.0 / width)
    back = inv_std * (scaled - first - normal * second)
    return back, jnp.sum(grad * normal, axis=0, keepdims=True)


def probabilities(query, key):
    scores = contract(query, key, 1, 1) * INV_ROOT
    terms = jnp.exp(scores - jnp.max(scores, axis=1, keepdims=True))
    return terms * (1.0 / jnp.sum(terms, axis=1, keepdims=True))


def head_slices(width):
    return [slice(at, at + HEAD_DIM) for at in range(0, width, HEAD_DIM)]


def attend(query, key, value):
    mixed = [
        contract(probabilities(query[:, h], key[:, h]).astype(BF16), value[:, h], 1, 0)
        for h in head_slices(query.shape[1])
    ]
    return jnp.concatenate(mixed, axis=1).astype(BF16)


def attend_back(grad, query, key, value):
    parts = []
    for h in head_slices(query.shape[1]):
        probs = probabilities(query[:, h], key[:, h])
        prob_grad = contract(grad[:, h], value[:, h], 1, 1)
        inner = jnp.sum(probs * prob_grad, axis=1, keepdims=True)
        score_grad = (probs * (prob_grad - inner)).astype(BF16)
        parts.append(
            (
                contract(score_grad, key[:, h], 1, 0) * INV_ROOT,
                contract(score_grad, query[:, h], 0, 0) * INV_ROOT,
                contract(probs.astype(BF16), grad[:, h], 0, 0),
            )
        )
    return [jnp.concatenate(group, axis=1).astype(BF16) for group in zip(*parts)]


def first_stream(mask, tok, pos, vec):
    base = jnp.where(mask[...] > 0.0, vec[0:1, :].astype(F32), tok[...].astype(F32))
    return base + pos[...].astype(F32)


def packed_specs(at, width):
    return [
        by_rows(IMG_LEN, 1),
        by_rows(IMG_LEN, width),
        fixed((IMG_LEN, width), at.pos // IMG_LEN),
        fixed((PAD, width), at.vec // PAD),
    ]


def self_forward(place, at, mask, packed, query_w, key_w, value_w, out_w):
    rows, width = mask.shape[0], packed.shape[1]
    columns = query_w.shape[1]

    def kernel(
        place, mask, tok, pos, vec, wq, wk, wv, wo, normed, query, key, value, mixed, part, stats
    ):
        normal, mean, inv_std = normalize(first_stream(mask, tok, pos, vec))
        stats[:, 0:1] = mean
        stats[:, 1:2] = inv_std
        low = (normal * vec[1:2, :].astype(F32)).astype(BF16)
        normed[...] = low
        q = contract(low, wq[...], 1, 0).astype(BF16)
        k = contract(low, wk[...], 1, 0).astype(BF16)
        v = contract(low, wv[...], 1, 0).astype(BF16)
        query[...], key[...], value[...] = q, k, v
        a = attend(q, k, v)
        mixed[...] = a
        part[...] = contract(a, wo[...], 1, 0).astype(BF16)

    outs = [struct((rows, width), BF16)] + [struct((rows, columns), BF16)] * 4
    outs += [struct((rows, width), BF16), struct((rows, 2), F32)]
    args = (mask, packed, packed, packed, query_w, key_w, value_w, out_w)
    return call(
        "self_forward",
        kernel,
        place,
        (rows // IMG_LEN,),
        packed_specs(at, width) + [fixed(w.shape) for w in (query_w, key_w, value_w, out_w)],
        [turned_rows(IMG_LEN, width)] + [by_rows(IMG_LEN, o.shape[1]) for o in outs[1:]],
        outs,
        args,
    )


def text_project(place, at, text, key_w, value_w):
    columns = key_w.shape[1]
    width = text.shape[1]
    shards = width // columns
    blocks = key_w.shape[0] // width
    text_rows = (at.seed - at.text) // blocks
    first = at.text // text_rows
    step = min(4, shards)

    def kernel(place, *refs):
        texts, (wk, wv, key, value, key_sum, value_sum) = refs[:blocks], refs[blocks:]

        @pl.when(pl.program_id(0) == 0)
        def _():
            key_sum[...] = jnp.zeros_like(key_sum)
            value_sum[...] = jnp.zeros_like(value_sum)

        for t in range(step):
            for k, text in enumerate(texts):
                piece = text[:, t * columns : (t + 1) * columns]
                key_sum[...] += contract(piece, wk[t, k], 1, 0)
                value_sum[...] += contract(piece, wv[t, k], 1, 0)

        @pl.when(pl.program_id(0) == pl.num_programs(0) - 1)
        def _():
            key[...] = key_sum[...].astype(BF16)
            value[...] = value_sum[...].astype(BF16)

    cut = (shards, blocks, columns, columns)
    outs = [struct((text_rows, columns), BF16)] * 2
    weight = pl.BlockSpec((step, *cut[1:]), lambda i, *_: (i, 0, 0, 0))
    args = (*[text] * blocks, key_w.reshape(cut), value_w.reshape(cut))
    return call(
        "text_project",
        kernel,
        place,
        (shards // step,),
        [
            pl.BlockSpec((text_rows, step * columns), lambda i, *_, k=k: (first + k, i))
            for k in range(blocks)
        ]
        + [weight] * 2,
        [fixed(o.shape) for o in outs],
        outs,
        args,
        scratch=[pltpu.VMEM((text_rows, columns), F32)] * 2,
    )


def cross_forward(place, at, mask, packed, added, query_w, key, value, out_w):
    rows, width = mask.shape[0], packed.shape[1]
    columns = query_w.shape[1]
    text_rows = key.shape[0] // (rows // IMG_LEN)

    def kernel(
        place, mask, tok, pos, vec, add, wq, k, v, wo, stream, normed, query, mixed, part, scale
    ):
        one = first_stream(mask, tok, pos, vec) + add[...].astype(F32)
        stream[...] = one
        normal, mean, inv_std = normalize(one)
        scale[...] = inv_std
        low = (normal * vec[2:3, :].astype(F32)).astype(BF16)
        normed[...] = low
        q = contract(low, wq[...], 1, 0).astype(BF16)
        query[...] = q
        a = attend(q, k[...], v[...])
        mixed[...] = a
        part[...] = contract(a, wo[...], 1, 0).astype(BF16)

    outs = [struct((rows, width), F32), struct((rows, width), BF16)]
    outs += [struct((rows, columns), BF16)] * 2 + [struct((rows, width), BF16)]
    outs += [struct((rows, 1), F32)]
    args = (mask, packed, packed, packed, added, query_w, key, value, out_w)
    return call(
        "cross_forward",
        kernel,
        place,
        (rows // IMG_LEN,),
        packed_specs(at, width)
        + [
            by_rows(IMG_LEN, width),
            fixed(query_w.shape),
            by_rows(text_rows, columns),
            by_rows(text_rows, columns),
            fixed(out_w.shape),
        ],
        [by_rows(IMG_LEN, o.shape[1]) for o in outs],
        outs,
        args,
    )


def seed_product(place, at, seed, down_w):
    rows, (hidden, width) = at.rows, down_w.shape

    def kernel(place, seed, down, out):
        out[...] = contract(seed[...], down[...], 1, 1)

    outs = [struct((rows, hidden), F32)]
    return call(
        "seed_product",
        kernel,
        place,
        (rows // IMG_LEN,),
        [by_rows(IMG_LEN, width, at.seed // IMG_LEN), fixed(down_w.shape)],
        [by_rows(IMG_LEN, hidden)],
        outs,
        (seed, down_w),
    )[0]


def gelu_parts(u):
    scale = 0.7978845608028654
    square = u * u
    bend = jnp.tanh(scale * (u + 0.044715 * square * u))
    half = 0.5 * (1.0 + bend)
    slope = half + 0.5 * u * (1.0 - bend * bend) * scale * (1.0 + 3.0 * 0.044715 * square)
    return u * half, slope


def image_turn(i, place, blocks):
    return (i // blocks + place[0] % 2) % 2 * blocks + i % blocks


def feed_both(place, at, stream, added, packed, act_grad, up_w):
    rows, width = stream.shape
    hidden, columns = up_w.shape[1], width // lax.axis_size("tensor")
    block = IMG_LEN

    def kernel(place, one, add, vec, dact, up, slim, scale, normed, act, grad, part, two):
        stream = one[...] + add[...].astype(F32)
        two[...] = stream
        slim[...] = two[:, pl.ds(pl.multiple_of(place[0] * columns, columns), columns)]
        normal, mean, inv_std = normalize(stream)
        scale[...] = inv_std
        low = (normal * vec[3:4, :].astype(F32)).astype(BF16)
        normed[...] = low
        value, slope = gelu_parts(contract(low, up[...], 1, 0))
        act[...] = value.astype(BF16)
        du = (dact[...] * slope).astype(BF16)
        grad[...] = du
        part[...] = contract(du, up[...], 1, 1).astype(BF16)

    outs = [
        struct((rows, columns), F32),
        struct((rows, 1), F32),
        struct((rows, width), BF16),
        struct((rows, hidden), BF16),
        struct((rows, hidden), BF16),
        struct((rows, width), BF16),
    ]
    args = (stream, added, packed, act_grad, up_w)
    return call(
        "feed_both",
        kernel,
        place,
        (rows // block,),
        [
            by_rows(block, width),
            by_rows(block, width),
            fixed((PAD, width), at.vec // PAD),
            by_rows(block, hidden),
            fixed(up_w.shape),
        ],
        [
            by_rows(block, columns),
            by_rows(block, 1),
            turned_rows(block, width),
            turned_rows(block, hidden),
            turned_rows(block, hidden),
            by_rows(block, width),
        ],
        outs,
        args,
        scratch=[pltpu.VMEM((block, width), F32)],
    )


def out_product(place, activation, down_w):
    rows, (hidden, width) = activation.shape[0], down_w.shape

    def kernel(place, act, down, out):
        out[...] = contract(act[...], down[...], 1, 0).astype(BF16)

    outs = [struct((2 * rows, width), BF16)]
    return call(
        "out_product",
        kernel,
        place,
        (rows // IMG_LEN,),
        [
            turned_rows(IMG_LEN, hidden),
            fixed(down_w.shape),
        ],
        [by_rows(IMG_LEN, width, rows // IMG_LEN)],
        outs,
        (activation, down_w),
    )[0]


def cross_backward(
    place, at, normed, scale, back, seed, packed, out_w, query, key, value, query_w, room
):
    rows, width = normed.shape
    columns = query.shape[1]
    text_rows = key.shape[0] // (rows // IMG_LEN)

    def kernel(place, three, inv, dn, g3, vec, wo, q, k, v, wq, room, grad, low, dq, dkv, part, gain):
        step, gain_step = norm_back(
            dn[...].astype(F32), three[...].astype(F32), inv[...], vec[3:4, :].astype(F32)
        )
        total = g3[...].astype(F32) + step
        grad[...] = total
        y = total.astype(BF16)
        low[...] = y

        @pl.when(pl.program_id(0) == 0)
        def _():
            gain[...] = jnp.zeros_like(gain)

        gain[...] += gain_step
        da = contract(y, wo[...], 1, 1).astype(BF16)
        query_grad, key_grad, value_grad = attend_back(da, q[...], k[...], v[...])
        dq[...] = query_grad
        dkv[:, :columns] = key_grad
        dkv[:, columns:] = value_grad
        part[...] = contract(query_grad, wq[...], 1, 1).astype(BF16)

    outs = [
        struct((rows, width), F32),
        struct((rows, width), BF16),
        struct((rows, columns), BF16),
        struct((key.shape[0], 2 * columns), BF16),
        struct(room.shape, BF16),
        struct((1, width), F32),
    ]
    args = (normed, scale, back, seed, packed, out_w, query, key, value, query_w, room)
    return call(
        "cross_backward",
        kernel,
        place,
        (rows // IMG_LEN,),
        [
            turned_rows(IMG_LEN, width),
            by_rows(IMG_LEN, 1),
            by_rows(IMG_LEN, width),
            by_rows(IMG_LEN, width, at.seed // IMG_LEN),
            fixed((PAD, width), at.vec // PAD),
            fixed(out_w.shape),
            by_rows(IMG_LEN, columns),
            by_rows(text_rows, columns),
            by_rows(text_rows, columns),
            fixed(query_w.shape),
            pl.BlockSpec(memory_space=pl.ANY),
        ],
        [
            by_rows(IMG_LEN, width),
            by_rows(IMG_LEN, width),
            by_rows(IMG_LEN, columns),
            by_rows(text_rows, 2 * columns),
            by_rows(IMG_LEN, width),
            fixed((1, width)),
        ],
        outs,
        args,
        aliases={len(args): 4},
    )


def text_back(place, pair, key_w, value_w, rows, width):
    columns = key_w.shape[1]
    shards = width // columns
    blocks = key_w.shape[0] // width
    text_rows = pair.shape[0]
    cut = (shards, blocks, columns, columns)

    def kernel(place, grads, wk, wv, out):
        for k in range(blocks):
            part = contract(grads[:, :columns], wk[0, k], 1, 1) + contract(
                grads[:, columns:], wv[0, k], 1, 1
            )
            out[k * text_rows : (k + 1) * text_rows, :] = part.astype(BF16)
        out[blocks * text_rows :, :] = jnp.zeros((rows - blocks * text_rows, columns), BF16)

    weight = pl.BlockSpec((1, *cut[1:]), lambda i, *_: (i, 0, 0, 0))
    outs = [struct((2 * rows, width), BF16)]
    return call(
        "text_back",
        kernel,
        place,
        (shards,),
        [fixed(pair.shape), weight, weight],
        [pl.BlockSpec((rows, columns), lambda i, *_: (1, i))],
        outs,
        (pair, key_w.reshape(cut), value_w.reshape(cut)),
    )[0]


def self_backward(
    place, at, start, normed, scale, back, packed, grad, out_w, query, key, value, weights, room
):
    rows, width = normed.shape
    columns = query.shape[1]
    parts = IMG_LEN // columns

    def kernel(
        place, one, two, inv, dn, vec, g2, wo, q, k, v, wq, wk, wv, room, mine, low, triple, part, gain, held, lines
    ):
        i = pl.program_id(0)
        step, gain_step = norm_back(
            dn[...].astype(F32), two[...].astype(F32), inv[...], vec[2:3, :].astype(F32)
        )
        total = g2[...] + step
        held[...] = total
        mine[...] = held[:, pl.ds(pl.multiple_of(place[0] * columns, columns), columns)]
        y = total.astype(BF16)
        low[...] = y

        @pl.when(i == 0)
        def _():
            gain[...] = jnp.zeros_like(gain)
            lines[...] = jnp.zeros_like(lines)

        gain[...] += gain_step
        da = contract(y, wo[...], 1, 1).astype(BF16)
        query_grad, key_grad, value_grad = attend_back(da, q[...], k[...], v[...])
        triple[:, :columns] = query_grad
        triple[:, columns : 2 * columns] = key_grad
        triple[:, 2 * columns :] = value_grad
        partial = (
            contract(query_grad, wq[...], 1, 1)
            + contract(key_grad, wk[...], 1, 1)
            + contract(value_grad, wv[...], 1, 1)
        )
        sent = partial.astype(BF16)
        part[pl.ds(pl.multiple_of(i * IMG_LEN, IMG_LEN), IMG_LEN), :] = sent
        first = contract(vec[...], sent, 1, 1)[1:2, :]
        weighted = (partial * one[...].astype(F32)).astype(BF16)
        second = contract(jnp.ones((PAD, width), BF16), weighted, 1, 1)[0:1, :]
        for stat, line in enumerate((first, second)):
            for k in range(parts):
                piece = line[:, k * columns : (k + 1) * columns]
                lines[pl.ds((2 * i + stat) * parts + k, 1), :] = jnp.concatenate(
                    [piece] * (width // columns), axis=1
                )

        @pl.when(i == pl.num_programs(0) - 1)
        def _():
            part[rows:, :] = lines[...].astype(BF16)

    outs = [
        struct((rows, columns), F32),
        struct((rows, width), BF16),
        struct((rows, 3 * columns), BF16),
        struct(room.shape, BF16),
        struct((1, width), F32),
    ]
    args = (start, normed, scale, back, packed, grad, out_w, query, key, value, *weights, room)
    return call(
        "self_backward",
        kernel,
        place,
        (rows // IMG_LEN,),
        [
            turned_rows(IMG_LEN, width),
            by_rows(IMG_LEN, width),
            by_rows(IMG_LEN, 1),
            by_rows(IMG_LEN, width),
            fixed((PAD, width), at.vec // PAD),
            by_rows(IMG_LEN, width),
            fixed(out_w.shape),
        ]
        + [by_rows(IMG_LEN, columns)] * 3
        + [fixed(w.shape) for w in weights]
        + [pl.BlockSpec(memory_space=pl.ANY)],
        [
            by_rows(IMG_LEN, columns),
            by_rows(IMG_LEN, width),
            turned_rows(IMG_LEN, 3 * columns),
            fixed((rows + PAD, width)),
            fixed((1, width)),
        ],
        outs,
        args,
        scratch=[pltpu.VMEM((IMG_LEN, width), F32), pltpu.VMEM((PAD, width), F32)],
        aliases={len(args): 3},
    )


def self_end(place, mask, tokens, position_embed, vectors, stats, back, grad, gains, width):
    rows, columns = tokens.shape
    images = rows // IMG_LEN
    parts = IMG_LEN // columns

    def kernel(place, mask, tok, pos, vec, stat, tot, dn, g1, cross, feed, out, small):
        i = pl.program_id(0)
        masked = mask[...] > 0.0
        stream = first_stream(mask, tok, pos, vec)
        normal = (stream - stat[:, 0:1]) * stat[:, 1:2]
        normed_grad = dn[...].astype(F32)
        scaled = normed_grad * vec[1:2, :].astype(F32)
        line = lax.broadcasted_iota(jnp.int32, (PAD, 128), 0)
        lane = lax.broadcasted_iota(jnp.int32, (PAD, 128), 1)
        turned = [
            contract(
                tot[...],
                ((line == (2 * i + lane) * parts + k) & (lane < 2)).astype(F32).astype(BF16),
                0,
                0,
            )
            for k in range(parts)
        ]
        sums = jnp.concatenate(turned, axis=0) * (1.0 / width)
        total = g1[...] + stat[:, 1:2] * (scaled - sums[:, 0:1] - normal * sums[:, 1:2])
        out[...] = jnp.where(masked, 0.0, total).astype(BF16)

        @pl.when(i == 0)
        def _():
            small[...] = jnp.zeros_like(small)
            small[IMG_LEN + 2 : IMG_LEN + 3, :] = cross[...]
            small[IMG_LEN + 3 : IMG_LEN + 4, :] = feed[...]

        small[:IMG_LEN, :] += total
        small[IMG_LEN : IMG_LEN + 1, :] += jnp.sum(
            jnp.where(masked, total, 0.0), axis=0, keepdims=True
        )
        small[IMG_LEN + 1 : IMG_LEN + 2, :] += jnp.sum(normed_grad * normal, axis=0, keepdims=True)

    outs = [struct((rows, columns), BF16), struct((IMG_LEN + PAD, columns), F32)]
    own = pl.BlockSpec((1, columns), lambda i, place: (0, place[0]))
    return call(
        "self_end",
        kernel,
        place,
        (images,),
        [
            by_rows(IMG_LEN, 1),
            by_rows(IMG_LEN, columns),
            fixed((IMG_LEN, columns)),
            fixed((PAD, columns)),
            by_rows(IMG_LEN, 2),
            fixed((PAD, columns), rows // PAD),
            by_rows(IMG_LEN, columns),
            by_rows(IMG_LEN, columns),
            own,
            own,
        ],
        [by_rows(IMG_LEN, columns), fixed((IMG_LEN + PAD, columns))],
        outs,
        (mask, tokens, position_embed, vectors, stats, back, back, grad, *gains),
    )


def grad_sum(name, place, left_groups, right_groups, splits, block, spans):
    lefts, rights, terms = [], [], []
    for left_group, right_group in zip(left_groups, right_groups):
        left_base, right_base = len(lefts), len(rights)
        lefts += [p if isinstance(p, tuple) else (p, p.shape[0], None) for p, at in left_group]
        rights += [p if isinstance(p, tuple) else (p, p.shape[0], None) for p, at in right_group]
        for i, (_, left_at) in enumerate(left_group):
            for j, (_, right_at) in enumerate(right_group):
                left_rows, right_rows = lefts[left_base + i][1], rights[right_base + j][1]
                low = max(left_at, right_at)
                high = min(left_at + left_rows, right_at + right_rows)
                if low < high:
                    terms.append(
                        (left_base + i, low - left_at, right_base + j, low - right_at, high - low)
                    )
    (left_turn, height), (right_turn, width) = spans
    block = min(block, height)
    left_turn = left_turn * (height // block)
    left_count, right_count = len(lefts), len(rights)

    def kernel(place, *refs):
        left_refs = refs[:left_count]
        right_refs = refs[left_count : left_count + right_count]
        outs = refs[left_count + right_count :]
        total = None
        for li, left_row, ri, right_row, rows in terms:
            part = contract(
                left_refs[li][left_row : left_row + rows, :],
                right_refs[ri][right_row : right_row + rows, :],
                0,
                0,
            )
            total = part if total is None else total + part
        at = 0
        for out in outs:
            out[...] = total[:, at : at + out.shape[1]]
            at += out.shape[1]

    def spec(rows, wide, col, turn):
        return pl.BlockSpec(
            (rows, wide), lambda i, place: (0 if turn is None else turn(place), col(i))
        )

    outs = [struct((height, n), F32) for n in splits]
    return call(
        name,
        kernel,
        place,
        (height // block,),
        [spec(rows, block, lambda i: left_turn + i, turn) for _, rows, turn in lefts]
        + [spec(rows, width, lambda i: right_turn, turn) for _, rows, turn in rights],
        [pl.BlockSpec((block, n), lambda i, *_: (i, 0)) for n in splits],
        outs,
        [a for a, _, _ in (*lefts, *rights)],
    )


def text_grads(place, at, text, pair, text_groups, pair_groups, blocks):
    width = text.shape[1]
    text_rows = pair.shape[0]
    columns = pair.shape[1] // 2
    shards = width // columns
    step = min(4, shards)
    core_split = square_batch()
    pieces, rights, terms = [], [pair], []
    for text_group, pair_group in zip(text_groups, pair_groups):
        rights.append(pair_group[0][0])
        for piece, row in text_group:
            pieces.append(piece)
            terms.append((row // text_rows, row % text_rows, len(rights) - 1))
    if not core_split:
        pieces, terms = [], []
        for k, text_group in enumerate(text_groups):
            for b in range(blocks):
                pieces.append(text_group[0][0][b * text_rows : (b + 1) * text_rows])
                terms.append((b, 0, k + 1))

    def which(s, place):
        return (s + place[0] % 2) % 2 if core_split else s

    def kernel(place, own, *refs):
        piece_refs = refs[: len(pieces)]
        right_refs = refs[len(pieces) : len(pieces) + len(rights)]
        key, value = refs[len(pieces) + len(rights) :]

        def run(s):
            total = contract(own[...], right_refs[0][...], 0, 0)
            for ref, (turn, row, k) in zip(piece_refs, terms):
                if turn == s:
                    total = total + contract(
                        ref[...], right_refs[k][row : row + ref.shape[0], :], 0, 0
                    )
            for t in range(step):
                rows = slice(t * columns, (t + 1) * columns)
                key[t, 0] = total[rows, :columns]
                value[t, 0] = total[rows, columns:]

        for s in range(blocks):
            pl.when(pl.program_id(0) == s)(lambda s=s: run(s))

    last = shards // step - 1

    def piece_spec(piece, turn):
        return pl.BlockSpec(
            (piece.shape[0], step * columns),
            lambda s, t, place: (0, jnp.where(s == turn, t, jnp.where(s > turn, last, 0))),
        )

    outs = [struct((shards, blocks, columns, columns), F32)] * 2
    out_spec = pl.BlockSpec(
        (step, 1, columns, columns), lambda s, t, place: (t, which(s, place), 0, 0)
    )
    key, value = call(
        "text_grads",
        kernel,
        place,
        (blocks, shards // step),
        [
            pl.BlockSpec(
                (text_rows, step * columns), lambda s, t, place: (at.text // text_rows + which(s, place), t)
            )
        ]
        + [piece_spec(p, term[0]) for p, term in zip(pieces, terms)]
        + [pl.BlockSpec(r.shape, lambda s, t, place: (0, 0)) for r in rights],
        [out_spec] * 2,
        outs,
        (text, *pieces, *rights),
    )
    return key.reshape(-1, columns), value.reshape(-1, columns)


class Plan:
    def __init__(self):
        self.makers, self.made = {}, {}

    def job(self, name, make):
        self.makers[name] = make

    def get(self, name):
        if name not in self.made:
            self.made[name] = self.makers[name]()
        return self.made[name]

    def behind(self, name, value):
        others = [self.get(n) for n in AFTER.get(name, ())]
        return tie(value, *others)[0] if others else value

    def tie(self, point, value):
        names = [n for n in self.makers if DONE_BY.get(n) == point]
        if not names:
            return value
        value, *done = tie(value, *[self.get(n) for n in names])
        self.made.update(zip(names, done))
        return value


class BatchSum:
    def __init__(self, name, place, products):
        self.name, self.place, self.products = name, place, products
        shapes = [
            (right.shape[1], left.shape[1]) if fold else (left.shape[1], right.shape[1])
            for left, right, fold in products
        ]
        if not square_batch():
            self.quarters = []
            return
        height, width = shapes[0]
        rows = height // 4

        def kernel(place, *refs):
            ins, outs, held = refs[: 2 * len(products)], refs[2 * len(products) : -1], refs[-1]
            for n, (_, _, fold) in enumerate(products):
                left, right = ins[2 * n], ins[2 * n + 1]
                if fold:
                    for at in range(0, width, height):
                        held[n, :, at : at + height] = contract(
                            left[:, at : at + height], right[...], 0, 0
                        ).astype(BF16)
                else:
                    held[n] = contract(left[...], right[...], 0, 0).astype(BF16)
                for k, out in enumerate(outs):
                    turn = pl.multiple_of((place[1] ^ k) * rows, rows)
                    out[n * rows : (n + 1) * rows, :] = held[n, pl.ds(turn, rows), :]

        args = [a for left, right, _ in products for a in (left, right)]
        outs = [struct((rows * len(products), width), BF16)] * 4
        self.quarters = call(
            name + "_parts",
            kernel,
            place,
            (1,),
            [fixed(a.shape) for a in args],
            [fixed(o.shape) for o in outs],
            outs,
            args,
            scratch=[pltpu.VMEM((len(products), height, width), BF16)],
        )
        self.height, self.width, self.rows = height, width, rows

    def step_one(self):
        if not square_batch():
            parts = [contract(left, right, 0, 0) for left, right, _ in self.products]
            return [lax.psum(p.astype(BF16), "batch") for p in parts]
        return [hop(self.sent[k - 1], k) for k in (1, 2, 3)]

    def step_two(self, held):
        if not square_batch():
            return held
        total = self.quarters[0].astype(F32)
        for moved in held:
            total = total + moved.astype(F32)
        low = total.astype(BF16)
        return [low] + [hop(low, k) for k in (1, 2, 3)]

    def finish(self, held):
        if not square_batch():
            return [h.astype(F32) for h in held]
        height, width, rows = self.height, self.width, self.rows
        folds = [fold for _, _, fold in self.products]

        def kernel(place, *refs):
            ins, outs = refs[:4], refs[4:]
            for n, (out, fold) in enumerate(zip(outs, folds)):
                for k, ref in enumerate(ins):
                    at = pl.multiple_of((place[1] ^ k) * rows, rows)
                    piece = ref[n * rows : (n + 1) * rows, :].astype(F32)
                    if fold:
                        for col in range(0, width, height):
                            out[pl.ds(col + at, rows), :] = piece[:, col : col + height]
                    else:
                        out[pl.ds(at, rows), :] = piece

        outs = [struct((width, height) if fold else (height, width), F32) for fold in folds]
        return call(
            self.name + "_finish",
            kernel,
            self.place,
            (1,),
            [fixed(a.shape) for a in held],
            [fixed(o.shape) for o in outs],
            outs,
            held,
        )


def body(
    tokens,
    captions,
    mask_counts,
    mask_positions,
    cotangent,
    mask_embed,
    position_embed,
    norm_self,
    query_self,
    key_self,
    value_self,
    out_self,
    norm_cross,
    query_cross,
    key_text,
    value_text,
    out_cross,
    norm_feed,
    up_weight,
    down_weight,
):
    rows, columns = tokens.shape
    width, hidden = query_self.shape[0], up_weight.shape[1]
    text_rows, text_blocks = captions.shape[0], captions.shape[1] // columns
    at = Packed(rows, text_rows * text_blocks)
    place = jnp.stack([lax.axis_index("tensor"), lax.axis_index("batch")]).astype(jnp.int32)
    core = place[0] % 2
    shared = square_batch()
    packed, vectors, mask = pack_rows(
        at,
        mask_counts,
        mask_positions,
        tokens,
        captions,
        cotangent,
        position_embed,
        (mask_embed, norm_self, norm_cross, norm_feed),
    )
    packed = gather_cols(packed)

    text_part, seed_part = packed[at.text : at.seed], packed[at.seed : at.vec]
    if shared:
        text_part = lax.dynamic_slice_in_dim(packed, at.text + core * text_rows, text_rows, 0)
        seed_part = lax.dynamic_slice_in_dim(packed, at.seed + core * IMG_LEN, IMG_LEN, 0)
    else:
        seed_part = jnp.concatenate(
            [
                lax.dynamic_slice_in_dim(seed_part, core * IMG_LEN, IMG_LEN, 0),
                lax.dynamic_slice_in_dim(seed_part, (1 - core) * IMG_LEN, IMG_LEN, 0),
            ],
            axis=0,
        )
    plan = Plan()

    def spread(name, source, shared):
        move = Spread(None, shared)

        def one():
            move.array = plan.behind(name + "1", source())
            return direct(move.array) if name in DIRECT else move.step_one()

        def two():
            held = plan.get(name + "1")
            return held if name in DIRECT else move.step_two(held)

        plan.job(name + "1", one)
        plan.job(name + "2", two)
        plan.job(name + "3", lambda: move.swap(plan.get(name + "2")))

    normed_self, query_one, key_one, value_one, mixed_self, partial, stats = self_forward(
        place, at, mask, packed, query_self, key_self, value_self, out_self
    )
    spread("T", lambda: text_part, shared)
    spread("X", lambda: normed_self[:IMG_LEN] if shared else normed_self, shared)
    spread("Y", lambda: seed_part, shared)
    plan.job("KV", lambda: text_project(place, at, packed, key_text, value_text))
    plan.job("DA", lambda: seed_product(place, at, packed, down_weight))
    scattered = plan.tie("scattered1", scatter_cols(partial))
    mixed_out = plan.tie("mixed1", gather_cols(scattered))
    key_two, value_two = plan.get("KV")

    stream_one, normed_cross, query_two, mixed_cross, partial, scale_cross = cross_forward(
        place, at, mask, packed, mixed_out, query_cross, key_two, value_two, out_cross
    )
    partial = plan.tie("partial2", partial)
    scattered = plan.tie("scattered2", scatter_cols(partial))
    mixed_out = plan.tie("mixed2", gather_cols(scattered))

    own_two, scale_feed, normed_feed, activation, hidden_grad, partial = feed_both(
        place, at, stream_one, mixed_out, packed, plan.get("DA"), up_weight
    )
    spread("F", lambda: normed_feed[:IMG_LEN] if shared else normed_feed, shared)
    spread("A", lambda: activation, False)
    spread("U", lambda: hidden_grad, False)
    plan.job("OUT", lambda: out_product(place, plan.behind("OUT", activation), down_weight))
    partial = plan.tie("partial3", partial)
    scattered = plan.tie("scattered3", scatter_cols(partial))
    feed_back = plan.tie("mixed3", gather_cols(scattered))

    grad_two, seed_cross, query_grad, pair, partial, feed_gain = cross_backward(
        place,
        at,
        normed_feed,
        scale_feed,
        feed_back,
        packed,
        packed,
        out_cross,
        query_two,
        key_two,
        value_two,
        query_cross,
        plan.get("OUT"),
    )
    own_seed = [
        ((packed, IMG_LEN, lambda p: at.seed // IMG_LEN + p[0] % 2), 0),
        ((packed, IMG_LEN, lambda p: at.seed // IMG_LEN + 1 - p[0] % 2), IMG_LEN),
    ]
    plan.job(
        "GD",
        lambda: grad_sum(
            "down_grads",
            place,
            [[(plan.behind("GD", activation), 0)], *plan.get("A2")],
            [own_seed, *plan.get("Y3")],
            (width,),
            256,
            ((0, hidden), (0, width)),
        ),
    )
    plan.job(
        "GU",
        lambda: grad_sum(
            "up_grads",
            place,
            [[(plan.behind("GU", normed_feed), 0)], *plan.get("F3")],
            [[(hidden_grad, 0)], *plan.get("U2")],
            (hidden,),
            512,
            ((0, width), (0, hidden)),
        ),
    )
    cross_sum = BatchSum(
        "cross", place, [(mixed_cross, seed_cross, False), (normed_cross, query_grad, True)]
    )

    def batch_sum(name, total):
        plan.job(name + "0", lambda: total.quarters)

        def one():
            total.sent = plan.behind(name + "1", plan.get(name + "0")[1:])
            return total.step_one()

        plan.job(name + "1", one)
        plan.job(name + "2", lambda: total.step_two(plan.behind(name + "2", plan.get(name + "1"))))

    batch_sum("C", cross_sum)
    plan.job(
        "TB",
        lambda: text_back(
            place, plan.behind("TB", pair), key_text, value_text, rows + PAD, width
        ),
    )
    plan.job("D", lambda: direct(plan.behind("D", pair)))
    plan.job(
        "GT",
        lambda: text_grads(
            place,
            at,
            packed,
            plan.behind("GT", pair),
            plan.get("T3"),
            plan.get("D"),
            text_blocks,
        ),
    )
    partial = plan.tie("partial4", partial)
    scattered = plan.tie("scattered4", scatter_cols(partial))
    out_slice = scattered[rows:]
    cross_back = plan.tie("mixed4", gather_cols(scattered[:rows]))

    own_one, seed_self, triple, partial, cross_gain = self_backward(
        place,
        at,
        normed_self,
        normed_cross,
        scale_cross,
        cross_back,
        packed,
        grad_two,
        out_self,
        query_one,
        key_one,
        value_one,
        (query_self, key_self, value_self),
        plan.get("TB"),
    )
    layer_out = (own_two + out_slice.astype(F32)).astype(BF16)
    self_sum = BatchSum("self", place, [(mixed_self, seed_self, False)])
    batch_sum("S", self_sum)
    spread("Q", lambda: triple, False)
    plan.job(
        "GQ",
        lambda: grad_sum(
            "self_grads",
            place,
            [[(plan.behind("GQ", normed_self), 0)], *plan.get("X3")],
            [[(triple, 0)], *plan.get("Q2")],
            (columns,) * 3,
            512,
            ((0, width), (0, 3 * columns)),
        ),
    )
    partial = plan.tie("partial5", partial)
    scattered = plan.tie("scattered5", scatter_cols(partial))
    low = rows + PAD
    captions_grad = jnp.concatenate(
        [
            scattered[low + k * text_rows : low + (k + 1) * text_rows]
            for k in range(text_blocks)
        ],
        axis=1,
    )
    tokens_grad, small = self_end(
        place,
        mask,
        tokens,
        position_embed,
        vectors,
        stats,
        scattered,
        own_one,
        (cross_gain, feed_gain),
        width,
    )
    small = plan.tie("small", small)
    small = direct_sum(small)
    (down_grad,) = plan.get("GD")
    (up_grad,) = plan.get("GU")
    key_text_grad, value_text_grad = plan.get("GT")
    query_self_grad, key_self_grad, value_self_grad = plan.get("GQ")
    out_cross_grad, query_cross_grad = cross_sum.finish(plan.get("C2"))
    (out_self_grad,) = self_sum.finish(plan.get("S2"))
    return (
        layer_out,
        tokens_grad,
        captions_grad,
        small[IMG_LEN],
        small[:IMG_LEN],
        small[IMG_LEN + 1],
        query_self_grad,
        key_self_grad,
        value_self_grad,
        out_self_grad,
        small[IMG_LEN + 2],
        query_cross_grad,
        key_text_grad,
        value_text_grad,
        out_cross_grad,
        small[IMG_LEN + 3],
        up_grad,
        down_grad,
    )


def solution(mesh):
    return jax.shard_map(
        body,
        mesh=mesh,
        in_specs=(
            P("batch", "tensor"),
            P("batch", "tensor"),
            P("batch"),
            P("batch", None),
            P("batch", "tensor"),
            P("tensor"),
            P(None, "tensor"),
            P("tensor"),
            P(None, "tensor"),
            P(None, "tensor"),
            P(None, "tensor"),
            P("tensor", None),
            P("tensor"),
            P(None, "tensor"),
            P(None, "tensor"),
            P(None, "tensor"),
            P("tensor", None),
            P("tensor"),
            P(None, "tensor"),
            P("tensor", None),
        ),
        out_specs=(
            P("batch", "tensor"),
            P("batch", "tensor"),
            P("batch", "tensor"),
            P("tensor"),
            P(None, "tensor"),
            P("tensor"),
            P(None, "tensor"),
            P(None, "tensor"),
            P(None, "tensor"),
            P("tensor", None),
            P("tensor"),
            P(None, "tensor"),
            P(None, "tensor"),
            P(None, "tensor"),
            P("tensor", None),
            P("tensor"),
            P(None, "tensor"),
            P("tensor", None),
        ),
        check_vma=False,
    )
```

```python
import jax
import jax.numpy as jnp
from jax import lax
from jax.experimental import pallas as pl
from jax.experimental.pallas import tpu as pltpu
from jax.sharding import PartitionSpec as P

HEAD_DIM = 128
IMG_LEN = 256
EPS = 1e-06
F32 = jnp.float32
BF16 = jnp.bfloat16
INV_ROOT = float(HEAD_DIM) ** (-0.5)
PAD = 16
BATCH, TENSOR = "batch", "tensor"
(
    T1, T2, T3, X1, X2, X3, Y1, Y2, Y3, KV, DA, F1, F2, F3, A1, A2, A3, U1, U2, U3, OUT, GD, GU,
    C0, C1, CA, C2, C3, TB, D1, D2, D3, GT, S0, S1, SA, S2, S3, Q1, Q2, Q3, GQ, SM, CF, SF,
) = range(45)
(
    SCATTERED1, MIXED1, PARTIAL2, SCATTERED2, MIXED2, PARTIAL3, SCATTERED3, MIXED3, PARTIAL4,
    SCATTERED4, MIXED4, PARTIAL5, SCATTERED5, SMALL,
) = range(14)
DONE_BY = {
    T1: SCATTERED1, KV: SCATTERED1, T2: PARTIAL2, X1: MIXED1, X2: SCATTERED2, T3: SCATTERED2,
    DA: SCATTERED2, Y1: PARTIAL3, X3: SCATTERED2, Y2: PARTIAL3, F1: SCATTERED3, OUT: SCATTERED3,
    Y3: SCATTERED3, F2: MIXED3, A1: PARTIAL4, A2: SCATTERED4, F3: MIXED3, C0: SCATTERED5,
    TB: SCATTERED4, U1: MIXED4, C1: SCATTERED4, GD: MIXED4, U2: PARTIAL5, GU: SCATTERED5,
    GT: SCATTERED5, Q1: SCATTERED5, Q2: SMALL, S0: SCATTERED5, C2: SCATTERED5, D2: SCATTERED5,
    C3: SMALL,
}
AFTER = {
    A1: (F2,), U1: (TB,), S1: (Q2,), GQ: (S1, SM,), F1: (Y3,), GT: (GU,), CF: (SM,), SF: (SM,),
    D1: (C1, U1,), SA: (SM,), C3: (U2,),
}
DIRECT = (C2, D1, S2,)
COST = dict(
    self_forward=17, text_project=25, cross_forward=0, seed_product=3, feed_both=6, out_product=15,
    cross_backward=20, self_backward=27, self_end=5, text_back=8, down_grads=0, up_grads=14,
    text_grads=15, self_grads=40, cross_parts=0, self_parts=6, cross_finish=0, self_finish=25,
)


def contract(left, right, left_dim, right_dim):
    return lax.dot_general(
        left, right, (((left_dim,), (right_dim,)), ((), ())), preferred_element_type=F32
    )


def tie(*values):
    leaves, tree = jax.tree.flatten(values)
    arrays = iter(lax.optimization_barrier([v for v in leaves if not isinstance(v, int)]))
    return tree.unflatten([v if isinstance(v, int) else next(arrays) for v in leaves])


def gather_cols(array):
    return lax.all_gather(array, TENSOR, axis=1, tiled=True)


def scatter_cols(array):
    return lax.psum_scatter(array, TENSOR, scatter_dimension=1, tiled=True)


def square_batch():
    return lax.axis_size(BATCH) == 4


def hop(array, flip):
    pairs = [(i, i ^ flip) for i in range(lax.axis_size(BATCH))]
    return lax.ppermute(array, BATCH, pairs)


def swap_core(array):
    pairs = [(i, i ^ 1) for i in range(lax.axis_size(TENSOR))]
    return lax.ppermute(array, TENSOR, pairs)


def ring_others(array):
    size, own = lax.axis_size(BATCH), lax.axis_index(BATCH)
    whole = lax.all_gather(array, BATCH, axis=0, tiled=False)
    return [
        lax.dynamic_index_in_dim(whole, lax.rem(own + k, size), 0, keepdims=False)
        for k in range(1, size)
    ]


def direct(array):
    moved = [hop(array, k) for k in (1, 2, 3)] if square_batch() else ring_others(array)
    return [[(m, 0)] for m in moved]


class Spread:
    def __init__(self, array, shared):
        self.array, self.shared = array, shared

    def step_one(self):
        if not square_batch():
            return ring_others(self.array)
        return [hop(self.array, 1), hop(self.array, 2)]

    def step_two(self, held):
        rows = self.array.shape[0]
        if square_batch():
            cut = rows // 2
            along, across = held
            groups = [
                [(along, 0)],
                [(across, 0)],
                [(hop(along[:cut], 2), 0), (hop(across[cut:], 1), cut)],
            ]
        else:
            groups = [[(piece, 0)] for piece in held]
        return groups

    def swap(self, groups):
        if self.shared:
            rows = self.array.shape[0]
            groups = [g + [(swap_core(piece), rows + at) for piece, at in g] for g in groups]
        return groups


def direct_sum(array):
    if not square_batch():
        return lax.psum(array.astype(BF16), BATCH).astype(F32)
    low = array.astype(BF16)
    moved = [hop(low, k) for k in (1, 2, 3)]
    return array + moved[0].astype(F32) + moved[1].astype(F32) + moved[2].astype(F32)


def params():
    return pltpu.CompilerParams(vmem_limit_bytes=56 << 20)


def cost(micros):
    return pl.CostEstimate(
        flops=1000, bytes_accessed=int(1e6 * micros) + 1000, transcendentals=0
    )


def struct(shape, dtype):
    return jax.ShapeDtypeStruct(shape, dtype)


def by_rows(rows, width, first=0):
    return pl.BlockSpec((rows, width), lambda i, *_: (first + i, 0))


def turned_rows(rows, width):
    blocks = IMG_LEN // rows
    return pl.BlockSpec((rows, width), lambda i, place: (image_turn(i, place, blocks), 0))


def fixed(shape, row=0, col=0):
    return pl.BlockSpec(shape, lambda i, *_: (row, col))


def call(name, kernel, place, grid, in_specs, out_specs, outs, args, scratch=(), aliases=None):
    return pl.pallas_call(
        kernel,
        grid_spec=pltpu.PrefetchScalarGridSpec(
            num_scalar_prefetch=1,
            grid=grid,
            in_specs=in_specs,
            out_specs=out_specs,
            scratch_shapes=list(scratch),
        ),
        out_shape=outs,
        input_output_aliases=aliases or {},
        compiler_params=params(),
        cost_estimate=cost(COST[name]),
        name=name,
    )(place, *args)


def core_of(place):
    return place[0] % 2


class Packed:
    def __init__(self, rows, text_rows):
        self.rows = rows
        self.text = rows
        self.seed = self.text + text_rows
        self.vec = self.seed + rows
        self.total = self.vec + PAD


def pack_rows(at, counts, positions, tokens, captions, cotangent, position_embed, vectors):
    rows, columns = tokens.shape
    images = rows // IMG_LEN
    text_rows = captions.shape[0]
    text_blocks = captions.shape[1] // columns

    def kernel(counts, order, tok, cap, cot, pos, *rest):
        out, block, mask = rest[-3:]
        for k in range(text_blocks):
            low = at.text + k * text_rows
            out[low : low + text_rows, :] = cap[:, k * columns : (k + 1) * columns]
        lines = [v[...].astype(F32).reshape(1, columns) for v in rest[:-3]]
        lines.append(jnp.zeros((PAD - len(lines), columns), F32))
        vec = jnp.concatenate(lines, axis=0).astype(BF16)
        out[at.vec :, :] = vec
        block[...] = vec
        place = lax.broadcasted_iota(jnp.int32, (IMG_LEN, IMG_LEN), 0)
        slot = lax.broadcasted_iota(jnp.int32, (IMG_LEN, IMG_LEN), 1)
        for i in range(images):
            hit = (order[i : i + 1, :] == place) & (slot < counts[i])
            column = jnp.max(hit.astype(F32), axis=1, keepdims=True)
            own = slice(i * IMG_LEN, (i + 1) * IMG_LEN)
            mask[own, :] = column
            base = jnp.where(column > 0.0, vec[0:1, :].astype(F32), tok[own, :].astype(F32))
            out[own, :] = (base + pos[...].astype(F32)).astype(BF16)
            out[at.seed + i * IMG_LEN : at.seed + (i + 1) * IMG_LEN, :] = jnp.where(
                column > 0.0, cot[own, :].astype(F32), 0.0
            ).astype(BF16)

    vmem = pl.BlockSpec(memory_space=pltpu.VMEM)
    outs = [
        struct((at.total, columns), BF16),
        struct((PAD, columns), BF16),
        struct((rows, 1), F32),
    ]
    args = (counts, positions, tokens, captions, cotangent, position_embed, *vectors)
    return pl.pallas_call(
        kernel,
        in_specs=[pl.BlockSpec(memory_space=pltpu.SMEM)] + [vmem] * (len(args) - 1),
        out_specs=[vmem] * 3,
        out_shape=outs,
        compiler_params=params(),
        cost_estimate=cost(2),
        name="pack_rows",
    )(*args)


def normalize(stream):
    width = stream.shape[1]
    mean = jnp.sum(stream, axis=1, keepdims=True) * (1.0 / width)
    var = jnp.sum(stream * stream, axis=1, keepdims=True) * (1.0 / width) - mean * mean
    inv_std = lax.rsqrt(var + EPS)
    return (stream - mean) * inv_std, mean, inv_std


def norm_back(grad, normed, inv_std, gain):
    width = grad.shape[1]
    normal = normed * (1.0 / gain)
    scaled = grad * gain
    first = jnp.sum(scaled, axis=1, keepdims=True) * (1.0 / width)
    second = jnp.sum(grad * normed, axis=1, keepdims=True) * (1.0 / width)
    back = inv_std * (scaled - first - normal * second)
    return back, jnp.sum(grad * normal, axis=0, keepdims=True)


def probabilities(query, key):
    scores = contract(query, key, 1, 1) * INV_ROOT
    terms = jnp.exp(scores - jnp.max(scores, axis=1, keepdims=True))
    return terms * (1.0 / jnp.sum(terms, axis=1, keepdims=True))


def head_slices(width):
    return [slice(at, at + HEAD_DIM) for at in range(0, width, HEAD_DIM)]


def attend(query, key, value):
    mixed = [
        contract(probabilities(query[:, h], key[:, h]).astype(BF16), value[:, h], 1, 0)
        for h in head_slices(query.shape[1])
    ]
    return jnp.concatenate(mixed, axis=1).astype(BF16)


def attend_back(grad, query, key, value):
    parts = []
    for h in head_slices(query.shape[1]):
        probs = probabilities(query[:, h], key[:, h])
        prob_grad = contract(grad[:, h], value[:, h], 1, 1)
        inner = jnp.sum(probs * prob_grad, axis=1, keepdims=True)
        score_grad = (probs * (prob_grad - inner)).astype(BF16)
        parts.append(
            (
                contract(score_grad, key[:, h], 1, 0) * INV_ROOT,
                contract(score_grad, query[:, h], 0, 0) * INV_ROOT,
                contract(probs.astype(BF16), grad[:, h], 0, 0),
            )
        )
    return [jnp.concatenate(group, axis=1).astype(BF16) for group in zip(*parts)]


def first_stream(mask, tok, pos, vec):
    base = jnp.where(mask[...] > 0.0, vec[0:1, :].astype(F32), tok[...].astype(F32))
    return base + pos[...].astype(F32)


def packed_specs(at, width):
    return [by_rows(IMG_LEN, width), fixed((PAD, width), at.vec // PAD)]


def self_forward(place, at, packed, query_w, key_w, value_w, out_w):
    rows, width = at.rows, packed.shape[1]
    columns = query_w.shape[1]

    def kernel(
        place, zero, vec, wq, wk, wv, wo, normed, query, key, value, mixed, part, stats
    ):
        normal, mean, inv_std = normalize(zero[...].astype(F32))
        stats[:, 0:1] = mean
        stats[:, 1:2] = inv_std
        low = (normal * vec[1:2, :].astype(F32)).astype(BF16)
        normed[...] = low
        q = contract(low, wq[...], 1, 0).astype(BF16)
        k = contract(low, wk[...], 1, 0).astype(BF16)
        v = contract(low, wv[...], 1, 0).astype(BF16)
        query[...], key[...], value[...] = q, k, v
        a = attend(q, k, v)
        mixed[...] = a
        part[...] = contract(a, wo[...], 1, 0).astype(BF16)

    outs = [struct((rows, width), BF16)] + [struct((rows, columns), BF16)] * 4
    outs += [struct((rows, width), BF16), struct((rows, 2), F32)]
    args = (packed, packed, query_w, key_w, value_w, out_w)
    return call(
        "self_forward",
        kernel,
        place,
        (rows // IMG_LEN,),
        packed_specs(at, width) + [fixed(w.shape) for w in (query_w, key_w, value_w, out_w)],
        [turned_rows(IMG_LEN, width)] + [by_rows(IMG_LEN, o.shape[1]) for o in outs[1:]],
        outs,
        args,
    )


def text_project(place, at, text, key_w, value_w):
    columns = key_w.shape[1]
    width = text.shape[1]
    shards = width // columns
    blocks = key_w.shape[0] // width
    text_rows = (at.seed - at.text) // blocks
    first = at.text // text_rows
    step = min(4, shards)

    def kernel(place, *refs):
        texts, (wk, wv, key, value, key_sum, value_sum) = refs[:blocks], refs[blocks:]

        @pl.when(pl.program_id(0) == 0)
        def _():
            key_sum[...] = jnp.zeros_like(key_sum)
            value_sum[...] = jnp.zeros_like(value_sum)

        for t in range(step):
            for k, text in enumerate(texts):
                piece = text[:, t * columns : (t + 1) * columns]
                key_sum[...] += contract(piece, wk[t, k], 1, 0)
                value_sum[...] += contract(piece, wv[t, k], 1, 0)

        @pl.when(pl.program_id(0) == pl.num_programs(0) - 1)
        def _():
            key[...] = key_sum[...].astype(BF16)
            value[...] = value_sum[...].astype(BF16)

    cut = (shards, blocks, columns, columns)
    outs = [struct((text_rows, columns), BF16)] * 2
    weight = pl.BlockSpec((step, *cut[1:]), lambda i, *_: (i, 0, 0, 0))
    args = (*[text] * blocks, key_w.reshape(cut), value_w.reshape(cut))
    return call(
        "text_project",
        kernel,
        place,
        (shards // step,),
        [
            pl.BlockSpec((text_rows, step * columns), lambda i, *_, k=k: (first + k, i))
            for k in range(blocks)
        ]
        + [weight] * 2,
        [fixed(o.shape) for o in outs],
        outs,
        args,
        scratch=[pltpu.VMEM((text_rows, columns), F32)] * 2,
    )


def cross_forward(place, at, packed, added, query_w, key, value, out_w):
    rows, width = at.rows, packed.shape[1]
    columns = query_w.shape[1]
    text_rows = key.shape[0] // (rows // IMG_LEN)

    def kernel(
        place, zero, vec, add, wq, k, v, wo, stream, normed, query, mixed, part, scale
    ):
        one = zero[...].astype(F32) + add[...].astype(F32)
        stream[...] = one.astype(BF16)
        normal, mean, inv_std = normalize(one)
        scale[...] = inv_std
        low = (normal * vec[2:3, :].astype(F32)).astype(BF16)
        normed[...] = low
        q = contract(low, wq[...], 1, 0).astype(BF16)
        query[...] = q
        a = attend(q, k[...], v[...])
        mixed[...] = a
        part[...] = contract(a, wo[...], 1, 0).astype(BF16)

    outs = [struct((rows, width), BF16)] * 2
    outs += [struct((rows, columns), BF16)] * 2 + [struct((rows, width), BF16)]
    outs += [struct((rows, 1), F32)]
    args = (packed, packed, added, query_w, key, value, out_w)
    return call(
        "cross_forward",
        kernel,
        place,
        (rows // IMG_LEN,),
        packed_specs(at, width)
        + [
            by_rows(IMG_LEN, width),
            fixed(query_w.shape),
            by_rows(text_rows, columns),
            by_rows(text_rows, columns),
            fixed(out_w.shape),
        ],
        [by_rows(IMG_LEN, o.shape[1]) for o in outs],
        outs,
        args,
    )


def seed_product(place, at, seed, down_w):
    rows, (hidden, width) = at.rows, down_w.shape

    def kernel(place, seed, down, out):
        out[...] = contract(seed[...], down[...], 1, 1)

    outs = [struct((rows, hidden), F32)]
    return call(
        "seed_product",
        kernel,
        place,
        (rows // IMG_LEN,),
        [by_rows(IMG_LEN, width, at.seed // IMG_LEN), fixed(down_w.shape)],
        [by_rows(IMG_LEN, hidden)],
        outs,
        (seed, down_w),
    )[0]


def gelu_parts(u):
    scale = 0.7978845608028654
    square = u * u
    bend = jnp.tanh(scale * (u + 0.044715 * square * u))
    half = 0.5 * (1.0 + bend)
    slope = half + 0.5 * u * (1.0 - bend * bend) * scale * (1.0 + 3.0 * 0.044715 * square)
    return u * half, slope


def image_turn(i, place, blocks):
    return (i // blocks + place[0] % 2) % 2 * blocks + i % blocks


def feed_both(place, at, stream, added, packed, act_grad, up_w):
    rows, width = stream.shape
    hidden, columns = up_w.shape[1], width // lax.axis_size(TENSOR)
    block = IMG_LEN

    def kernel(place, one, add, vec, dact, up, slim, scale, normed, act, grad, part, two):
        stream = one[...].astype(F32) + add[...].astype(F32)
        two[...] = stream
        slim[...] = two[:, pl.ds(pl.multiple_of(place[0] * columns, columns), columns)]
        normal, mean, inv_std = normalize(stream)
        scale[...] = inv_std
        low = (normal * vec[3:4, :].astype(F32)).astype(BF16)
        normed[...] = low
        value, slope = gelu_parts(contract(low, up[...], 1, 0))
        act[...] = value.astype(BF16)
        du = (dact[...] * slope).astype(BF16)
        grad[...] = du
        part[...] = contract(du, up[...], 1, 1).astype(BF16)

    outs = [
        struct((rows, columns), F32),
        struct((rows, 1), F32),
        struct((rows, width), BF16),
        struct((rows, hidden), BF16),
        struct((rows, hidden), BF16),
        struct((rows, width), BF16),
    ]
    args = (stream, added, packed, act_grad, up_w)
    return call(
        "feed_both",
        kernel,
        place,
        (rows // block,),
        [
            by_rows(block, width),
            by_rows(block, width),
            fixed((PAD, width), at.vec // PAD),
            by_rows(block, hidden),
            fixed(up_w.shape),
        ],
        [
            by_rows(block, columns),
            by_rows(block, 1),
            turned_rows(block, width),
            turned_rows(block, hidden),
            turned_rows(block, hidden),
            by_rows(block, width),
        ],
        outs,
        args,
        scratch=[pltpu.VMEM((block, width), F32)],
    )


def out_product(place, activation, down_w):
    rows, (hidden, width) = activation.shape[0], down_w.shape

    def kernel(place, act, down, out):
        out[...] = contract(act[...], down[...], 1, 0).astype(BF16)

    outs = [struct((2 * rows, width), BF16)]
    return call(
        "out_product",
        kernel,
        place,
        (rows // IMG_LEN,),
        [
            turned_rows(IMG_LEN, hidden),
            fixed(down_w.shape),
        ],
        [by_rows(IMG_LEN, width, rows // IMG_LEN)],
        outs,
        (activation, down_w),
    )[0]


def cross_backward(
    place, at, normed, scale, back, seed, packed, out_w, query, key, value, query_w, room
):
    rows, width = normed.shape
    columns = query.shape[1]
    text_rows = key.shape[0] // (rows // IMG_LEN)

    def kernel(place, three, inv, dn, g3, vec, wo, q, k, v, wq, room, low, dq, dkv, part, gain):
        step, gain_step = norm_back(
            dn[...].astype(F32), three[...].astype(F32), inv[...], vec[3:4, :].astype(F32)
        )
        total = g3[...].astype(F32) + step
        y = total.astype(BF16)
        low[...] = y

        @pl.when(pl.program_id(0) == 0)
        def _():
            gain[...] = jnp.zeros_like(gain)

        gain[...] += gain_step
        da = contract(y, wo[...], 1, 1).astype(BF16)
        query_grad, key_grad, value_grad = attend_back(da, q[...], k[...], v[...])
        dq[...] = query_grad
        dkv[:, :columns] = key_grad
        dkv[:, columns:] = value_grad
        part[...] = contract(query_grad, wq[...], 1, 1).astype(BF16)

    outs = [
        struct((rows, width), BF16),
        struct((rows, columns), BF16),
        struct((key.shape[0], 2 * columns), BF16),
        struct(room.shape, BF16),
        struct((1, width), F32),
    ]
    args = (normed, scale, back, seed, packed, out_w, query, key, value, query_w, room)
    return call(
        "cross_backward",
        kernel,
        place,
        (rows // IMG_LEN,),
        [
            turned_rows(IMG_LEN, width),
            by_rows(IMG_LEN, 1),
            by_rows(IMG_LEN, width),
            by_rows(IMG_LEN, width, at.seed // IMG_LEN),
            fixed((PAD, width), at.vec // PAD),
            fixed(out_w.shape),
            by_rows(IMG_LEN, columns),
            by_rows(text_rows, columns),
            by_rows(text_rows, columns),
            fixed(query_w.shape),
            pl.BlockSpec(memory_space=pl.ANY),
        ],
        [
            by_rows(IMG_LEN, width),
            by_rows(IMG_LEN, columns),
            by_rows(text_rows, 2 * columns),
            by_rows(IMG_LEN, width),
            fixed((1, width)),
        ],
        outs,
        args,
        aliases={len(args): 3},
    )


def text_back(place, pair, key_w, value_w, rows, width):
    columns = key_w.shape[1]
    shards = width // columns
    blocks = key_w.shape[0] // width
    text_rows = pair.shape[0]
    cut = (shards, blocks, columns, columns)

    def kernel(place, grads, wk, wv, out):
        for t in range(step):
            cols = slice(t * columns, (t + 1) * columns)
            for k in range(blocks):
                part = contract(grads[:, :columns], wk[t, k], 1, 1) + contract(
                    grads[:, columns:], wv[t, k], 1, 1
                )
                out[k * text_rows : (k + 1) * text_rows, cols] = part.astype(BF16)
        out[blocks * text_rows :, :] = jnp.zeros(
            (rows - blocks * text_rows, step * columns), BF16
        )

    step = min(4, shards)
    weight = pl.BlockSpec((step, *cut[1:]), lambda i, *_: (i, 0, 0, 0))
    outs = [struct((2 * rows, width), BF16)]
    return call(
        "text_back",
        kernel,
        place,
        (shards // step,),
        [fixed(pair.shape), weight, weight],
        [pl.BlockSpec((rows, step * columns), lambda i, *_: (1, i))],
        outs,
        (pair, key_w.reshape(cut), value_w.reshape(cut)),
    )[0]


def self_backward(
    place, at, start, normed, scale, back, packed, grad, out_w, query, key, value, weights, room
):
    rows, width = normed.shape
    columns = query.shape[1]
    parts = IMG_LEN // columns

    def kernel(
        place, one, two, inv, dn, vec, g2, wo, q, k, v, wq, wk, wv, room, mine, low, triple, part, gain, held, lines
    ):
        i = pl.program_id(0)
        step, gain_step = norm_back(
            dn[...].astype(F32), two[...].astype(F32), inv[...], vec[2:3, :].astype(F32)
        )
        total = g2[...].astype(F32) + step
        held[...] = total
        mine[...] = held[:, pl.ds(pl.multiple_of(place[0] * columns, columns), columns)]
        y = total.astype(BF16)
        low[...] = y

        @pl.when(i == 0)
        def _():
            gain[...] = jnp.zeros_like(gain)
            lines[...] = jnp.zeros_like(lines)

        gain[...] += gain_step
        da = contract(y, wo[...], 1, 1).astype(BF16)
        query_grad, key_grad, value_grad = attend_back(da, q[...], k[...], v[...])
        triple[:, :columns] = query_grad
        triple[:, columns : 2 * columns] = key_grad
        triple[:, 2 * columns :] = value_grad
        partial = (
            contract(query_grad, wq[...], 1, 1)
            + contract(key_grad, wk[...], 1, 1)
            + contract(value_grad, wv[...], 1, 1)
        )
        sent = partial.astype(BF16)
        part[pl.ds(pl.multiple_of(i * IMG_LEN, IMG_LEN), IMG_LEN), :] = sent
        first = contract(vec[...], sent, 1, 1)[1:2, :]
        weighted = (partial * one[...].astype(F32)).astype(BF16)
        second = contract(jnp.ones((PAD, width), BF16), weighted, 1, 1)[0:1, :]
        for stat, line in enumerate((first, second)):
            for k in range(parts):
                piece = line[:, k * columns : (k + 1) * columns]
                lines[pl.ds((2 * i + stat) * parts + k, 1), :] = jnp.concatenate(
                    [piece] * (width // columns), axis=1
                )

        @pl.when(i == pl.num_programs(0) - 1)
        def _():
            part[rows:, :] = lines[...].astype(BF16)

    outs = [
        struct((rows, columns), F32),
        struct((rows, width), BF16),
        struct((rows, 3 * columns), BF16),
        struct(room.shape, BF16),
        struct((1, width), F32),
    ]
    args = (start, normed, scale, back, packed, grad, out_w, query, key, value, *weights, room)
    return call(
        "self_backward",
        kernel,
        place,
        (rows // IMG_LEN,),
        [
            turned_rows(IMG_LEN, width),
            by_rows(IMG_LEN, width),
            by_rows(IMG_LEN, 1),
            by_rows(IMG_LEN, width),
            fixed((PAD, width), at.vec // PAD),
            by_rows(IMG_LEN, width),
            fixed(out_w.shape),
        ]
        + [by_rows(IMG_LEN, columns)] * 3
        + [fixed(w.shape) for w in weights]
        + [pl.BlockSpec(memory_space=pl.ANY)],
        [
            by_rows(IMG_LEN, columns),
            by_rows(IMG_LEN, width),
            turned_rows(IMG_LEN, 3 * columns),
            fixed((rows + PAD, width)),
            fixed((1, width)),
        ],
        outs,
        args,
        scratch=[pltpu.VMEM((IMG_LEN, width), F32), pltpu.VMEM((PAD, width), F32)],
        aliases={len(args): 3},
    )


def self_end(place, mask, tokens, position_embed, vectors, stats, back, grad, gains, width):
    rows, columns = tokens.shape
    images = rows // IMG_LEN
    parts = IMG_LEN // columns

    def kernel(place, mask, tok, pos, vec, stat, tot, dn, g1, cross, feed, out, small):
        i = pl.program_id(0)
        masked = mask[...] > 0.0
        stream = first_stream(mask, tok, pos, vec)
        normal = (stream - stat[:, 0:1]) * stat[:, 1:2]
        normed_grad = dn[...].astype(F32)
        scaled = normed_grad * vec[1:2, :].astype(F32)
        line = lax.broadcasted_iota(jnp.int32, (PAD, 128), 0)
        lane = lax.broadcasted_iota(jnp.int32, (PAD, 128), 1)
        turned = [
            contract(
                tot[...],
                ((line == (2 * i + lane) * parts + k) & (lane < 2)).astype(F32).astype(BF16),
                0,
                0,
            )
            for k in range(parts)
        ]
        sums = jnp.concatenate(turned, axis=0) * (1.0 / width)
        total = g1[...] + stat[:, 1:2] * (scaled - sums[:, 0:1] - normal * sums[:, 1:2])
        out[...] = jnp.where(masked, 0.0, total).astype(BF16)

        @pl.when(i == 0)
        def _():
            small[...] = jnp.zeros_like(small)
            small[IMG_LEN + 2 : IMG_LEN + 3, :] = cross[...]
            small[IMG_LEN + 3 : IMG_LEN + 4, :] = feed[...]

        small[:IMG_LEN, :] += total
        small[IMG_LEN : IMG_LEN + 1, :] += jnp.sum(
            jnp.where(masked, total, 0.0), axis=0, keepdims=True
        )
        small[IMG_LEN + 1 : IMG_LEN + 2, :] += jnp.sum(normed_grad * normal, axis=0, keepdims=True)

    outs = [struct((rows, columns), BF16), struct((IMG_LEN + PAD, columns), F32)]
    own = pl.BlockSpec((1, columns), lambda i, place: (0, place[0]))
    return call(
        "self_end",
        kernel,
        place,
        (images,),
        [
            by_rows(IMG_LEN, 1),
            by_rows(IMG_LEN, columns),
            fixed((IMG_LEN, columns)),
            fixed((PAD, columns)),
            by_rows(IMG_LEN, 2),
            fixed((PAD, columns), rows // PAD),
            by_rows(IMG_LEN, columns),
            by_rows(IMG_LEN, columns),
            own,
            own,
        ],
        [by_rows(IMG_LEN, columns), fixed((IMG_LEN + PAD, columns))],
        outs,
        (mask, tokens, position_embed, vectors, stats, back, back, grad, *gains),
    )


def grad_sum(name, place, left_groups, right_groups, splits, block, spans):
    lefts, rights, terms = [], [], []
    for left_group, right_group in zip(left_groups, right_groups):
        left_base, right_base = len(lefts), len(rights)
        lefts += [p if isinstance(p, tuple) else (p, p.shape[0], None) for p, at in left_group]
        rights += [p if isinstance(p, tuple) else (p, p.shape[0], None) for p, at in right_group]
        for i, (_, left_at) in enumerate(left_group):
            for j, (_, right_at) in enumerate(right_group):
                left_rows, right_rows = lefts[left_base + i][1], rights[right_base + j][1]
                low = max(left_at, right_at)
                high = min(left_at + left_rows, right_at + right_rows)
                if low < high:
                    terms.append(
                        (left_base + i, low - left_at, right_base + j, low - right_at, high - low)
                    )
    (left_turn, height), (right_turn, width) = spans
    block = min(block, height)
    left_turn = left_turn * (height // block)
    left_count, right_count = len(lefts), len(rights)

    def kernel(place, *refs):
        left_refs = refs[:left_count]
        right_refs = refs[left_count : left_count + right_count]
        outs = refs[left_count + right_count :]
        total = None
        for li, left_row, ri, right_row, rows in terms:
            part = contract(
                left_refs[li][left_row : left_row + rows, :],
                right_refs[ri][right_row : right_row + rows, :],
                0,
                0,
            )
            total = part if total is None else total + part
        at = 0
        for out in outs:
            out[...] = total[:, at : at + out.shape[1]]
            at += out.shape[1]

    def spec(rows, wide, col, turn):
        return pl.BlockSpec(
            (rows, wide), lambda i, place: (0 if turn is None else turn(place), col(i))
        )

    outs = [struct((height, n), F32) for n in splits]
    return call(
        name,
        kernel,
        place,
        (height // block,),
        [spec(rows, block, lambda i: left_turn + i, turn) for _, rows, turn in lefts]
        + [spec(rows, width, lambda i: right_turn, turn) for _, rows, turn in rights],
        [pl.BlockSpec((block, n), lambda i, *_: (i, 0)) for n in splits],
        outs,
        [a for a, _, _ in (*lefts, *rights)],
    )


def text_grads(place, at, text, pair, text_groups, pair_groups, blocks):
    width = text.shape[1]
    text_rows = pair.shape[0]
    columns = pair.shape[1] // 2
    shards = width // columns
    step = min(4, shards)
    core_split = square_batch()
    pieces, rights, terms = [], [pair], []
    for text_group, pair_group in zip(text_groups, pair_groups):
        base = len(rights)
        rights += [piece for piece, _ in pair_group]
        for piece, row in text_group:
            pieces.append(piece)
            for k, (right, low) in enumerate(pair_group):
                if low <= row % text_rows < low + right.shape[0]:
                    terms.append((row // text_rows, row % text_rows - low, base + k))
    if not core_split:
        pieces, terms = [], []
        for k, text_group in enumerate(text_groups):
            for b in range(blocks):
                pieces.append(text_group[0][0][b * text_rows : (b + 1) * text_rows])
                terms.append((b, 0, k + 1))

    def which(s, place):
        return (s + place[0] % 2) % 2 if core_split else s

    def kernel(place, own, *refs):
        piece_refs = refs[: len(pieces)]
        right_refs = refs[len(pieces) : len(pieces) + len(rights)]
        key, value = refs[len(pieces) + len(rights) :]

        def run(s):
            total = contract(own[...], right_refs[0][...], 0, 0)
            for ref, (turn, row, k) in zip(piece_refs, terms):
                if turn == s:
                    total = total + contract(
                        ref[...], right_refs[k][row : row + ref.shape[0], :], 0, 0
                    )
            for t in range(step):
                rows = slice(t * columns, (t + 1) * columns)
                key[t, 0] = total[rows, :columns]
                value[t, 0] = total[rows, columns:]

        for s in range(blocks):
            pl.when(pl.program_id(0) == s)(lambda s=s: run(s))

    last = shards // step - 1

    def piece_spec(piece, turn):
        return pl.BlockSpec(
            (piece.shape[0], step * columns),
            lambda s, t, place: (0, jnp.where(s == turn, t, jnp.where(s > turn, last, 0))),
        )

    outs = [struct((shards, blocks, columns, columns), F32)] * 2
    out_spec = pl.BlockSpec(
        (step, 1, columns, columns), lambda s, t, place: (t, which(s, place), 0, 0)
    )
    key, value = call(
        "text_grads",
        kernel,
        place,
        (blocks, shards // step),
        [
            pl.BlockSpec(
                (text_rows, step * columns), lambda s, t, place: (at.text // text_rows + which(s, place), t)
            )
        ]
        + [piece_spec(p, term[0]) for p, term in zip(pieces, terms)]
        + [pl.BlockSpec(r.shape, lambda s, t, place: (0, 0)) for r in rights],
        [out_spec] * 2,
        outs,
        (text, *pieces, *rights),
    )
    return key.reshape(-1, columns), value.reshape(-1, columns)


class Plan:
    def __init__(self):
        self.makers, self.made = {}, {}

    def job(self, name, make):
        self.makers[name] = make

    def get(self, name):
        if name not in self.made:
            self.made[name] = self.makers[name]()
        return self.made[name]

    def behind(self, name, value):
        others = [self.get(n) for n in AFTER.get(name, ())]
        return tie(value, *others)[0] if others else value

    def tie(self, point, value):
        names = [n for n in self.makers if DONE_BY.get(n) == point]
        if not names:
            return value
        value, *done = tie(value, *[self.get(n) for n in names])
        self.made.update(zip(names, done))
        return value


class BatchSum:
    def __init__(self, name, place, products):
        self.name, self.place, self.products = name, place, products
        shapes = [
            (right.shape[1], left.shape[1]) if fold else (left.shape[1], right.shape[1])
            for left, right, fold in products
        ]
        if not square_batch():
            self.quarters = []
            return
        height, width = shapes[0]
        rows = height // 4

        def kernel(place, *refs):
            ins, outs, held = refs[: 2 * len(products)], refs[2 * len(products) : -1], refs[-1]
            for n, (_, _, fold) in enumerate(products):
                left, right = ins[2 * n], ins[2 * n + 1]
                if fold:
                    for at in range(0, width, height):
                        held[n, :, at : at + height] = contract(
                            left[:, at : at + height], right[...], 0, 0
                        ).astype(BF16)
                else:
                    held[n] = contract(left[...], right[...], 0, 0).astype(BF16)
                for k, out in enumerate(outs):
                    turn = pl.multiple_of((place[1] ^ k) * rows, rows)
                    out[n * rows : (n + 1) * rows, :] = held[n, pl.ds(turn, rows), :]

        args = [a for left, right, _ in products for a in (left, right)]
        outs = [struct((rows * len(products), width), BF16)] * 4
        self.quarters = call(
            name + "_parts",
            kernel,
            place,
            (1,),
            [fixed(a.shape) for a in args],
            [fixed(o.shape) for o in outs],
            outs,
            args,
            scratch=[pltpu.VMEM((len(products), height, width), BF16)],
        )
        self.height, self.width, self.rows = height, width, rows

    def step_one(self):
        if not square_batch():
            parts = [contract(left, right, 0, 0) for left, right, _ in self.products]
            return [lax.psum(p.astype(BF16), BATCH) for p in parts]
        return [hop(self.sent[k - 1], k) for k in (1, 2, 3)]

    def add(self, held):
        if not square_batch():
            return held
        total = self.quarters[0].astype(F32)
        for moved in held:
            total = total + moved.astype(F32)
        return [total.astype(BF16)]

    def step_two(self, held):
        if not square_batch():
            return held
        self.groups = self.move.step_two(held)
        return [self.low] + [piece for group in self.groups for piece, _ in group]

    def finish(self, held):
        if not square_batch():
            return [h.astype(F32) for h in held]
        height, width, rows = self.height, self.width, self.rows
        folds = [fold for _, _, fold in self.products]
        spots = [(0, 0)] + [
            (k + 1, first) for k, group in enumerate(self.groups) for _, first in group
        ]

        def kernel(place, *refs):
            ins, outs = refs[: len(held)], refs[len(held) :]
            for ref, (k, first) in zip(ins, spots):
                for n, (out, fold) in enumerate(zip(outs, folds)):
                    low, high = max(n * rows, first), min((n + 1) * rows, first + ref.shape[0])
                    if low >= high:
                        continue
                    count = high - low
                    at = pl.multiple_of((place[1] ^ k) * rows + low - n * rows, count)
                    piece = ref[low - first : high - first, :].astype(F32)
                    if fold:
                        for col in range(0, width, height):
                            out[pl.ds(col + at, count), :] = piece[:, col : col + height]
                    else:
                        out[pl.ds(at, count), :] = piece

        outs = [struct((width, height) if fold else (height, width), F32) for fold in folds]
        return call(
            self.name + "_finish",
            kernel,
            self.place,
            (1,),
            [fixed(a.shape) for a in held],
            [fixed(o.shape) for o in outs],
            outs,
            held,
        )


def body(
    tokens,
    captions,
    mask_counts,
    mask_positions,
    cotangent,
    mask_embed,
    position_embed,
    norm_self,
    query_self,
    key_self,
    value_self,
    out_self,
    norm_cross,
    query_cross,
    key_text,
    value_text,
    out_cross,
    norm_feed,
    up_weight,
    down_weight,
):
    rows, columns = tokens.shape
    width, hidden = query_self.shape[0], up_weight.shape[1]
    text_rows, text_blocks = captions.shape[0], captions.shape[1] // columns
    at = Packed(rows, text_rows * text_blocks)
    place = jnp.stack([lax.axis_index(TENSOR), lax.axis_index(BATCH)]).astype(jnp.int32)
    core = place[0] % 2
    shared = square_batch()
    packed, vectors, mask = pack_rows(
        at,
        mask_counts,
        mask_positions,
        tokens,
        captions,
        cotangent,
        position_embed,
        (mask_embed, norm_self, norm_cross, norm_feed),
    )
    packed = gather_cols(packed)

    text_part, seed_part = packed[at.text : at.seed], packed[at.seed : at.vec]
    if shared:
        text_part = lax.dynamic_slice_in_dim(packed, at.text + core * text_rows, text_rows, 0)
        seed_part = lax.dynamic_slice_in_dim(packed, at.seed + core * IMG_LEN, IMG_LEN, 0)
    else:
        seed_part = jnp.concatenate(
            [
                lax.dynamic_slice_in_dim(seed_part, core * IMG_LEN, IMG_LEN, 0),
                lax.dynamic_slice_in_dim(seed_part, (1 - core) * IMG_LEN, IMG_LEN, 0),
            ],
            axis=0,
        )
    plan = Plan()

    def spread(names, source, shared):
        near, far, cores = names
        move = Spread(None, shared)

        def one():
            move.array = plan.behind(near, source())
            return direct(move.array) if near in DIRECT else move.step_one()

        def two():
            held = plan.behind(far, plan.get(near))
            return held if near in DIRECT else move.step_two(held)

        plan.job(near, one)
        plan.job(far, two)
        plan.job(cores, lambda: move.swap(plan.get(far)))

    normed_self, query_one, key_one, value_one, mixed_self, partial, stats = self_forward(
        place, at, packed, query_self, key_self, value_self, out_self
    )
    spread((T1, T2, T3), lambda: text_part, shared)
    spread((X1, X2, X3), lambda: normed_self[:IMG_LEN] if shared else normed_self, shared)
    spread((Y1, Y2, Y3), lambda: seed_part, shared)
    plan.job(KV, lambda: text_project(place, at, packed, key_text, value_text))
    plan.job(DA, lambda: seed_product(place, at, packed, down_weight))
    scattered = plan.tie(SCATTERED1, scatter_cols(partial))
    mixed_out = plan.tie(MIXED1, gather_cols(scattered))
    key_two, value_two = plan.get(KV)

    stream_one, normed_cross, query_two, mixed_cross, partial, scale_cross = cross_forward(
        place, at, packed, mixed_out, query_cross, key_two, value_two, out_cross
    )
    partial = plan.tie(PARTIAL2, partial)
    scattered = plan.tie(SCATTERED2, scatter_cols(partial))
    mixed_out = plan.tie(MIXED2, gather_cols(scattered))

    own_two, scale_feed, normed_feed, activation, hidden_grad, partial = feed_both(
        place, at, stream_one, mixed_out, packed, plan.get(DA), up_weight
    )
    spread((F1, F2, F3), lambda: normed_feed[:IMG_LEN] if shared else normed_feed, shared)
    spread((A1, A2, A3), lambda: activation, False)
    spread((U1, U2, U3), lambda: hidden_grad, False)
    plan.job(OUT, lambda: out_product(place, plan.behind(OUT, activation), down_weight))
    partial = plan.tie(PARTIAL3, partial)
    scattered = plan.tie(SCATTERED3, scatter_cols(partial))
    feed_back = plan.tie(MIXED3, gather_cols(scattered))

    seed_cross, query_grad, pair, partial, feed_gain = cross_backward(
        place,
        at,
        normed_feed,
        scale_feed,
        feed_back,
        packed,
        packed,
        out_cross,
        query_two,
        key_two,
        value_two,
        query_cross,
        plan.get(OUT),
    )
    own_seed = [
        ((packed, IMG_LEN, lambda p: at.seed // IMG_LEN + p[0] % 2), 0),
        ((packed, IMG_LEN, lambda p: at.seed // IMG_LEN + 1 - p[0] % 2), IMG_LEN),
    ]
    plan.job(GD,
        lambda: grad_sum(
            "down_grads",
            place,
            [[(plan.behind(GD, activation), 0)], *plan.get(A2)],
            [own_seed, *plan.get(Y3)],
            (width,),
            256,
            ((0, hidden), (0, width)),
        ),
    )
    plan.job(GU,
        lambda: grad_sum(
            "up_grads",
            place,
            [[(plan.behind(GU, normed_feed), 0)], *plan.get(F3)],
            [[(hidden_grad, 0)], *plan.get(U2)],
            (hidden,),
            512,
            ((0, width), (0, hidden)),
        ),
    )
    cross_sum = BatchSum(
        "cross", place, [(mixed_cross, seed_cross, False), (normed_cross, query_grad, True)]
    )

    def batch_sum(names, total):
        make, out, add, near, far = names
        plan.job(make, lambda: total.quarters)

        def one():
            total.sent = plan.behind(out, plan.get(make)[1:])
            return total.step_one()

        def back():
            (total.low, *_) = held = plan.behind(near, plan.get(add))
            if not shared:
                return held
            total.move = Spread(total.low, False)
            return direct(total.low) if near in DIRECT else total.move.step_one()

        def rest():
            held = plan.behind(far, plan.get(near))
            if near in DIRECT and shared:
                total.groups = held
                return [total.low] + [piece for group in held for piece, _ in group]
            return total.step_two(held)

        plan.job(out, one)
        plan.job(add, lambda: total.add(plan.behind(add, plan.get(out))))
        plan.job(near, back)
        plan.job(far, rest)

    batch_sum((C0, C1, CA, C2, C3), cross_sum)
    plan.job(TB,
        lambda: text_back(
            place, plan.behind(TB, pair), key_text, value_text, rows + PAD, width
        ),
    )
    spread((D1, D2, D3), lambda: pair, False)
    plan.job(GT,
        lambda: text_grads(
            place,
            at,
            packed,
            plan.behind(GT, pair),
            plan.get(T3),
            plan.get(D2),
            text_blocks,
        ),
    )
    partial = plan.tie(PARTIAL4, partial)
    scattered = plan.tie(SCATTERED4, scatter_cols(partial))
    out_slice = scattered[rows:]
    cross_back = plan.tie(MIXED4, gather_cols(scattered[:rows]))

    own_one, seed_self, triple, partial, cross_gain = self_backward(
        place,
        at,
        normed_self,
        normed_cross,
        scale_cross,
        cross_back,
        packed,
        seed_cross,
        out_self,
        query_one,
        key_one,
        value_one,
        (query_self, key_self, value_self),
        plan.get(TB),
    )
    layer_out = (own_two + out_slice.astype(F32)).astype(BF16)
    self_sum = BatchSum("self", place, [(mixed_self, seed_self, False)])
    batch_sum((S0, S1, SA, S2, S3), self_sum)
    spread((Q1, Q2, Q3), lambda: triple, False)
    plan.job(GQ,
        lambda: grad_sum(
            "self_grads",
            place,
            [[(plan.behind(GQ, normed_self), 0)], *plan.get(X3)],
            [[(triple, 0)], *plan.get(Q2)],
            (columns,) * 3,
            512,
            ((0, width), (0, 3 * columns)),
        ),
    )
    partial = plan.tie(PARTIAL5, partial)
    scattered = plan.tie(SCATTERED5, scatter_cols(partial))
    low = rows + PAD
    captions_grad = jnp.concatenate(
        [
            scattered[low + k * text_rows : low + (k + 1) * text_rows]
            for k in range(text_blocks)
        ],
        axis=1,
    )
    tokens_grad, small = self_end(
        place,
        mask,
        tokens,
        position_embed,
        vectors,
        stats,
        scattered,
        own_one,
        (cross_gain, feed_gain),
        width,
    )
    small = plan.tie(SMALL, small)
    seen = small
    plan.job(SM, lambda: seen)
    plan.job(CF, lambda: cross_sum.finish(plan.behind(CF, plan.get(C3))))
    plan.job(SF, lambda: self_sum.finish(plan.behind(SF, plan.get(S3))))
    small = direct_sum(small)
    (down_grad,) = plan.get(GD)
    (up_grad,) = plan.get(GU)
    key_text_grad, value_text_grad = plan.get(GT)
    query_self_grad, key_self_grad, value_self_grad = plan.get(GQ)
    out_cross_grad, query_cross_grad = plan.get(CF)
    (out_self_grad,) = plan.get(SF)
    return (
        layer_out,
        tokens_grad,
        captions_grad,
        small[IMG_LEN],
        small[:IMG_LEN],
        small[IMG_LEN + 1],
        query_self_grad,
        key_self_grad,
        value_self_grad,
        out_self_grad,
        small[IMG_LEN + 2],
        query_cross_grad,
        key_text_grad,
        value_text_grad,
        out_cross_grad,
        small[IMG_LEN + 3],
        up_grad,
        down_grad,
    )


def solution(mesh):
    return jax.shard_map(
        body,
        mesh=mesh,
        in_specs=(
            P(BATCH, TENSOR),
            P(BATCH, TENSOR),
            P(BATCH),
            P(BATCH, None),
            P(BATCH, TENSOR),
            P(TENSOR),
            P(None, TENSOR),
            P(TENSOR),
            P(None, TENSOR),
            P(None, TENSOR),
            P(None, TENSOR),
            P(TENSOR, None),
            P(TENSOR),
            P(None, TENSOR),
            P(None, TENSOR),
            P(None, TENSOR),
            P(TENSOR, None),
            P(TENSOR),
            P(None, TENSOR),
            P(TENSOR, None),
        ),
        out_specs=(
            P(BATCH, TENSOR),
            P(BATCH, TENSOR),
            P(BATCH, TENSOR),
            P(TENSOR),
            P(None, TENSOR),
            P(TENSOR),
            P(None, TENSOR),
            P(None, TENSOR),
            P(None, TENSOR),
            P(TENSOR, None),
            P(TENSOR),
            P(None, TENSOR),
            P(None, TENSOR),
            P(None, TENSOR),
            P(TENSOR, None),
            P(TENSOR),
            P(None, TENSOR),
            P(TENSOR, None),
        ),
        check_vma=False,
    )
```

```python
import jax
import jax.numpy as jnp
from jax import lax
from jax.experimental import pallas as pl
from jax.experimental.pallas import tpu as pltpu
from jax.sharding import PartitionSpec as P

HEAD_DIM = 128
IMG_LEN = 256
EPS = 1e-06
F32 = jnp.float32
BF16 = jnp.bfloat16
INV_ROOT = float(HEAD_DIM) ** (-0.5)
PAD = 16
BATCH, TENSOR = "batch", "tensor"
(
    T1, T2, T3, X1, X2, X3, Y1, Y2, Y3, KV, DA, F1, F2, F3, A1, A2, A3, U1, U2, U3, OUT, GD, GU,
    C0, C1, CA, C2, C3, TB, D1, D2, D3, GT, S0, S1, SA, S2, S3, Q1, Q2, Q3, GQ, SM, CF, SF,
) = range(45)
(
    SCATTERED1, MIXED1, PARTIAL2, SCATTERED2, MIXED2, PARTIAL3, SCATTERED3, MIXED3, PARTIAL4,
    SCATTERED4, MIXED4, PARTIAL5, SCATTERED5, SMALL,
) = range(14)
DONE_BY = {
    T1: SCATTERED1, KV: SCATTERED1, T2: PARTIAL2, X1: MIXED1, X2: SCATTERED2, T3: SCATTERED2,
    DA: SCATTERED2, Y1: PARTIAL3, X3: SCATTERED2, Y2: PARTIAL3, F1: SCATTERED3, OUT: MIXED3,
    Y3: SCATTERED3, F2: MIXED3, A1: PARTIAL4, A2: MIXED4, F3: MIXED3, C0: SCATTERED4,
    TB: SCATTERED4, U1: SCATTERED4, C1: PARTIAL5, GD: SCATTERED4, U2: MIXED4, GU: SCATTERED5,
    GT: MIXED4, Q1: SMALL, Q2: SCATTERED5, S0: SCATTERED5, D2: PARTIAL5, GQ: SCATTERED5, C2: SMALL,
}
AFTER = {
    A1: (F2,), U1: (A2,), S1: (Q2,), F1: (Y3,), CF: (SM,), SF: (SM,), D1: (U1,), SA: (SM,),
}
DIRECT = (C2, D1, Q1,)
COST = dict(
    self_forward=17, text_project=25, cross_forward=0, seed_product=3, feed_both=6, out_product=15,
    cross_backward=20, self_backward=27, self_end=10, text_back=8, down_grads=0, up_grads=14,
    text_grads=15, self_grads=40, cross_parts=0, self_parts=10, cross_finish=0, self_finish=0,
)


def contract(left, right, left_dim, right_dim):
    return lax.dot_general(
        left, right, (((left_dim,), (right_dim,)), ((), ())), preferred_element_type=F32
    )


def tie(*values):
    leaves, tree = jax.tree.flatten(values)
    arrays = iter(lax.optimization_barrier([v for v in leaves if not isinstance(v, int)]))
    return tree.unflatten([v if isinstance(v, int) else next(arrays) for v in leaves])


def gather_cols(array):
    return lax.all_gather(array, TENSOR, axis=1, tiled=True)


def scatter_cols(array):
    return lax.psum_scatter(array, TENSOR, scatter_dimension=1, tiled=True)


def square_batch():
    return lax.axis_size(BATCH) == 4


def hop(array, flip):
    pairs = [(i, i ^ flip) for i in range(lax.axis_size(BATCH))]
    return lax.ppermute(array, BATCH, pairs)


def swap_core(array):
    pairs = [(i, i ^ 1) for i in range(lax.axis_size(TENSOR))]
    return lax.ppermute(array, TENSOR, pairs)


def ring_others(array):
    size, own = lax.axis_size(BATCH), lax.axis_index(BATCH)
    whole = lax.all_gather(array, BATCH, axis=0, tiled=False)
    return [
        lax.dynamic_index_in_dim(whole, lax.rem(own + k, size), 0, keepdims=False)
        for k in range(1, size)
    ]


def direct(array):
    moved = [hop(array, k) for k in (1, 2, 3)] if square_batch() else ring_others(array)
    return [[(m, 0)] for m in moved]


class Spread:
    def __init__(self, array, shared):
        self.array, self.shared = array, shared

    def step_one(self):
        if not square_batch():
            return ring_others(self.array)
        return [hop(self.array, 1), hop(self.array, 2)]

    def step_two(self, held):
        rows = self.array.shape[0]
        if square_batch():
            cut = rows // 2
            along, across = held
            groups = [
                [(along, 0)],
                [(across, 0)],
                [(hop(along[:cut], 2), 0), (hop(across[cut:], 1), cut)],
            ]
        else:
            groups = [[(piece, 0)] for piece in held]
        return groups

    def swap(self, groups):
        if self.shared:
            rows = self.array.shape[0]
            groups = [g + [(swap_core(piece), rows + at) for piece, at in g] for g in groups]
        return groups


def direct_sum(array):
    if not square_batch():
        return lax.psum(array.astype(BF16), BATCH).astype(F32)
    low = array.astype(BF16)
    moved = [hop(low, k) for k in (1, 2, 3)]
    return array + moved[0].astype(F32) + moved[1].astype(F32) + moved[2].astype(F32)


def params():
    return pltpu.CompilerParams(vmem_limit_bytes=56 << 20)


def cost(micros):
    return pl.CostEstimate(
        flops=1000, bytes_accessed=int(1e6 * micros) + 1000, transcendentals=0
    )


def struct(shape, dtype):
    return jax.ShapeDtypeStruct(shape, dtype)


def by_rows(rows, width, first=0):
    return pl.BlockSpec((rows, width), lambda i, *_: (first + i, 0))


def turned_rows(rows, width):
    blocks = IMG_LEN // rows
    return pl.BlockSpec((rows, width), lambda i, place: (image_turn(i, place, blocks), 0))


def fixed(shape, row=0, col=0):
    return pl.BlockSpec(shape, lambda i, *_: (row, col))


def call(name, kernel, place, grid, in_specs, out_specs, outs, args, scratch=(), aliases=None):
    return pl.pallas_call(
        kernel,
        grid_spec=pltpu.PrefetchScalarGridSpec(
            num_scalar_prefetch=1,
            grid=grid,
            in_specs=in_specs,
            out_specs=out_specs,
            scratch_shapes=list(scratch),
        ),
        out_shape=outs,
        input_output_aliases=aliases or {},
        compiler_params=params(),
        cost_estimate=cost(COST[name]),
        name=name,
    )(place, *args)


def core_of(place):
    return place[0] % 2


class Packed:
    def __init__(self, rows, text_rows):
        self.rows = rows
        self.text = rows
        self.seed = self.text + text_rows
        self.vec = self.seed + rows
        self.total = self.vec + PAD


def pack_rows(at, counts, positions, tokens, captions, cotangent, position_embed, vectors):
    rows, columns = tokens.shape
    images = rows // IMG_LEN
    text_rows = captions.shape[0]
    text_blocks = captions.shape[1] // columns

    def kernel(counts, order, tok, cap, cot, pos, *rest):
        out, block, mask = rest[-3:]
        for k in range(text_blocks):
            low = at.text + k * text_rows
            out[low : low + text_rows, :] = cap[:, k * columns : (k + 1) * columns]
        lines = [v[...].astype(F32).reshape(1, columns) for v in rest[:-3]]
        lines.append(jnp.zeros((PAD - len(lines), columns), F32))
        vec = jnp.concatenate(lines, axis=0).astype(BF16)
        out[at.vec :, :] = vec
        block[...] = vec
        place = lax.broadcasted_iota(jnp.int32, (IMG_LEN, IMG_LEN), 0)
        slot = lax.broadcasted_iota(jnp.int32, (IMG_LEN, IMG_LEN), 1)
        for i in range(images):
            hit = (order[i : i + 1, :] == place) & (slot < counts[i])
            column = jnp.max(hit.astype(F32), axis=1, keepdims=True)
            own = slice(i * IMG_LEN, (i + 1) * IMG_LEN)
            mask[own, :] = column
            base = jnp.where(column > 0.0, vec[0:1, :].astype(F32), tok[own, :].astype(F32))
            out[own, :] = (base + pos[...].astype(F32)).astype(BF16)
            out[at.seed + i * IMG_LEN : at.seed + (i + 1) * IMG_LEN, :] = jnp.where(
                column > 0.0, cot[own, :].astype(F32), 0.0
            ).astype(BF16)

    vmem = pl.BlockSpec(memory_space=pltpu.VMEM)
    outs = [
        struct((at.total, columns), BF16),
        struct((PAD, columns), BF16),
        struct((rows, 1), F32),
    ]
    args = (counts, positions, tokens, captions, cotangent, position_embed, *vectors)
    return pl.pallas_call(
        kernel,
        in_specs=[pl.BlockSpec(memory_space=pltpu.SMEM)] + [vmem] * (len(args) - 1),
        out_specs=[vmem] * 3,
        out_shape=outs,
        compiler_params=params(),
        cost_estimate=cost(2),
        name="pack_rows",
    )(*args)


def normalize(stream):
    width = stream.shape[1]
    mean = jnp.sum(stream, axis=1, keepdims=True) * (1.0 / width)
    var = jnp.sum(stream * stream, axis=1, keepdims=True) * (1.0 / width) - mean * mean
    inv_std = lax.rsqrt(var + EPS)
    return (stream - mean) * inv_std, mean, inv_std


def norm_back(grad, normed, inv_std, gain):
    width = grad.shape[1]
    normal = normed * (1.0 / gain)
    scaled = grad * gain
    first = jnp.sum(scaled, axis=1, keepdims=True) * (1.0 / width)
    second = jnp.sum(grad * normed, axis=1, keepdims=True) * (1.0 / width)
    back = inv_std * (scaled - first - normal * second)
    return back, jnp.sum(grad * normal, axis=0, keepdims=True)


def probabilities(query, key):
    scores = contract(query, key, 1, 1) * INV_ROOT
    terms = jnp.exp(scores - jnp.max(scores, axis=1, keepdims=True))
    return terms * (1.0 / jnp.sum(terms, axis=1, keepdims=True))


def head_slices(width):
    return [slice(at, at + HEAD_DIM) for at in range(0, width, HEAD_DIM)]


def attend(query, key, value):
    mixed = [
        contract(probabilities(query[:, h], key[:, h]).astype(BF16), value[:, h], 1, 0)
        for h in head_slices(query.shape[1])
    ]
    return jnp.concatenate(mixed, axis=1).astype(BF16)


def attend_back(grad, query, key, value):
    parts = []
    for h in head_slices(query.shape[1]):
        probs = probabilities(query[:, h], key[:, h])
        prob_grad = contract(grad[:, h], value[:, h], 1, 1)
        inner = jnp.sum(probs * prob_grad, axis=1, keepdims=True)
        score_grad = (probs * (prob_grad - inner)).astype(BF16)
        parts.append(
            (
                contract(score_grad, key[:, h], 1, 0) * INV_ROOT,
                contract(score_grad, query[:, h], 0, 0) * INV_ROOT,
                contract(probs.astype(BF16), grad[:, h], 0, 0),
            )
        )
    return [jnp.concatenate(group, axis=1).astype(BF16) for group in zip(*parts)]


def first_stream(mask, tok, pos, vec):
    base = jnp.where(mask[...] > 0.0, vec[0:1, :].astype(F32), tok[...].astype(F32))
    return base + pos[...].astype(F32)


def packed_specs(at, width):
    return [by_rows(IMG_LEN, width), fixed((PAD, width), at.vec // PAD)]


def self_forward(place, at, packed, query_w, key_w, value_w, out_w):
    rows, width = at.rows, packed.shape[1]
    columns = query_w.shape[1]

    def kernel(
        place, zero, vec, wq, wk, wv, wo, normed, query, key, value, mixed, part, stats
    ):
        normal, mean, inv_std = normalize(zero[...].astype(F32))
        stats[:, 0:1] = mean
        stats[:, 1:2] = inv_std
        low = (normal * vec[1:2, :].astype(F32)).astype(BF16)
        normed[...] = low
        q = contract(low, wq[...], 1, 0).astype(BF16)
        k = contract(low, wk[...], 1, 0).astype(BF16)
        v = contract(low, wv[...], 1, 0).astype(BF16)
        query[...], key[...], value[...] = q, k, v
        a = attend(q, k, v)
        mixed[...] = a
        part[...] = contract(a, wo[...], 1, 0).astype(BF16)

    outs = [struct((rows, width), BF16)] + [struct((rows, columns), BF16)] * 4
    outs += [struct((rows, width), BF16), struct((rows, 2), F32)]
    args = (packed, packed, query_w, key_w, value_w, out_w)
    return call(
        "self_forward",
        kernel,
        place,
        (rows // IMG_LEN,),
        packed_specs(at, width) + [fixed(w.shape) for w in (query_w, key_w, value_w, out_w)],
        [turned_rows(IMG_LEN, width)] + [by_rows(IMG_LEN, o.shape[1]) for o in outs[1:]],
        outs,
        args,
    )


def text_project(place, at, text, key_w, value_w):
    columns = key_w.shape[1]
    width = text.shape[1]
    shards = width // columns
    blocks = key_w.shape[0] // width
    text_rows = (at.seed - at.text) // blocks
    first = at.text // text_rows
    step = min(4, shards)

    def kernel(place, *refs):
        texts, (wk, wv, key, value, key_sum, value_sum) = refs[:blocks], refs[blocks:]

        @pl.when(pl.program_id(0) == 0)
        def _():
            key_sum[...] = jnp.zeros_like(key_sum)
            value_sum[...] = jnp.zeros_like(value_sum)

        for t in range(step):
            for k, text in enumerate(texts):
                piece = text[:, t * columns : (t + 1) * columns]
                key_sum[...] += contract(piece, wk[t, k], 1, 0)
                value_sum[...] += contract(piece, wv[t, k], 1, 0)

        @pl.when(pl.program_id(0) == pl.num_programs(0) - 1)
        def _():
            key[...] = key_sum[...].astype(BF16)
            value[...] = value_sum[...].astype(BF16)

    cut = (shards, blocks, columns, columns)
    outs = [struct((text_rows, columns), BF16)] * 2
    weight = pl.BlockSpec((step, *cut[1:]), lambda i, *_: (i, 0, 0, 0))
    args = (*[text] * blocks, key_w.reshape(cut), value_w.reshape(cut))
    return call(
        "text_project",
        kernel,
        place,
        (shards // step,),
        [
            pl.BlockSpec((text_rows, step * columns), lambda i, *_, k=k: (first + k, i))
            for k in range(blocks)
        ]
        + [weight] * 2,
        [fixed(o.shape) for o in outs],
        outs,
        args,
        scratch=[pltpu.VMEM((text_rows, columns), F32)] * 2,
    )


def cross_forward(place, at, packed, added, query_w, key, value, out_w):
    rows, width = at.rows, packed.shape[1]
    columns = query_w.shape[1]
    text_rows = key.shape[0] // (rows // IMG_LEN)

    def kernel(
        place, zero, vec, add, wq, k, v, wo, stream, normed, query, mixed, part, scale
    ):
        one = zero[...].astype(F32) + add[...].astype(F32)
        stream[...] = one.astype(BF16)
        normal, mean, inv_std = normalize(one)
        scale[...] = inv_std
        low = (normal * vec[2:3, :].astype(F32)).astype(BF16)
        normed[...] = low
        q = contract(low, wq[...], 1, 0).astype(BF16)
        query[...] = q
        a = attend(q, k[...], v[...])
        mixed[...] = a
        part[...] = contract(a, wo[...], 1, 0).astype(BF16)

    outs = [struct((rows, width), BF16)] * 2
    outs += [struct((rows, columns), BF16)] * 2 + [struct((rows, width), BF16)]
    outs += [struct((rows, 1), F32)]
    args = (packed, packed, added, query_w, key, value, out_w)
    return call(
        "cross_forward",
        kernel,
        place,
        (rows // IMG_LEN,),
        packed_specs(at, width)
        + [
            by_rows(IMG_LEN, width),
            fixed(query_w.shape),
            by_rows(text_rows, columns),
            by_rows(text_rows, columns),
            fixed(out_w.shape),
        ],
        [by_rows(IMG_LEN, o.shape[1]) for o in outs],
        outs,
        args,
    )


def seed_product(place, at, seed, down_w):
    rows, (hidden, width) = at.rows, down_w.shape

    def kernel(place, seed, down, out):
        out[...] = contract(seed[...], down[...], 1, 1)

    outs = [struct((rows, hidden), F32)]
    return call(
        "seed_product",
        kernel,
        place,
        (rows // IMG_LEN,),
        [by_rows(IMG_LEN, width, at.seed // IMG_LEN), fixed(down_w.shape)],
        [by_rows(IMG_LEN, hidden)],
        outs,
        (seed, down_w),
    )[0]


def gelu_parts(u):
    scale = 0.7978845608028654
    square = u * u
    bend = jnp.tanh(scale * (u + 0.044715 * square * u))
    half = 0.5 * (1.0 + bend)
    slope = half + 0.5 * u * (1.0 - bend * bend) * scale * (1.0 + 3.0 * 0.044715 * square)
    return u * half, slope


def image_turn(i, place, blocks):
    return (i // blocks + place[0] % 2) % 2 * blocks + i % blocks


def feed_both(place, at, stream, added, packed, act_grad, up_w):
    rows, width = stream.shape
    hidden, columns = up_w.shape[1], width // lax.axis_size(TENSOR)
    block = IMG_LEN

    def kernel(place, one, add, vec, dact, up, slim, scale, normed, act, grad, part, two):
        stream = one[...].astype(F32) + add[...].astype(F32)
        two[...] = stream
        slim[...] = two[:, pl.ds(pl.multiple_of(place[0] * columns, columns), columns)]
        normal, mean, inv_std = normalize(stream)
        scale[...] = inv_std
        low = (normal * vec[3:4, :].astype(F32)).astype(BF16)
        normed[...] = low
        value, slope = gelu_parts(contract(low, up[...], 1, 0))
        act[...] = value.astype(BF16)
        du = (dact[...] * slope).astype(BF16)
        grad[...] = du
        part[...] = contract(du, up[...], 1, 1).astype(BF16)

    outs = [
        struct((rows, columns), F32),
        struct((rows, 1), F32),
        struct((rows, width), BF16),
        struct((rows, hidden), BF16),
        struct((rows, hidden), BF16),
        struct((rows, width), BF16),
    ]
    args = (stream, added, packed, act_grad, up_w)
    return call(
        "feed_both",
        kernel,
        place,
        (rows // block,),
        [
            by_rows(block, width),
            by_rows(block, width),
            fixed((PAD, width), at.vec // PAD),
            by_rows(block, hidden),
            fixed(up_w.shape),
        ],
        [
            by_rows(block, columns),
            by_rows(block, 1),
            turned_rows(block, width),
            turned_rows(block, hidden),
            turned_rows(block, hidden),
            by_rows(block, width),
        ],
        outs,
        args,
        scratch=[pltpu.VMEM((block, width), F32)],
    )


def out_product(place, activation, down_w):
    rows, (hidden, width) = activation.shape[0], down_w.shape

    def kernel(place, act, down, out):
        out[...] = contract(act[...], down[...], 1, 0).astype(BF16)

    outs = [struct((2 * rows, width), BF16)]
    return call(
        "out_product",
        kernel,
        place,
        (rows // IMG_LEN,),
        [
            turned_rows(IMG_LEN, hidden),
            fixed(down_w.shape),
        ],
        [by_rows(IMG_LEN, width, rows // IMG_LEN)],
        outs,
        (activation, down_w),
    )[0]


def cross_backward(
    place, at, normed, scale, back, seed, packed, out_w, query, key, value, query_w, room
):
    rows, width = normed.shape
    columns = query.shape[1]
    text_rows = key.shape[0] // (rows // IMG_LEN)

    def kernel(place, three, inv, dn, g3, vec, wo, q, k, v, wq, room, low, dq, dkv, part, gain):
        step, gain_step = norm_back(
            dn[...].astype(F32), three[...].astype(F32), inv[...], vec[3:4, :].astype(F32)
        )
        total = g3[...].astype(F32) + step
        y = total.astype(BF16)
        low[...] = y

        @pl.when(pl.program_id(0) == 0)
        def _():
            gain[...] = jnp.zeros_like(gain)

        gain[...] += gain_step
        da = contract(y, wo[...], 1, 1).astype(BF16)
        query_grad, key_grad, value_grad = attend_back(da, q[...], k[...], v[...])
        dq[...] = query_grad
        dkv[:, :columns] = key_grad
        dkv[:, columns:] = value_grad
        part[...] = contract(query_grad, wq[...], 1, 1).astype(BF16)

    outs = [
        struct((rows, width), BF16),
        struct((rows, columns), BF16),
        struct((key.shape[0], 2 * columns), BF16),
        struct(room.shape, BF16),
        struct((1, width), F32),
    ]
    args = (normed, scale, back, seed, packed, out_w, query, key, value, query_w, room)
    return call(
        "cross_backward",
        kernel,
        place,
        (rows // IMG_LEN,),
        [
            turned_rows(IMG_LEN, width),
            by_rows(IMG_LEN, 1),
            by_rows(IMG_LEN, width),
            by_rows(IMG_LEN, width, at.seed // IMG_LEN),
            fixed((PAD, width), at.vec // PAD),
            fixed(out_w.shape),
            by_rows(IMG_LEN, columns),
            by_rows(text_rows, columns),
            by_rows(text_rows, columns),
            fixed(query_w.shape),
            pl.BlockSpec(memory_space=pl.ANY),
        ],
        [
            by_rows(IMG_LEN, width),
            by_rows(IMG_LEN, columns),
            by_rows(text_rows, 2 * columns),
            by_rows(IMG_LEN, width),
            fixed((1, width)),
        ],
        outs,
        args,
        aliases={len(args): 3},
    )


def text_back(place, pair, key_w, value_w, rows, width):
    columns = key_w.shape[1]
    shards = width // columns
    blocks = key_w.shape[0] // width
    text_rows = pair.shape[0]
    cut = (shards, blocks, columns, columns)

    def kernel(place, grads, wk, wv, out):
        for t in range(step):
            cols = slice(t * columns, (t + 1) * columns)
            for k in range(blocks):
                part = contract(grads[:, :columns], wk[t, k], 1, 1) + contract(
                    grads[:, columns:], wv[t, k], 1, 1
                )
                out[k * text_rows : (k + 1) * text_rows, cols] = part.astype(BF16)
        out[blocks * text_rows :, :] = jnp.zeros(
            (rows - blocks * text_rows, step * columns), BF16
        )

    step = min(4, shards)
    weight = pl.BlockSpec((step, *cut[1:]), lambda i, *_: (i, 0, 0, 0))
    outs = [struct((2 * rows, width), BF16)]
    return call(
        "text_back",
        kernel,
        place,
        (shards // step,),
        [fixed(pair.shape), weight, weight],
        [pl.BlockSpec((rows, step * columns), lambda i, *_: (1, i))],
        outs,
        (pair, key_w.reshape(cut), value_w.reshape(cut)),
    )[0]


def self_backward(
    place, at, start, normed, scale, back, packed, grad, out_w, query, key, value, weights, room
):
    rows, width = normed.shape
    columns = query.shape[1]
    parts = IMG_LEN // columns

    def kernel(
        place, one, two, inv, dn, vec, g2, wo, q, k, v, wq, wk, wv, room, mine, low, triple, part, gain, held, lines
    ):
        i = pl.program_id(0)
        step, gain_step = norm_back(
            dn[...].astype(F32), two[...].astype(F32), inv[...], vec[2:3, :].astype(F32)
        )
        total = g2[...].astype(F32) + step
        held[...] = total
        mine[...] = held[:, pl.ds(pl.multiple_of(place[0] * columns, columns), columns)]
        y = total.astype(BF16)
        low[...] = y

        @pl.when(i == 0)
        def _():
            gain[...] = jnp.zeros_like(gain)
            lines[...] = jnp.zeros_like(lines)

        gain[...] += gain_step
        da = contract(y, wo[...], 1, 1).astype(BF16)
        query_grad, key_grad, value_grad = attend_back(da, q[...], k[...], v[...])
        triple[:, :columns] = query_grad
        triple[:, columns : 2 * columns] = key_grad
        triple[:, 2 * columns :] = value_grad
        partial = (
            contract(query_grad, wq[...], 1, 1)
            + contract(key_grad, wk[...], 1, 1)
            + contract(value_grad, wv[...], 1, 1)
        )
        sent = partial.astype(BF16)
        part[pl.ds(pl.multiple_of(i * IMG_LEN, IMG_LEN), IMG_LEN), :] = sent
        first = contract(vec[...], sent, 1, 1)[1:2, :]
        weighted = (partial * one[...].astype(F32)).astype(BF16)
        second = contract(jnp.ones((PAD, width), BF16), weighted, 1, 1)[0:1, :]
        for stat, line in enumerate((first, second)):
            for k in range(parts):
                piece = line[:, k * columns : (k + 1) * columns]
                lines[pl.ds((2 * i + stat) * parts + k, 1), :] = jnp.concatenate(
                    [piece] * (width // columns), axis=1
                )

        @pl.when(i == pl.num_programs(0) - 1)
        def _():
            part[rows:, :] = lines[...].astype(BF16)

    outs = [
        struct((rows, columns), F32),
        struct((rows, width), BF16),
        struct((rows, 3 * columns), BF16),
        struct(room.shape, BF16),
        struct((1, width), F32),
    ]
    args = (start, normed, scale, back, packed, grad, out_w, query, key, value, *weights, room)
    return call(
        "self_backward",
        kernel,
        place,
        (rows // IMG_LEN,),
        [
            turned_rows(IMG_LEN, width),
            by_rows(IMG_LEN, width),
            by_rows(IMG_LEN, 1),
            by_rows(IMG_LEN, width),
            fixed((PAD, width), at.vec // PAD),
            by_rows(IMG_LEN, width),
            fixed(out_w.shape),
        ]
        + [by_rows(IMG_LEN, columns)] * 3
        + [fixed(w.shape) for w in weights]
        + [pl.BlockSpec(memory_space=pl.ANY)],
        [
            by_rows(IMG_LEN, columns),
            by_rows(IMG_LEN, width),
            turned_rows(IMG_LEN, 3 * columns),
            fixed((rows + PAD, width)),
            fixed((1, width)),
        ],
        outs,
        args,
        scratch=[pltpu.VMEM((IMG_LEN, width), F32), pltpu.VMEM((PAD, width), F32)],
        aliases={len(args): 3},
    )


def self_end(place, mask, tokens, position_embed, vectors, stats, back, grad, gains, width):
    rows, columns = tokens.shape
    images = rows // IMG_LEN
    parts = IMG_LEN // columns

    def kernel(place, mask, tok, pos, vec, stat, tot, dn, g1, cross, feed, out, small):
        i = pl.program_id(0)
        masked = mask[...] > 0.0
        stream = first_stream(mask, tok, pos, vec)
        normal = (stream - stat[:, 0:1]) * stat[:, 1:2]
        normed_grad = dn[...].astype(F32)
        scaled = normed_grad * vec[1:2, :].astype(F32)
        line = lax.broadcasted_iota(jnp.int32, (PAD, 128), 0)
        lane = lax.broadcasted_iota(jnp.int32, (PAD, 128), 1)
        turned = [
            contract(
                tot[...],
                ((line == (2 * i + lane) * parts + k) & (lane < 2)).astype(F32).astype(BF16),
                0,
                0,
            )
            for k in range(parts)
        ]
        sums = jnp.concatenate(turned, axis=0) * (1.0 / width)
        total = g1[...] + stat[:, 1:2] * (scaled - sums[:, 0:1] - normal * sums[:, 1:2])
        out[...] = jnp.where(masked, 0.0, total).astype(BF16)

        @pl.when(i == 0)
        def _():
            small[...] = jnp.zeros_like(small)
            small[IMG_LEN + 2 : IMG_LEN + 3, :] = cross[...]
            small[IMG_LEN + 3 : IMG_LEN + 4, :] = feed[...]

        small[:IMG_LEN, :] += total
        small[IMG_LEN : IMG_LEN + 1, :] += jnp.sum(
            jnp.where(masked, total, 0.0), axis=0, keepdims=True
        )
        small[IMG_LEN + 1 : IMG_LEN + 2, :] += jnp.sum(normed_grad * normal, axis=0, keepdims=True)

    outs = [struct((rows, columns), BF16), struct((IMG_LEN + PAD, columns), F32)]
    own = pl.BlockSpec((1, columns), lambda i, place: (0, place[0]))
    return call(
        "self_end",
        kernel,
        place,
        (images,),
        [
            by_rows(IMG_LEN, 1),
            by_rows(IMG_LEN, columns),
            fixed((IMG_LEN, columns)),
            fixed((PAD, columns)),
            by_rows(IMG_LEN, 2),
            fixed((PAD, columns), rows // PAD),
            by_rows(IMG_LEN, columns),
            by_rows(IMG_LEN, columns),
            own,
            own,
        ],
        [by_rows(IMG_LEN, columns), fixed((IMG_LEN + PAD, columns))],
        outs,
        (mask, tokens, position_embed, vectors, stats, back, back, grad, *gains),
    )


def grad_sum(name, place, left_groups, right_groups, splits, block, spans):
    lefts, rights, terms = [], [], []
    for left_group, right_group in zip(left_groups, right_groups):
        left_base, right_base = len(lefts), len(rights)
        lefts += [p if isinstance(p, tuple) else (p, p.shape[0], None) for p, at in left_group]
        rights += [p if isinstance(p, tuple) else (p, p.shape[0], None) for p, at in right_group]
        for i, (_, left_at) in enumerate(left_group):
            for j, (_, right_at) in enumerate(right_group):
                left_rows, right_rows = lefts[left_base + i][1], rights[right_base + j][1]
                low = max(left_at, right_at)
                high = min(left_at + left_rows, right_at + right_rows)
                if low < high:
                    terms.append(
                        (left_base + i, low - left_at, right_base + j, low - right_at, high - low)
                    )
    (left_turn, height), (right_turn, width) = spans
    block = min(block, height)
    left_turn = left_turn * (height // block)
    left_count, right_count = len(lefts), len(rights)

    def kernel(place, *refs):
        left_refs = refs[:left_count]
        right_refs = refs[left_count : left_count + right_count]
        outs = refs[left_count + right_count :]
        total = None
        for li, left_row, ri, right_row, rows in terms:
            part = contract(
                left_refs[li][left_row : left_row + rows, :],
                right_refs[ri][right_row : right_row + rows, :],
                0,
                0,
            )
            total = part if total is None else total + part
        at = 0
        for out in outs:
            out[...] = total[:, at : at + out.shape[1]]
            at += out.shape[1]

    def spec(rows, wide, col, turn):
        return pl.BlockSpec(
            (rows, wide), lambda i, place: (0 if turn is None else turn(place), col(i))
        )

    outs = [struct((height, n), F32) for n in splits]
    return call(
        name,
        kernel,
        place,
        (height // block,),
        [spec(rows, block, lambda i: left_turn + i, turn) for _, rows, turn in lefts]
        + [spec(rows, width, lambda i: right_turn, turn) for _, rows, turn in rights],
        [pl.BlockSpec((block, n), lambda i, *_: (i, 0)) for n in splits],
        outs,
        [a for a, _, _ in (*lefts, *rights)],
    )


def text_grads(place, at, text, pair, text_groups, pair_groups, blocks):
    width = text.shape[1]
    text_rows = pair.shape[0]
    columns = pair.shape[1] // 2
    shards = width // columns
    step = min(4, shards)
    core_split = square_batch()
    pieces, rights, terms = [], [pair], []
    for text_group, pair_group in zip(text_groups, pair_groups):
        base = len(rights)
        rights += [piece for piece, _ in pair_group]
        for piece, row in text_group:
            pieces.append(piece)
            for k, (right, low) in enumerate(pair_group):
                if low <= row % text_rows < low + right.shape[0]:
                    terms.append((row // text_rows, row % text_rows - low, base + k))
    if not core_split:
        pieces, terms = [], []
        for k, text_group in enumerate(text_groups):
            for b in range(blocks):
                pieces.append(text_group[0][0][b * text_rows : (b + 1) * text_rows])
                terms.append((b, 0, k + 1))

    def which(s, place):
        return (s + place[0] % 2) % 2 if core_split else s

    def kernel(place, own, *refs):
        piece_refs = refs[: len(pieces)]
        right_refs = refs[len(pieces) : len(pieces) + len(rights)]
        key, value = refs[len(pieces) + len(rights) :]

        def run(s):
            total = contract(own[...], right_refs[0][...], 0, 0)
            for ref, (turn, row, k) in zip(piece_refs, terms):
                if turn == s:
                    total = total + contract(
                        ref[...], right_refs[k][row : row + ref.shape[0], :], 0, 0
                    )
            for t in range(step):
                rows = slice(t * columns, (t + 1) * columns)
                key[t, 0] = total[rows, :columns]
                value[t, 0] = total[rows, columns:]

        for s in range(blocks):
            pl.when(pl.program_id(0) == s)(lambda s=s: run(s))

    last = shards // step - 1

    def piece_spec(piece, turn):
        return pl.BlockSpec(
            (piece.shape[0], step * columns),
            lambda s, t, place: (0, jnp.where(s == turn, t, jnp.where(s > turn, last, 0))),
        )

    outs = [struct((shards, blocks, columns, columns), F32)] * 2
    out_spec = pl.BlockSpec(
        (step, 1, columns, columns), lambda s, t, place: (t, which(s, place), 0, 0)
    )
    key, value = call(
        "text_grads",
        kernel,
        place,
        (blocks, shards // step),
        [
            pl.BlockSpec(
                (text_rows, step * columns), lambda s, t, place: (at.text // text_rows + which(s, place), t)
            )
        ]
        + [piece_spec(p, term[0]) for p, term in zip(pieces, terms)]
        + [pl.BlockSpec(r.shape, lambda s, t, place: (0, 0)) for r in rights],
        [out_spec] * 2,
        outs,
        (text, *pieces, *rights),
    )
    return key.reshape(-1, columns), value.reshape(-1, columns)


class Plan:
    def __init__(self):
        self.makers, self.made = {}, {}

    def job(self, name, make):
        self.makers[name] = make

    def get(self, name):
        if name not in self.made:
            self.made[name] = self.makers[name]()
        return self.made[name]

    def behind(self, name, value):
        others = [self.get(n) for n in AFTER.get(name, ())]
        return tie(value, *others)[0] if others else value

    def tie(self, point, value):
        names = [n for n in self.makers if DONE_BY.get(n) == point]
        if not names:
            return value
        value, *done = tie(value, *[self.get(n) for n in names])
        self.made.update(zip(names, done))
        return value


class BatchSum:
    def __init__(self, name, place, products):
        self.name, self.place, self.products = name, place, products
        shapes = [
            (right.shape[1], left.shape[1]) if fold else (left.shape[1], right.shape[1])
            for left, right, fold in products
        ]
        if not square_batch():
            self.quarters = []
            return
        height, width = shapes[0]
        rows = height // 4

        def kernel(place, *refs):
            ins, outs, held = refs[: 2 * len(products)], refs[2 * len(products) : -1], refs[-1]
            for n, (_, _, fold) in enumerate(products):
                left, right = ins[2 * n], ins[2 * n + 1]
                if fold:
                    for at in range(0, width, height):
                        held[n, :, at : at + height] = contract(
                            left[:, at : at + height], right[...], 0, 0
                        ).astype(BF16)
                else:
                    held[n] = contract(left[...], right[...], 0, 0).astype(BF16)
                for k, out in enumerate(outs):
                    turn = pl.multiple_of((place[1] ^ k) * rows, rows)
                    out[n * rows : (n + 1) * rows, :] = held[n, pl.ds(turn, rows), :]

        args = [a for left, right, _ in products for a in (left, right)]
        outs = [struct((rows * len(products), width), BF16)] * 4
        self.quarters = call(
            name + "_parts",
            kernel,
            place,
            (1,),
            [fixed(a.shape) for a in args],
            [fixed(o.shape) for o in outs],
            outs,
            args,
            scratch=[pltpu.VMEM((len(products), height, width), BF16)],
        )
        self.height, self.width, self.rows = height, width, rows

    def step_one(self):
        if not square_batch():
            parts = [contract(left, right, 0, 0) for left, right, _ in self.products]
            return [lax.psum(p.astype(BF16), BATCH) for p in parts]
        return [hop(self.sent[k - 1], k) for k in (1, 2, 3)]

    def add(self, held):
        if not square_batch():
            return held
        total = self.quarters[0].astype(F32)
        for moved in held:
            total = total + moved.astype(F32)
        return [total.astype(BF16)]

    def step_two(self, held):
        if not square_batch():
            return held
        self.groups = self.move.step_two(held)
        return [self.low] + [piece for group in self.groups for piece, _ in group]

    def finish(self, held):
        if not square_batch():
            return [h.astype(F32) for h in held]
        height, width, rows = self.height, self.width, self.rows
        folds = [fold for _, _, fold in self.products]
        spots = [(0, 0)] + [
            (k + 1, first) for k, group in enumerate(self.groups) for _, first in group
        ]

        def kernel(place, *refs):
            ins, outs = refs[: len(held)], refs[len(held) :]
            for ref, (k, first) in zip(ins, spots):
                for n, (out, fold) in enumerate(zip(outs, folds)):
                    low, high = max(n * rows, first), min((n + 1) * rows, first + ref.shape[0])
                    if low >= high:
                        continue
                    count = high - low
                    at = pl.multiple_of((place[1] ^ k) * rows + low - n * rows, count)
                    piece = ref[low - first : high - first, :].astype(F32)
                    if fold:
                        for col in range(0, width, height):
                            out[pl.ds(col + at, count), :] = piece[:, col : col + height]
                    else:
                        out[pl.ds(at, count), :] = piece

        outs = [struct((width, height) if fold else (height, width), F32) for fold in folds]
        return call(
            self.name + "_finish",
            kernel,
            self.place,
            (1,),
            [fixed(a.shape) for a in held],
            [fixed(o.shape) for o in outs],
            outs,
            held,
        )


def body(
    tokens,
    captions,
    mask_counts,
    mask_positions,
    cotangent,
    mask_embed,
    position_embed,
    norm_self,
    query_self,
    key_self,
    value_self,
    out_self,
    norm_cross,
    query_cross,
    key_text,
    value_text,
    out_cross,
    norm_feed,
    up_weight,
    down_weight,
):
    rows, columns = tokens.shape
    width, hidden = query_self.shape[0], up_weight.shape[1]
    text_rows, text_blocks = captions.shape[0], captions.shape[1] // columns
    at = Packed(rows, text_rows * text_blocks)
    place = jnp.stack([lax.axis_index(TENSOR), lax.axis_index(BATCH)]).astype(jnp.int32)
    core = place[0] % 2
    shared = square_batch()
    packed, vectors, mask = pack_rows(
        at,
        mask_counts,
        mask_positions,
        tokens,
        captions,
        cotangent,
        position_embed,
        (mask_embed, norm_self, norm_cross, norm_feed),
    )
    packed = gather_cols(packed)

    text_part, seed_part = packed[at.text : at.seed], packed[at.seed : at.vec]
    if shared:
        text_part = lax.dynamic_slice_in_dim(packed, at.text + core * text_rows, text_rows, 0)
        seed_part = lax.dynamic_slice_in_dim(packed, at.seed + core * IMG_LEN, IMG_LEN, 0)
    else:
        seed_part = jnp.concatenate(
            [
                lax.dynamic_slice_in_dim(seed_part, core * IMG_LEN, IMG_LEN, 0),
                lax.dynamic_slice_in_dim(seed_part, (1 - core) * IMG_LEN, IMG_LEN, 0),
            ],
            axis=0,
        )
    plan = Plan()

    def spread(names, source, shared):
        near, far, cores = names
        move = Spread(None, shared)

        def one():
            move.array = plan.behind(near, source())
            return direct(move.array) if near in DIRECT else move.step_one()

        def two():
            held = plan.behind(far, plan.get(near))
            return held if near in DIRECT else move.step_two(held)

        plan.job(near, one)
        plan.job(far, two)
        plan.job(cores, lambda: move.swap(plan.get(far)))

    normed_self, query_one, key_one, value_one, mixed_self, partial, stats = self_forward(
        place, at, packed, query_self, key_self, value_self, out_self
    )
    spread((T1, T2, T3), lambda: text_part, shared)
    spread((X1, X2, X3), lambda: normed_self[:IMG_LEN] if shared else normed_self, shared)
    spread((Y1, Y2, Y3), lambda: seed_part, shared)
    plan.job(KV, lambda: text_project(place, at, packed, key_text, value_text))
    plan.job(DA, lambda: seed_product(place, at, packed, down_weight))
    scattered = plan.tie(SCATTERED1, scatter_cols(partial))
    mixed_out = plan.tie(MIXED1, gather_cols(scattered))
    key_two, value_two = plan.get(KV)

    stream_one, normed_cross, query_two, mixed_cross, partial, scale_cross = cross_forward(
        place, at, packed, mixed_out, query_cross, key_two, value_two, out_cross
    )
    partial = plan.tie(PARTIAL2, partial)
    scattered = plan.tie(SCATTERED2, scatter_cols(partial))
    mixed_out = plan.tie(MIXED2, gather_cols(scattered))

    own_two, scale_feed, normed_feed, activation, hidden_grad, partial = feed_both(
        place, at, stream_one, mixed_out, packed, plan.get(DA), up_weight
    )
    spread((F1, F2, F3), lambda: normed_feed[:IMG_LEN] if shared else normed_feed, shared)
    spread((A1, A2, A3), lambda: activation, False)
    spread((U1, U2, U3), lambda: hidden_grad, False)
    plan.job(OUT, lambda: out_product(place, plan.behind(OUT, activation), down_weight))
    partial = plan.tie(PARTIAL3, partial)
    scattered = plan.tie(SCATTERED3, scatter_cols(partial))
    feed_back = plan.tie(MIXED3, gather_cols(scattered))

    seed_cross, query_grad, pair, partial, feed_gain = cross_backward(
        place,
        at,
        normed_feed,
        scale_feed,
        feed_back,
        packed,
        packed,
        out_cross,
        query_two,
        key_two,
        value_two,
        query_cross,
        plan.get(OUT),
    )
    own_seed = [
        ((packed, IMG_LEN, lambda p: at.seed // IMG_LEN + p[0] % 2), 0),
        ((packed, IMG_LEN, lambda p: at.seed // IMG_LEN + 1 - p[0] % 2), IMG_LEN),
    ]
    plan.job(GD,
        lambda: grad_sum(
            "down_grads",
            place,
            [[(plan.behind(GD, activation), 0)], *plan.get(A2)],
            [own_seed, *plan.get(Y3)],
            (width,),
            256,
            ((0, hidden), (0, width)),
        ),
    )
    plan.job(GU,
        lambda: grad_sum(
            "up_grads",
            place,
            [[(plan.behind(GU, normed_feed), 0)], *plan.get(F3)],
            [[(hidden_grad, 0)], *plan.get(U2)],
            (hidden,),
            512,
            ((0, width), (0, hidden)),
        ),
    )
    cross_sum = BatchSum(
        "cross", place, [(mixed_cross, seed_cross, False), (normed_cross, query_grad, True)]
    )

    def batch_sum(names, total):
        make, out, add, near, far = names
        plan.job(make, lambda: total.quarters)

        def one():
            total.sent = plan.behind(out, plan.get(make)[1:])
            return total.step_one()

        def back():
            (total.low, *_) = held = plan.behind(near, plan.get(add))
            if not shared:
                return held
            total.move = Spread(total.low, False)
            return direct(total.low) if near in DIRECT else total.move.step_one()

        def rest():
            held = plan.behind(far, plan.get(near))
            if near in DIRECT and shared:
                total.groups = held
                return [total.low] + [piece for group in held for piece, _ in group]
            return total.step_two(held)

        plan.job(out, one)
        plan.job(add, lambda: total.add(plan.behind(add, plan.get(out))))
        plan.job(near, back)
        plan.job(far, rest)

    batch_sum((C0, C1, CA, C2, C3), cross_sum)
    plan.job(TB,
        lambda: text_back(
            place, plan.behind(TB, pair), key_text, value_text, rows + PAD, width
        ),
    )
    spread((D1, D2, D3), lambda: pair, False)
    plan.job(GT,
        lambda: text_grads(
            place,
            at,
            packed,
            plan.behind(GT, pair),
            plan.get(T3),
            plan.get(D2),
            text_blocks,
        ),
    )
    partial = plan.tie(PARTIAL4, partial)
    scattered = plan.tie(SCATTERED4, scatter_cols(partial))
    out_slice = scattered[rows:]
    cross_back = plan.tie(MIXED4, gather_cols(scattered[:rows]))

    own_one, seed_self, triple, partial, cross_gain = self_backward(
        place,
        at,
        normed_self,
        normed_cross,
        scale_cross,
        cross_back,
        packed,
        seed_cross,
        out_self,
        query_one,
        key_one,
        value_one,
        (query_self, key_self, value_self),
        plan.get(TB),
    )
    layer_out = (own_two + out_slice.astype(F32)).astype(BF16)
    self_sum = BatchSum("self", place, [(mixed_self, seed_self, False)])
    batch_sum((S0, S1, SA, S2, S3), self_sum)
    spread((Q1, Q2, Q3), lambda: triple, False)
    plan.job(GQ,
        lambda: grad_sum(
            "self_grads",
            place,
            [[(plan.behind(GQ, normed_self), 0)], *plan.get(X3)],
            [[(triple, 0)], *plan.get(Q2)],
            (columns,) * 3,
            512,
            ((0, width), (0, 3 * columns)),
        ),
    )
    partial = plan.tie(PARTIAL5, partial)
    scattered = plan.tie(SCATTERED5, scatter_cols(partial))
    low = rows + PAD
    captions_grad = jnp.concatenate(
        [
            scattered[low + k * text_rows : low + (k + 1) * text_rows]
            for k in range(text_blocks)
        ],
        axis=1,
    )
    tokens_grad, small = self_end(
        place,
        mask,
        tokens,
        position_embed,
        vectors,
        stats,
        scattered,
        own_one,
        (cross_gain, feed_gain),
        width,
    )
    small = plan.tie(SMALL, small)
    seen = small
    plan.job(SM, lambda: seen)
    plan.job(CF, lambda: cross_sum.finish(plan.behind(CF, plan.get(C3))))
    plan.job(SF, lambda: self_sum.finish(plan.behind(SF, plan.get(S3))))
    small = direct_sum(small)
    (down_grad,) = plan.get(GD)
    (up_grad,) = plan.get(GU)
    key_text_grad, value_text_grad = plan.get(GT)
    query_self_grad, key_self_grad, value_self_grad = plan.get(GQ)
    out_cross_grad, query_cross_grad = plan.get(CF)
    (out_self_grad,) = plan.get(SF)
    return (
        layer_out,
        tokens_grad,
        captions_grad,
        small[IMG_LEN],
        small[:IMG_LEN],
        small[IMG_LEN + 1],
        query_self_grad,
        key_self_grad,
        value_self_grad,
        out_self_grad,
        small[IMG_LEN + 2],
        query_cross_grad,
        key_text_grad,
        value_text_grad,
        out_cross_grad,
        small[IMG_LEN + 3],
        up_grad,
        down_grad,
    )


def solution(mesh):
    return jax.shard_map(
        body,
        mesh=mesh,
        in_specs=(
            P(BATCH, TENSOR),
            P(BATCH, TENSOR),
            P(BATCH),
            P(BATCH, None),
            P(BATCH, TENSOR),
            P(TENSOR),
            P(None, TENSOR),
            P(TENSOR),
            P(None, TENSOR),
            P(None, TENSOR),
            P(None, TENSOR),
            P(TENSOR, None),
            P(TENSOR),
            P(None, TENSOR),
            P(None, TENSOR),
            P(None, TENSOR),
            P(TENSOR, None),
            P(TENSOR),
            P(None, TENSOR),
            P(TENSOR, None),
        ),
        out_specs=(
            P(BATCH, TENSOR),
            P(BATCH, TENSOR),
            P(BATCH, TENSOR),
            P(TENSOR),
            P(None, TENSOR),
            P(TENSOR),
            P(None, TENSOR),
            P(None, TENSOR),
            P(None, TENSOR),
            P(TENSOR, None),
            P(TENSOR),
            P(None, TENSOR),
            P(None, TENSOR),
            P(None, TENSOR),
            P(TENSOR, None),
            P(TENSOR),
            P(None, TENSOR),
            P(TENSOR, None),
        ),
        check_vma=False,
    )
```

```python
import jax
import jax.numpy as jnp
from jax import lax
from jax.experimental import pallas as pl
from jax.experimental.pallas import tpu as pltpu
from jax.sharding import PartitionSpec as P

HEAD_DIM = 128
IMG_LEN = 256
EPS = 1e-06
F32 = jnp.float32
BF16 = jnp.bfloat16
INV_ROOT = float(HEAD_DIM) ** (-0.5)
PAD = 16
BATCH, TENSOR = "batch", "tensor"
(
    T1, T2, T3, X1, X2, X3, Y1, Y2, Y3, KV, DA, F1, F2, F3, A1, A2, A3, U1, U2, U3, OUT, GD, GU,
    C0, C1, CA, C2, C3, TB, D1, D2, D3, GT, S0, S1, SA, S2, S3, Q1, Q2, Q3, GQ, SM, CF, SF,
) = range(45)
(
    SCATTERED1, MIXED1, PARTIAL2, SCATTERED2, MIXED2, PARTIAL3, SCATTERED3, MIXED3, PARTIAL4,
    SCATTERED4, MIXED4, PARTIAL5, SCATTERED5, SMALL,
) = range(14)
DONE_BY = {
    T1: SCATTERED1, KV: SCATTERED1, T2: PARTIAL2, X1: MIXED1, X2: SCATTERED2, T3: SCATTERED2,
    DA: SCATTERED2, Y1: PARTIAL3, X3: SCATTERED2, Y2: PARTIAL3, F1: SCATTERED3, OUT: MIXED3,
    Y3: SCATTERED3, F2: MIXED3, A1: PARTIAL4, A2: MIXED4, F3: MIXED3, C0: SCATTERED4,
    TB: SCATTERED4, U1: SCATTERED4, C1: PARTIAL5, GD: SCATTERED4, U2: PARTIAL5, GU: SCATTERED5,
    GT: MIXED4, Q1: SMALL, Q2: SCATTERED5, S0: SCATTERED5, D2: PARTIAL5, GQ: SCATTERED5, C2: SMALL,
}
AFTER = {
    A1: (F2,), U1: (A2,), S1: (Q2,), F1: (Y3,), CF: (SM,), SF: (SM,), D1: (U1,), SA: (SM,),
    CA: (GD,),
}
DIRECT = (D1, Q1,)
COST = dict(
    self_forward=17, text_project=25, cross_forward=0, seed_product=3, feed_both=6, out_product=15,
    cross_backward=20, self_backward=27, self_end=10, text_back=8, down_grads=0, up_grads=14,
    text_grads=15, self_grads=40, cross_parts=0, self_parts=10, cross_finish=0, self_finish=0,
)


def contract(left, right, left_dim, right_dim):
    return lax.dot_general(
        left, right, (((left_dim,), (right_dim,)), ((), ())), preferred_element_type=F32
    )


def tie(*values):
    leaves, tree = jax.tree.flatten(values)
    arrays = iter(lax.optimization_barrier([v for v in leaves if not isinstance(v, int)]))
    return tree.unflatten([v if isinstance(v, int) else next(arrays) for v in leaves])


def gather_cols(array):
    return lax.all_gather(array, TENSOR, axis=1, tiled=True)


def scatter_cols(array):
    return lax.psum_scatter(array, TENSOR, scatter_dimension=1, tiled=True)


def square_batch():
    return lax.axis_size(BATCH) == 4


def hop(array, flip):
    pairs = [(i, i ^ flip) for i in range(lax.axis_size(BATCH))]
    return lax.ppermute(array, BATCH, pairs)


def swap_core(array):
    pairs = [(i, i ^ 1) for i in range(lax.axis_size(TENSOR))]
    return lax.ppermute(array, TENSOR, pairs)


def ring_others(array):
    size, own = lax.axis_size(BATCH), lax.axis_index(BATCH)
    whole = lax.all_gather(array, BATCH, axis=0, tiled=False)
    return [
        lax.dynamic_index_in_dim(whole, lax.rem(own + k, size), 0, keepdims=False)
        for k in range(1, size)
    ]


def direct(array):
    moved = [hop(array, k) for k in (1, 2, 3)] if square_batch() else ring_others(array)
    return [[(m, 0)] for m in moved]


class Spread:
    def __init__(self, array, shared):
        self.array, self.shared = array, shared

    def step_one(self):
        if not square_batch():
            return ring_others(self.array)
        return [hop(self.array, 1), hop(self.array, 2)]

    def step_two(self, held):
        rows = self.array.shape[0]
        if square_batch():
            cut = rows // 2
            along, across = held
            groups = [
                [(along, 0)],
                [(across, 0)],
                [(hop(along[:cut], 2), 0), (hop(across[cut:], 1), cut)],
            ]
        else:
            groups = [[(piece, 0)] for piece in held]
        return groups

    def swap(self, groups):
        if self.shared:
            rows = self.array.shape[0]
            groups = [g + [(swap_core(piece), rows + at) for piece, at in g] for g in groups]
        return groups


def direct_sum(array):
    if not square_batch():
        return lax.psum(array.astype(BF16), BATCH).astype(F32)
    low = array.astype(BF16)
    moved = [hop(low, k) for k in (1, 2, 3)]
    return array + moved[0].astype(F32) + moved[1].astype(F32) + moved[2].astype(F32)


def params():
    return pltpu.CompilerParams(vmem_limit_bytes=56 << 20)


def cost(micros):
    return pl.CostEstimate(
        flops=1000, bytes_accessed=int(1e6 * micros) + 1000, transcendentals=0
    )


def struct(shape, dtype):
    return jax.ShapeDtypeStruct(shape, dtype)


def by_rows(rows, width, first=0):
    return pl.BlockSpec((rows, width), lambda i, *_: (first + i, 0))


def turned_rows(rows, width):
    blocks = IMG_LEN // rows
    return pl.BlockSpec((rows, width), lambda i, place: (image_turn(i, place, blocks), 0))


def fixed(shape, row=0, col=0):
    return pl.BlockSpec(shape, lambda i, *_: (row, col))


def call(name, kernel, place, grid, in_specs, out_specs, outs, args, scratch=(), aliases=None):
    return pl.pallas_call(
        kernel,
        grid_spec=pltpu.PrefetchScalarGridSpec(
            num_scalar_prefetch=1,
            grid=grid,
            in_specs=in_specs,
            out_specs=out_specs,
            scratch_shapes=list(scratch),
        ),
        out_shape=outs,
        input_output_aliases=aliases or {},
        compiler_params=params(),
        cost_estimate=cost(COST[name]),
        name=name,
    )(place, *args)


def core_of(place):
    return place[0] % 2


class Packed:
    def __init__(self, rows, text_rows):
        self.rows = rows
        self.text = rows
        self.seed = self.text + text_rows
        self.vec = self.seed + rows
        self.total = self.vec + PAD


def pack_rows(at, counts, positions, tokens, captions, cotangent, position_embed, vectors):
    rows, columns = tokens.shape
    images = rows // IMG_LEN
    text_rows = captions.shape[0]
    text_blocks = captions.shape[1] // columns

    def kernel(counts, order, tok, cap, cot, pos, *rest):
        out, block, mask = rest[-3:]
        for k in range(text_blocks):
            low = at.text + k * text_rows
            out[low : low + text_rows, :] = cap[:, k * columns : (k + 1) * columns]
        lines = [v[...].astype(F32).reshape(1, columns) for v in rest[:-3]]
        lines.append(jnp.zeros((PAD - len(lines), columns), F32))
        vec = jnp.concatenate(lines, axis=0).astype(BF16)
        out[at.vec :, :] = vec
        block[...] = vec
        place = lax.broadcasted_iota(jnp.int32, (IMG_LEN, IMG_LEN), 0)
        slot = lax.broadcasted_iota(jnp.int32, (IMG_LEN, IMG_LEN), 1)
        for i in range(images):
            hit = (order[i : i + 1, :] == place) & (slot < counts[i])
            column = jnp.max(hit.astype(F32), axis=1, keepdims=True)
            own = slice(i * IMG_LEN, (i + 1) * IMG_LEN)
            mask[own, :] = column
            base = jnp.where(column > 0.0, vec[0:1, :].astype(F32), tok[own, :].astype(F32))
            out[own, :] = (base + pos[...].astype(F32)).astype(BF16)
            out[at.seed + i * IMG_LEN : at.seed + (i + 1) * IMG_LEN, :] = jnp.where(
                column > 0.0, cot[own, :].astype(F32), 0.0
            ).astype(BF16)

    vmem = pl.BlockSpec(memory_space=pltpu.VMEM)
    outs = [
        struct((at.total, columns), BF16),
        struct((PAD, columns), BF16),
        struct((rows, 1), F32),
    ]
    args = (counts, positions, tokens, captions, cotangent, position_embed, *vectors)
    return pl.pallas_call(
        kernel,
        in_specs=[pl.BlockSpec(memory_space=pltpu.SMEM)] + [vmem] * (len(args) - 1),
        out_specs=[vmem] * 3,
        out_shape=outs,
        compiler_params=params(),
        cost_estimate=cost(2),
        name="pack_rows",
    )(*args)


def normalize(stream):
    width = stream.shape[1]
    mean = jnp.sum(stream, axis=1, keepdims=True) * (1.0 / width)
    var = jnp.sum(stream * stream, axis=1, keepdims=True) * (1.0 / width) - mean * mean
    inv_std = lax.rsqrt(var + EPS)
    return (stream - mean) * inv_std, mean, inv_std


def norm_back(grad, normed, inv_std, gain):
    width = grad.shape[1]
    normal = normed * (1.0 / gain)
    scaled = grad * gain
    first = jnp.sum(scaled, axis=1, keepdims=True) * (1.0 / width)
    second = jnp.sum(grad * normed, axis=1, keepdims=True) * (1.0 / width)
    back = inv_std * (scaled - first - normal * second)
    return back, jnp.sum(grad * normal, axis=0, keepdims=True)


def probabilities(query, key):
    scores = contract(query, key, 1, 1) * INV_ROOT
    terms = jnp.exp(scores - jnp.max(scores, axis=1, keepdims=True))
    return terms * (1.0 / jnp.sum(terms, axis=1, keepdims=True))


def head_slices(width):
    return [slice(at, at + HEAD_DIM) for at in range(0, width, HEAD_DIM)]


def attend(query, key, value):
    mixed = [
        contract(probabilities(query[:, h], key[:, h]).astype(BF16), value[:, h], 1, 0)
        for h in head_slices(query.shape[1])
    ]
    return jnp.concatenate(mixed, axis=1).astype(BF16)


def attend_back(grad, query, key, value):
    parts = []
    for h in head_slices(query.shape[1]):
        probs = probabilities(query[:, h], key[:, h])
        prob_grad = contract(grad[:, h], value[:, h], 1, 1)
        inner = jnp.sum(probs * prob_grad, axis=1, keepdims=True)
        score_grad = (probs * (prob_grad - inner)).astype(BF16)
        parts.append(
            (
                contract(score_grad, key[:, h], 1, 0) * INV_ROOT,
                contract(score_grad, query[:, h], 0, 0) * INV_ROOT,
                contract(probs.astype(BF16), grad[:, h], 0, 0),
            )
        )
    return [jnp.concatenate(group, axis=1).astype(BF16) for group in zip(*parts)]


def first_stream(mask, tok, pos, vec):
    base = jnp.where(mask[...] > 0.0, vec[0:1, :].astype(F32), tok[...].astype(F32))
    return base + pos[...].astype(F32)


def packed_specs(at, width):
    return [by_rows(IMG_LEN, width), fixed((PAD, width), at.vec // PAD)]


def self_forward(place, at, packed, query_w, key_w, value_w, out_w):
    rows, width = at.rows, packed.shape[1]
    columns = query_w.shape[1]

    def kernel(
        place, zero, vec, wq, wk, wv, wo, normed, query, key, value, mixed, part, stats
    ):
        normal, mean, inv_std = normalize(zero[...].astype(F32))
        stats[:, 0:1] = mean
        stats[:, 1:2] = inv_std
        low = (normal * vec[1:2, :].astype(F32)).astype(BF16)
        normed[...] = low
        q = contract(low, wq[...], 1, 0).astype(BF16)
        k = contract(low, wk[...], 1, 0).astype(BF16)
        v = contract(low, wv[...], 1, 0).astype(BF16)
        query[...], key[...], value[...] = q, k, v
        a = attend(q, k, v)
        mixed[...] = a
        part[...] = contract(a, wo[...], 1, 0).astype(BF16)

    outs = [struct((rows, width), BF16)] + [struct((rows, columns), BF16)] * 4
    outs += [struct((rows, width), BF16), struct((rows, 2), F32)]
    args = (packed, packed, query_w, key_w, value_w, out_w)
    return call(
        "self_forward",
        kernel,
        place,
        (rows // IMG_LEN,),
        packed_specs(at, width) + [fixed(w.shape) for w in (query_w, key_w, value_w, out_w)],
        [turned_rows(IMG_LEN, width)] + [by_rows(IMG_LEN, o.shape[1]) for o in outs[1:]],
        outs,
        args,
    )


def text_project(place, at, text, key_w, value_w):
    columns = key_w.shape[1]
    width = text.shape[1]
    shards = width // columns
    blocks = key_w.shape[0] // width
    text_rows = (at.seed - at.text) // blocks
    first = at.text // text_rows
    step = min(4, shards)

    def kernel(place, *refs):
        texts, (wk, wv, key, value, key_sum, value_sum) = refs[:blocks], refs[blocks:]

        @pl.when(pl.program_id(0) == 0)
        def _():
            key_sum[...] = jnp.zeros_like(key_sum)
            value_sum[...] = jnp.zeros_like(value_sum)

        for t in range(step):
            for k, text in enumerate(texts):
                piece = text[:, t * columns : (t + 1) * columns]
                key_sum[...] += contract(piece, wk[t, k], 1, 0)
                value_sum[...] += contract(piece, wv[t, k], 1, 0)

        @pl.when(pl.program_id(0) == pl.num_programs(0) - 1)
        def _():
            key[...] = key_sum[...].astype(BF16)
            value[...] = value_sum[...].astype(BF16)

    cut = (shards, blocks, columns, columns)
    outs = [struct((text_rows, columns), BF16)] * 2
    weight = pl.BlockSpec((step, *cut[1:]), lambda i, *_: (i, 0, 0, 0))
    args = (*[text] * blocks, key_w.reshape(cut), value_w.reshape(cut))
    return call(
        "text_project",
        kernel,
        place,
        (shards // step,),
        [
            pl.BlockSpec((text_rows, step * columns), lambda i, *_, k=k: (first + k, i))
            for k in range(blocks)
        ]
        + [weight] * 2,
        [fixed(o.shape) for o in outs],
        outs,
        args,
        scratch=[pltpu.VMEM((text_rows, columns), F32)] * 2,
    )


def cross_forward(place, at, packed, added, query_w, key, value, out_w):
    rows, width = at.rows, packed.shape[1]
    columns = query_w.shape[1]
    text_rows = key.shape[0] // (rows // IMG_LEN)

    def kernel(
        place, zero, vec, add, wq, k, v, wo, stream, normed, query, mixed, part, scale
    ):
        one = zero[...].astype(F32) + add[...].astype(F32)
        stream[...] = one.astype(BF16)
        normal, mean, inv_std = normalize(one)
        scale[...] = inv_std
        low = (normal * vec[2:3, :].astype(F32)).astype(BF16)
        normed[...] = low
        q = contract(low, wq[...], 1, 0).astype(BF16)
        query[...] = q
        a = attend(q, k[...], v[...])
        mixed[...] = a
        part[...] = contract(a, wo[...], 1, 0).astype(BF16)

    outs = [struct((rows, width), BF16)] * 2
    outs += [struct((rows, columns), BF16)] * 2 + [struct((rows, width), BF16)]
    outs += [struct((rows, 1), F32)]
    args = (packed, packed, added, query_w, key, value, out_w)
    return call(
        "cross_forward",
        kernel,
        place,
        (rows // IMG_LEN,),
        packed_specs(at, width)
        + [
            by_rows(IMG_LEN, width),
            fixed(query_w.shape),
            by_rows(text_rows, columns),
            by_rows(text_rows, columns),
            fixed(out_w.shape),
        ],
        [by_rows(IMG_LEN, o.shape[1]) for o in outs],
        outs,
        args,
    )


def seed_product(place, at, seed, down_w):
    rows, (hidden, width) = at.rows, down_w.shape

    def kernel(place, seed, down, out):
        out[...] = contract(seed[...], down[...], 1, 1)

    outs = [struct((rows, hidden), F32)]
    return call(
        "seed_product",
        kernel,
        place,
        (rows // IMG_LEN,),
        [by_rows(IMG_LEN, width, at.seed // IMG_LEN), fixed(down_w.shape)],
        [by_rows(IMG_LEN, hidden)],
        outs,
        (seed, down_w),
    )[0]


def gelu_parts(u):
    scale = 0.7978845608028654
    square = u * u
    bend = jnp.tanh(scale * (u + 0.044715 * square * u))
    half = 0.5 * (1.0 + bend)
    slope = half + 0.5 * u * (1.0 - bend * bend) * scale * (1.0 + 3.0 * 0.044715 * square)
    return u * half, slope


def image_turn(i, place, blocks):
    return (i // blocks + place[0] % 2) % 2 * blocks + i % blocks


def feed_both(place, at, stream, added, packed, act_grad, up_w):
    rows, width = stream.shape
    hidden, columns = up_w.shape[1], width // lax.axis_size(TENSOR)
    block = IMG_LEN

    def kernel(place, one, add, vec, dact, up, slim, scale, normed, act, grad, part, two):
        stream = one[...].astype(F32) + add[...].astype(F32)
        two[...] = stream
        slim[...] = two[:, pl.ds(pl.multiple_of(place[0] * columns, columns), columns)]
        normal, mean, inv_std = normalize(stream)
        scale[...] = inv_std
        low = (normal * vec[3:4, :].astype(F32)).astype(BF16)
        normed[...] = low
        value, slope = gelu_parts(contract(low, up[...], 1, 0))
        act[...] = value.astype(BF16)
        du = (dact[...] * slope).astype(BF16)
        grad[...] = du
        part[...] = contract(du, up[...], 1, 1).astype(BF16)

    outs = [
        struct((rows, columns), F32),
        struct((rows, 1), F32),
        struct((rows, width), BF16),
        struct((rows, hidden), BF16),
        struct((rows, hidden), BF16),
        struct((rows, width), BF16),
    ]
    args = (stream, added, packed, act_grad, up_w)
    return call(
        "feed_both",
        kernel,
        place,
        (rows // block,),
        [
            by_rows(block, width),
            by_rows(block, width),
            fixed((PAD, width), at.vec // PAD),
            by_rows(block, hidden),
            fixed(up_w.shape),
        ],
        [
            by_rows(block, columns),
            by_rows(block, 1),
            turned_rows(block, width),
            turned_rows(block, hidden),
            turned_rows(block, hidden),
            by_rows(block, width),
        ],
        outs,
        args,
        scratch=[pltpu.VMEM((block, width), F32)],
    )


def out_product(place, activation, down_w):
    rows, (hidden, width) = activation.shape[0], down_w.shape

    def kernel(place, act, down, out):
        out[...] = contract(act[...], down[...], 1, 0).astype(BF16)

    outs = [struct((2 * rows, width), BF16)]
    return call(
        "out_product",
        kernel,
        place,
        (rows // IMG_LEN,),
        [
            turned_rows(IMG_LEN, hidden),
            fixed(down_w.shape),
        ],
        [by_rows(IMG_LEN, width, rows // IMG_LEN)],
        outs,
        (activation, down_w),
    )[0]


def cross_backward(
    place, at, normed, scale, back, seed, packed, out_w, query, key, value, query_w, room
):
    rows, width = normed.shape
    columns = query.shape[1]
    text_rows = key.shape[0] // (rows // IMG_LEN)

    def kernel(place, three, inv, dn, g3, vec, wo, q, k, v, wq, room, low, dq, dkv, part, gain):
        step, gain_step = norm_back(
            dn[...].astype(F32), three[...].astype(F32), inv[...], vec[3:4, :].astype(F32)
        )
        total = g3[...].astype(F32) + step
        y = total.astype(BF16)
        low[...] = y

        @pl.when(pl.program_id(0) == 0)
        def _():
            gain[...] = jnp.zeros_like(gain)

        gain[...] += gain_step
        da = contract(y, wo[...], 1, 1).astype(BF16)
        query_grad, key_grad, value_grad = attend_back(da, q[...], k[...], v[...])
        dq[...] = query_grad
        dkv[:, :columns] = key_grad
        dkv[:, columns:] = value_grad
        part[...] = contract(query_grad, wq[...], 1, 1).astype(BF16)

    outs = [
        struct((rows, width), BF16),
        struct((rows, columns), BF16),
        struct((key.shape[0], 2 * columns), BF16),
        struct(room.shape, BF16),
        struct((1, width), F32),
    ]
    args = (normed, scale, back, seed, packed, out_w, query, key, value, query_w, room)
    return call(
        "cross_backward",
        kernel,
        place,
        (rows // IMG_LEN,),
        [
            turned_rows(IMG_LEN, width),
            by_rows(IMG_LEN, 1),
            by_rows(IMG_LEN, width),
            by_rows(IMG_LEN, width, at.seed // IMG_LEN),
            fixed((PAD, width), at.vec // PAD),
            fixed(out_w.shape),
            by_rows(IMG_LEN, columns),
            by_rows(text_rows, columns),
            by_rows(text_rows, columns),
            fixed(query_w.shape),
            pl.BlockSpec(memory_space=pl.ANY),
        ],
        [
            by_rows(IMG_LEN, width),
            by_rows(IMG_LEN, columns),
            by_rows(text_rows, 2 * columns),
            by_rows(IMG_LEN, width),
            fixed((1, width)),
        ],
        outs,
        args,
        aliases={len(args): 3},
    )


def text_back(place, pair, key_w, value_w, rows, width):
    columns = key_w.shape[1]
    shards = width // columns
    blocks = key_w.shape[0] // width
    text_rows = pair.shape[0]
    cut = (shards, blocks, columns, columns)

    def kernel(place, grads, wk, wv, out):
        for t in range(step):
            cols = slice(t * columns, (t + 1) * columns)
            for k in range(blocks):
                part = contract(grads[:, :columns], wk[t, k], 1, 1) + contract(
                    grads[:, columns:], wv[t, k], 1, 1
                )
                out[k * text_rows : (k + 1) * text_rows, cols] = part.astype(BF16)
        out[blocks * text_rows :, :] = jnp.zeros(
            (rows - blocks * text_rows, step * columns), BF16
        )

    step = min(4, shards)
    weight = pl.BlockSpec((step, *cut[1:]), lambda i, *_: (i, 0, 0, 0))
    outs = [struct((2 * rows, width), BF16)]
    return call(
        "text_back",
        kernel,
        place,
        (shards // step,),
        [fixed(pair.shape), weight, weight],
        [pl.BlockSpec((rows, step * columns), lambda i, *_: (1, i))],
        outs,
        (pair, key_w.reshape(cut), value_w.reshape(cut)),
    )[0]


def self_backward(
    place, at, start, normed, scale, back, packed, grad, out_w, query, key, value, weights, room
):
    rows, width = normed.shape
    columns = query.shape[1]
    parts = IMG_LEN // columns

    def kernel(
        place, one, two, inv, dn, vec, g2, wo, q, k, v, wq, wk, wv, room, mine, low, triple, part, gain, held, lines
    ):
        i = pl.program_id(0)
        step, gain_step = norm_back(
            dn[...].astype(F32), two[...].astype(F32), inv[...], vec[2:3, :].astype(F32)
        )
        total = g2[...].astype(F32) + step
        held[...] = total
        mine[...] = held[:, pl.ds(pl.multiple_of(place[0] * columns, columns), columns)]
        y = total.astype(BF16)
        low[...] = y

        @pl.when(i == 0)
        def _():
            gain[...] = jnp.zeros_like(gain)
            lines[...] = jnp.zeros_like(lines)

        gain[...] += gain_step
        da = contract(y, wo[...], 1, 1).astype(BF16)
        query_grad, key_grad, value_grad = attend_back(da, q[...], k[...], v[...])
        triple[:, :columns] = query_grad
        triple[:, columns : 2 * columns] = key_grad
        triple[:, 2 * columns :] = value_grad
        partial = (
            contract(query_grad, wq[...], 1, 1)
            + contract(key_grad, wk[...], 1, 1)
            + contract(value_grad, wv[...], 1, 1)
        )
        sent = partial.astype(BF16)
        part[pl.ds(pl.multiple_of(i * IMG_LEN, IMG_LEN), IMG_LEN), :] = sent
        first = contract(vec[...], sent, 1, 1)[1:2, :]
        weighted = (partial * one[...].astype(F32)).astype(BF16)
        second = contract(jnp.ones((PAD, width), BF16), weighted, 1, 1)[0:1, :]
        for stat, line in enumerate((first, second)):
            for k in range(parts):
                piece = line[:, k * columns : (k + 1) * columns]
                lines[pl.ds((2 * i + stat) * parts + k, 1), :] = jnp.concatenate(
                    [piece] * (width // columns), axis=1
                )

        @pl.when(i == pl.num_programs(0) - 1)
        def _():
            part[rows:, :] = lines[...].astype(BF16)

    outs = [
        struct((rows, columns), F32),
        struct((rows, width), BF16),
        struct((rows, 3 * columns), BF16),
        struct(room.shape, BF16),
        struct((1, width), F32),
    ]
    args = (start, normed, scale, back, packed, grad, out_w, query, key, value, *weights, room)
    return call(
        "self_backward",
        kernel,
        place,
        (rows // IMG_LEN,),
        [
            turned_rows(IMG_LEN, width),
            by_rows(IMG_LEN, width),
            by_rows(IMG_LEN, 1),
            by_rows(IMG_LEN, width),
            fixed((PAD, width), at.vec // PAD),
            by_rows(IMG_LEN, width),
            fixed(out_w.shape),
        ]
        + [by_rows(IMG_LEN, columns)] * 3
        + [fixed(w.shape) for w in weights]
        + [pl.BlockSpec(memory_space=pl.ANY)],
        [
            by_rows(IMG_LEN, columns),
            by_rows(IMG_LEN, width),
            turned_rows(IMG_LEN, 3 * columns),
            fixed((rows + PAD, width)),
            fixed((1, width)),
        ],
        outs,
        args,
        scratch=[pltpu.VMEM((IMG_LEN, width), F32), pltpu.VMEM((PAD, width), F32)],
        aliases={len(args): 3},
    )


def self_end(place, mask, tokens, position_embed, vectors, stats, back, grad, gains, width):
    rows, columns = tokens.shape
    images = rows // IMG_LEN
    parts = IMG_LEN // columns

    def kernel(place, mask, tok, pos, vec, stat, tot, dn, g1, cross, feed, out, small):
        i = pl.program_id(0)
        masked = mask[...] > 0.0
        stream = first_stream(mask, tok, pos, vec)
        normal = (stream - stat[:, 0:1]) * stat[:, 1:2]
        normed_grad = dn[...].astype(F32)
        scaled = normed_grad * vec[1:2, :].astype(F32)
        line = lax.broadcasted_iota(jnp.int32, (PAD, 128), 0)
        lane = lax.broadcasted_iota(jnp.int32, (PAD, 128), 1)
        turned = [
            contract(
                tot[...],
                ((line == (2 * i + lane) * parts + k) & (lane < 2)).astype(F32).astype(BF16),
                0,
                0,
            )
            for k in range(parts)
        ]
        sums = jnp.concatenate(turned, axis=0) * (1.0 / width)
        total = g1[...] + stat[:, 1:2] * (scaled - sums[:, 0:1] - normal * sums[:, 1:2])
        out[...] = jnp.where(masked, 0.0, total).astype(BF16)

        @pl.when(i == 0)
        def _():
            small[...] = jnp.zeros_like(small)
            small[IMG_LEN + 2 : IMG_LEN + 3, :] = cross[...]
            small[IMG_LEN + 3 : IMG_LEN + 4, :] = feed[...]

        small[:IMG_LEN, :] += total
        small[IMG_LEN : IMG_LEN + 1, :] += jnp.sum(
            jnp.where(masked, total, 0.0), axis=0, keepdims=True
        )
        small[IMG_LEN + 1 : IMG_LEN + 2, :] += jnp.sum(normed_grad * normal, axis=0, keepdims=True)

    outs = [struct((rows, columns), BF16), struct((IMG_LEN + PAD, columns), F32)]
    own = pl.BlockSpec((1, columns), lambda i, place: (0, place[0]))
    return call(
        "self_end",
        kernel,
        place,
        (images,),
        [
            by_rows(IMG_LEN, 1),
            by_rows(IMG_LEN, columns),
            fixed((IMG_LEN, columns)),
            fixed((PAD, columns)),
            by_rows(IMG_LEN, 2),
            fixed((PAD, columns), rows // PAD),
            by_rows(IMG_LEN, columns),
            by_rows(IMG_LEN, columns),
            own,
            own,
        ],
        [by_rows(IMG_LEN, columns), fixed((IMG_LEN + PAD, columns))],
        outs,
        (mask, tokens, position_embed, vectors, stats, back, back, grad, *gains),
    )


def grad_sum(name, place, left_groups, right_groups, splits, block, spans):
    lefts, rights, terms = [], [], []
    for left_group, right_group in zip(left_groups, right_groups):
        left_base, right_base = len(lefts), len(rights)
        lefts += [p if isinstance(p, tuple) else (p, p.shape[0], None) for p, at in left_group]
        rights += [p if isinstance(p, tuple) else (p, p.shape[0], None) for p, at in right_group]
        for i, (_, left_at) in enumerate(left_group):
            for j, (_, right_at) in enumerate(right_group):
                left_rows, right_rows = lefts[left_base + i][1], rights[right_base + j][1]
                low = max(left_at, right_at)
                high = min(left_at + left_rows, right_at + right_rows)
                if low < high:
                    terms.append(
                        (left_base + i, low - left_at, right_base + j, low - right_at, high - low)
                    )
    (left_turn, height), (right_turn, width) = spans
    block = min(block, height)
    left_turn = left_turn * (height // block)
    left_count, right_count = len(lefts), len(rights)

    def kernel(place, *refs):
        left_refs = refs[:left_count]
        right_refs = refs[left_count : left_count + right_count]
        outs = refs[left_count + right_count :]
        total = None
        for li, left_row, ri, right_row, rows in terms:
            part = contract(
                left_refs[li][left_row : left_row + rows, :],
                right_refs[ri][right_row : right_row + rows, :],
                0,
                0,
            )
            total = part if total is None else total + part
        at = 0
        for out in outs:
            out[...] = total[:, at : at + out.shape[1]]
            at += out.shape[1]

    def spec(rows, wide, col, turn):
        return pl.BlockSpec(
            (rows, wide), lambda i, place: (0 if turn is None else turn(place), col(i))
        )

    outs = [struct((height, n), F32) for n in splits]
    return call(
        name,
        kernel,
        place,
        (height // block,),
        [spec(rows, block, lambda i: left_turn + i, turn) for _, rows, turn in lefts]
        + [spec(rows, width, lambda i: right_turn, turn) for _, rows, turn in rights],
        [pl.BlockSpec((block, n), lambda i, *_: (i, 0)) for n in splits],
        outs,
        [a for a, _, _ in (*lefts, *rights)],
    )


def text_grads(place, at, text, pair, text_groups, pair_groups, blocks):
    width = text.shape[1]
    text_rows = pair.shape[0]
    columns = pair.shape[1] // 2
    shards = width // columns
    step = min(4, shards)
    core_split = square_batch()
    pieces, rights, terms = [], [pair], []
    for text_group, pair_group in zip(text_groups, pair_groups):
        base = len(rights)
        rights += [piece for piece, _ in pair_group]
        for piece, row in text_group:
            pieces.append(piece)
            for k, (right, low) in enumerate(pair_group):
                if low <= row % text_rows < low + right.shape[0]:
                    terms.append((row // text_rows, row % text_rows - low, base + k))
    if not core_split:
        pieces, terms = [], []
        for k, text_group in enumerate(text_groups):
            for b in range(blocks):
                pieces.append(text_group[0][0][b * text_rows : (b + 1) * text_rows])
                terms.append((b, 0, k + 1))

    def which(s, place):
        return (s + place[0] % 2) % 2 if core_split else s

    def kernel(place, own, *refs):
        piece_refs = refs[: len(pieces)]
        right_refs = refs[len(pieces) : len(pieces) + len(rights)]
        key, value = refs[len(pieces) + len(rights) :]

        def run(s):
            total = contract(own[...], right_refs[0][...], 0, 0)
            for ref, (turn, row, k) in zip(piece_refs, terms):
                if turn == s:
                    total = total + contract(
                        ref[...], right_refs[k][row : row + ref.shape[0], :], 0, 0
                    )
            for t in range(step):
                rows = slice(t * columns, (t + 1) * columns)
                key[t, 0] = total[rows, :columns]
                value[t, 0] = total[rows, columns:]

        for s in range(blocks):
            pl.when(pl.program_id(0) == s)(lambda s=s: run(s))

    last = shards // step - 1

    def piece_spec(piece, turn):
        return pl.BlockSpec(
            (piece.shape[0], step * columns),
            lambda s, t, place: (0, jnp.where(s == turn, t, jnp.where(s > turn, last, 0))),
        )

    outs = [struct((shards, blocks, columns, columns), F32)] * 2
    out_spec = pl.BlockSpec(
        (step, 1, columns, columns), lambda s, t, place: (t, which(s, place), 0, 0)
    )
    key, value = call(
        "text_grads",
        kernel,
        place,
        (blocks, shards // step),
        [
            pl.BlockSpec(
                (text_rows, step * columns), lambda s, t, place: (at.text // text_rows + which(s, place), t)
            )
        ]
        + [piece_spec(p, term[0]) for p, term in zip(pieces, terms)]
        + [pl.BlockSpec(r.shape, lambda s, t, place: (0, 0)) for r in rights],
        [out_spec] * 2,
        outs,
        (text, *pieces, *rights),
    )
    return key.reshape(-1, columns), value.reshape(-1, columns)


class Plan:
    def __init__(self):
        self.makers, self.made = {}, {}

    def job(self, name, make):
        self.makers[name] = make

    def get(self, name):
        if name not in self.made:
            self.made[name] = self.makers[name]()
        return self.made[name]

    def behind(self, name, value):
        others = [self.get(n) for n in AFTER.get(name, ())]
        return tie(value, *others)[0] if others else value

    def tie(self, point, value):
        names = [n for n in self.makers if DONE_BY.get(n) == point]
        if not names:
            return value
        value, *done = tie(value, *[self.get(n) for n in names])
        self.made.update(zip(names, done))
        return value


class BatchSum:
    def __init__(self, name, place, products):
        self.name, self.place, self.products = name, place, products
        shapes = [
            (right.shape[1], left.shape[1]) if fold else (left.shape[1], right.shape[1])
            for left, right, fold in products
        ]
        if not square_batch():
            self.quarters = []
            return
        height, width = shapes[0]
        rows = height // 4

        def kernel(place, *refs):
            ins, outs, held = refs[: 2 * len(products)], refs[2 * len(products) : -1], refs[-1]
            for n, (_, _, fold) in enumerate(products):
                left, right = ins[2 * n], ins[2 * n + 1]
                if fold:
                    for at in range(0, width, height):
                        held[n, :, at : at + height] = contract(
                            left[:, at : at + height], right[...], 0, 0
                        ).astype(BF16)
                else:
                    held[n] = contract(left[...], right[...], 0, 0).astype(BF16)
                for k, out in enumerate(outs):
                    turn = pl.multiple_of((place[1] ^ k) * rows, rows)
                    out[n * rows : (n + 1) * rows, :] = held[n, pl.ds(turn, rows), :]

        args = [a for left, right, _ in products for a in (left, right)]
        outs = [struct((rows * len(products), width), BF16)] * 4
        self.quarters = call(
            name + "_parts",
            kernel,
            place,
            (1,),
            [fixed(a.shape) for a in args],
            [fixed(o.shape) for o in outs],
            outs,
            args,
            scratch=[pltpu.VMEM((len(products), height, width), BF16)],
        )
        self.height, self.width, self.rows = height, width, rows

    def step_one(self):
        if not square_batch():
            parts = [contract(left, right, 0, 0) for left, right, _ in self.products]
            return [lax.psum(p.astype(BF16), BATCH) for p in parts]
        return [hop(self.sent[k - 1], k) for k in (1, 2, 3)]

    def add(self, held):
        if not square_batch():
            return held
        total = self.quarters[0].astype(F32)
        for moved in held:
            total = total + moved.astype(F32)
        return [total.astype(BF16)]

    def step_two(self, held):
        if not square_batch():
            return held
        self.groups = self.move.step_two(held)
        return [self.low] + [piece for group in self.groups for piece, _ in group]

    def finish(self, held):
        if not square_batch():
            return [h.astype(F32) for h in held]
        height, width, rows = self.height, self.width, self.rows
        folds = [fold for _, _, fold in self.products]
        spots = [(0, 0)] + [
            (k + 1, first) for k, group in enumerate(self.groups) for _, first in group
        ]

        def kernel(place, *refs):
            ins, outs = refs[: len(held)], refs[len(held) :]
            for ref, (k, first) in zip(ins, spots):
                for n, (out, fold) in enumerate(zip(outs, folds)):
                    low, high = max(n * rows, first), min((n + 1) * rows, first + ref.shape[0])
                    if low >= high:
                        continue
                    count = high - low
                    at = pl.multiple_of((place[1] ^ k) * rows + low - n * rows, count)
                    piece = ref[low - first : high - first, :].astype(F32)
                    if fold:
                        for col in range(0, width, height):
                            out[pl.ds(col + at, count), :] = piece[:, col : col + height]
                    else:
                        out[pl.ds(at, count), :] = piece

        outs = [struct((width, height) if fold else (height, width), F32) for fold in folds]
        return call(
            self.name + "_finish",
            kernel,
            self.place,
            (1,),
            [fixed(a.shape) for a in held],
            [fixed(o.shape) for o in outs],
            outs,
            held,
        )


def body(
    tokens,
    captions,
    mask_counts,
    mask_positions,
    cotangent,
    mask_embed,
    position_embed,
    norm_self,
    query_self,
    key_self,
    value_self,
    out_self,
    norm_cross,
    query_cross,
    key_text,
    value_text,
    out_cross,
    norm_feed,
    up_weight,
    down_weight,
):
    rows, columns = tokens.shape
    width, hidden = query_self.shape[0], up_weight.shape[1]
    text_rows, text_blocks = captions.shape[0], captions.shape[1] // columns
    at = Packed(rows, text_rows * text_blocks)
    place = jnp.stack([lax.axis_index(TENSOR), lax.axis_index(BATCH)]).astype(jnp.int32)
    core = place[0] % 2
    shared = square_batch()
    packed, vectors, mask = pack_rows(
        at,
        mask_counts,
        mask_positions,
        tokens,
        captions,
        cotangent,
        position_embed,
        (mask_embed, norm_self, norm_cross, norm_feed),
    )
    packed = gather_cols(packed)

    text_part, seed_part = packed[at.text : at.seed], packed[at.seed : at.vec]
    if shared:
        text_part = lax.dynamic_slice_in_dim(packed, at.text + core * text_rows, text_rows, 0)
        seed_part = lax.dynamic_slice_in_dim(packed, at.seed + core * IMG_LEN, IMG_LEN, 0)
    else:
        seed_part = jnp.concatenate(
            [
                lax.dynamic_slice_in_dim(seed_part, core * IMG_LEN, IMG_LEN, 0),
                lax.dynamic_slice_in_dim(seed_part, (1 - core) * IMG_LEN, IMG_LEN, 0),
            ],
            axis=0,
        )
    plan = Plan()

    def spread(names, source, shared):
        near, far, cores = names
        move = Spread(None, shared)

        def one():
            move.array = plan.behind(near, source())
            return direct(move.array) if near in DIRECT else move.step_one()

        def two():
            held = plan.behind(far, plan.get(near))
            return held if near in DIRECT else move.step_two(held)

        plan.job(near, one)
        plan.job(far, two)
        plan.job(cores, lambda: move.swap(plan.get(far)))

    normed_self, query_one, key_one, value_one, mixed_self, partial, stats = self_forward(
        place, at, packed, query_self, key_self, value_self, out_self
    )
    spread((T1, T2, T3), lambda: text_part, shared)
    spread((X1, X2, X3), lambda: normed_self[:IMG_LEN] if shared else normed_self, shared)
    spread((Y1, Y2, Y3), lambda: seed_part, shared)
    plan.job(KV, lambda: text_project(place, at, packed, key_text, value_text))
    plan.job(DA, lambda: seed_product(place, at, packed, down_weight))
    scattered = plan.tie(SCATTERED1, scatter_cols(partial))
    mixed_out = plan.tie(MIXED1, gather_cols(scattered))
    key_two, value_two = plan.get(KV)

    stream_one, normed_cross, query_two, mixed_cross, partial, scale_cross = cross_forward(
        place, at, packed, mixed_out, query_cross, key_two, value_two, out_cross
    )
    partial = plan.tie(PARTIAL2, partial)
    scattered = plan.tie(SCATTERED2, scatter_cols(partial))
    mixed_out = plan.tie(MIXED2, gather_cols(scattered))

    own_two, scale_feed, normed_feed, activation, hidden_grad, partial = feed_both(
        place, at, stream_one, mixed_out, packed, plan.get(DA), up_weight
    )
    spread((F1, F2, F3), lambda: normed_feed[:IMG_LEN] if shared else normed_feed, shared)
    spread((A1, A2, A3), lambda: activation, False)
    spread((U1, U2, U3), lambda: hidden_grad, False)
    plan.job(OUT, lambda: out_product(place, plan.behind(OUT, activation), down_weight))
    partial = plan.tie(PARTIAL3, partial)
    scattered = plan.tie(SCATTERED3, scatter_cols(partial))
    feed_back = plan.tie(MIXED3, gather_cols(scattered))

    seed_cross, query_grad, pair, partial, feed_gain = cross_backward(
        place,
        at,
        normed_feed,
        scale_feed,
        feed_back,
        packed,
        packed,
        out_cross,
        query_two,
        key_two,
        value_two,
        query_cross,
        plan.get(OUT),
    )
    own_seed = [
        ((packed, IMG_LEN, lambda p: at.seed // IMG_LEN + p[0] % 2), 0),
        ((packed, IMG_LEN, lambda p: at.seed // IMG_LEN + 1 - p[0] % 2), IMG_LEN),
    ]
    plan.job(GD,
        lambda: grad_sum(
            "down_grads",
            place,
            [[(plan.behind(GD, activation), 0)], *plan.get(A2)],
            [own_seed, *plan.get(Y3)],
            (width,),
            256,
            ((0, hidden), (0, width)),
        ),
    )
    plan.job(GU,
        lambda: grad_sum(
            "up_grads",
            place,
            [[(plan.behind(GU, normed_feed), 0)], *plan.get(F3)],
            [[(hidden_grad, 0)], *plan.get(U2)],
            (hidden,),
            512,
            ((0, width), (0, hidden)),
        ),
    )
    cross_sum = BatchSum(
        "cross", place, [(mixed_cross, seed_cross, False), (normed_cross, query_grad, True)]
    )

    def batch_sum(names, total):
        make, out, add, near, far = names
        plan.job(make, lambda: total.quarters)

        def one():
            total.sent = plan.behind(out, plan.get(make)[1:])
            return total.step_one()

        def back():
            (total.low, *_) = held = plan.behind(near, plan.get(add))
            if not shared:
                return held
            total.move = Spread(total.low, False)
            return direct(total.low) if near in DIRECT else total.move.step_one()

        def rest():
            held = plan.behind(far, plan.get(near))
            if near in DIRECT and shared:
                total.groups = held
                return [total.low] + [piece for group in held for piece, _ in group]
            return total.step_two(held)

        plan.job(out, one)
        plan.job(add, lambda: total.add(plan.behind(add, plan.get(out))))
        plan.job(near, back)
        plan.job(far, rest)

    batch_sum((C0, C1, CA, C2, C3), cross_sum)
    plan.job(TB,
        lambda: text_back(
            place, plan.behind(TB, pair), key_text, value_text, rows + PAD, width
        ),
    )
    spread((D1, D2, D3), lambda: pair, False)
    plan.job(GT,
        lambda: text_grads(
            place,
            at,
            packed,
            plan.behind(GT, pair),
            plan.get(T3),
            plan.get(D2),
            text_blocks,
        ),
    )
    partial = plan.tie(PARTIAL4, partial)
    scattered = plan.tie(SCATTERED4, scatter_cols(partial))
    out_slice = scattered[rows:]
    cross_back = plan.tie(MIXED4, gather_cols(scattered[:rows]))

    own_one, seed_self, triple, partial, cross_gain = self_backward(
        place,
        at,
        normed_self,
        normed_cross,
        scale_cross,
        cross_back,
        packed,
        seed_cross,
        out_self,
        query_one,
        key_one,
        value_one,
        (query_self, key_self, value_self),
        plan.get(TB),
    )
    layer_out = (own_two + out_slice.astype(F32)).astype(BF16)
    self_sum = BatchSum("self", place, [(mixed_self, seed_self, False)])
    batch_sum((S0, S1, SA, S2, S3), self_sum)
    spread((Q1, Q2, Q3), lambda: triple, False)
    plan.job(GQ,
        lambda: grad_sum(
            "self_grads",
            place,
            [[(plan.behind(GQ, normed_self), 0)], *plan.get(X3)],
            [[(triple, 0)], *plan.get(Q2)],
            (columns,) * 3,
            512,
            ((0, width), (0, 3 * columns)),
        ),
    )
    partial = plan.tie(PARTIAL5, partial)
    scattered = plan.tie(SCATTERED5, scatter_cols(partial))
    low = rows + PAD
    captions_grad = jnp.concatenate(
        [
            scattered[low + k * text_rows : low + (k + 1) * text_rows]
            for k in range(text_blocks)
        ],
        axis=1,
    )
    tokens_grad, small = self_end(
        place,
        mask,
        tokens,
        position_embed,
        vectors,
        stats,
        scattered,
        own_one,
        (cross_gain, feed_gain),
        width,
    )
    small = plan.tie(SMALL, small)
    seen = small
    plan.job(SM, lambda: seen)
    plan.job(CF, lambda: cross_sum.finish(plan.behind(CF, plan.get(C3))))
    plan.job(SF, lambda: self_sum.finish(plan.behind(SF, plan.get(S3))))
    small = direct_sum(small)
    (down_grad,) = plan.get(GD)
    (up_grad,) = plan.get(GU)
    key_text_grad, value_text_grad = plan.get(GT)
    query_self_grad, key_self_grad, value_self_grad = plan.get(GQ)
    out_cross_grad, query_cross_grad = plan.get(CF)
    (out_self_grad,) = plan.get(SF)
    return (
        layer_out,
        tokens_grad,
        captions_grad,
        small[IMG_LEN],
        small[:IMG_LEN],
        small[IMG_LEN + 1],
        query_self_grad,
        key_self_grad,
        value_self_grad,
        out_self_grad,
        small[IMG_LEN + 2],
        query_cross_grad,
        key_text_grad,
        value_text_grad,
        out_cross_grad,
        small[IMG_LEN + 3],
        up_grad,
        down_grad,
    )


def solution(mesh):
    return jax.shard_map(
        body,
        mesh=mesh,
        in_specs=(
            P(BATCH, TENSOR),
            P(BATCH, TENSOR),
            P(BATCH),
            P(BATCH, None),
            P(BATCH, TENSOR),
            P(TENSOR),
            P(None, TENSOR),
            P(TENSOR),
            P(None, TENSOR),
            P(None, TENSOR),
            P(None, TENSOR),
            P(TENSOR, None),
            P(TENSOR),
            P(None, TENSOR),
            P(None, TENSOR),
            P(None, TENSOR),
            P(TENSOR, None),
            P(TENSOR),
            P(None, TENSOR),
            P(TENSOR, None),
        ),
        out_specs=(
            P(BATCH, TENSOR),
            P(BATCH, TENSOR),
            P(BATCH, TENSOR),
            P(TENSOR),
            P(None, TENSOR),
            P(TENSOR),
            P(None, TENSOR),
            P(None, TENSOR),
            P(None, TENSOR),
            P(TENSOR, None),
            P(TENSOR),
            P(None, TENSOR),
            P(None, TENSOR),
            P(None, TENSOR),
            P(TENSOR, None),
            P(TENSOR),
            P(None, TENSOR),
            P(TENSOR, None),
        ),
        check_vma=False,
    )
```
